128 devices in a mesh: wide: 32 (over x_hi, y, z), narrow: 4 (over x_lo, core).
Axes of the slice: x: 4 (x_hi: 2, x_lo: 2; x = x_hi * 2 + x_lo), y: 4, z: 4, core: 2. Of those that a mesh axis runs over, the one named last changes fastest.
Arguments:
- field: bfloat16 [256, 16, 16, 400], P(('wide', 'narrow')), may hold values from -6 to 6
- cotangent: bfloat16 [256, 16, 16, 400], P(('wide', 'narrow')), may hold values from -6 to 6
- land: int32 [256, 16, 16], P(('wide', 'narrow')), may hold values from 0 to 1
- neighbours: int32 [256, 8], P(('wide', 'narrow')), may hold values from -1 to 255, as said below
- depth_weight: float32 [49, 400], replicated, may hold values from -0.875 to 0.875
- depth_bias: float32 [400], replicated, may hold values from -5 to 5
- ln_gain: float32 [400], replicated, may hold values from 0.25 to 1.75
- ln_shift: float32 [400], replicated, may hold values from -3 to 3
- up_weight: bfloat16 [400, 1600], replicated, may hold values from -0.3125 to 0.3125
- up_bias: float32 [1600], replicated, may hold values from -3 to 3
- down_weight: bfloat16 [1600, 400], replicated, may hold values from -0.15625 to 0.15625
Outputs:
- field_grad: bfloat16 [256, 16, 16, 400], P(('wide', 'narrow'))
- depth_weight_grad: float32 [49, 400], replicated
- depth_bias_grad: float32 [400], replicated
- gain_grad: float32 [400], replicated
- shift_grad: float32 [400], replicated
- up_weight_grad: float32 [400, 1600], replicated
- up_bias_grad: float32 [1600], replicated
- down_weight_grad: float32 [1600, 400], replicated
- down_bias_grad: float32 [400], replicated
The draws below stay inside these ranges and needn't reach their ends.
Inputs may be any that keep to these rules, and one draw needn't show every extreme that they name: `neighbours`: the slots form a tile grid of 64 columns (longitude, closed into a loop) by 8 rows; the device with wide index w and narrow index n (slots (4 w + n) * 2 onward) owns the 2 x 2 positions at columns 2w, 2w+1 and rows 2n, 2n+1, holding one or two of them as wet tiles; device 0 always holds two. Neighbour entries are -1 beyond the first and last rows, toward dry positions, and on every entry of an empty slot; the relation is symmetric.
All inputs are finite; a program needn't handle non-finite values.
Results may differ from the reference program's by a relative error of at most 0.0075.
Values may be sent and summed in bfloat16 or wider, within the bound.
No kernel may reach another device: no remote copies, remote signals or barrier semaphores. Data moves between devices by JAX's collectives and lax.ppermute only.
A program may use at most 64 MiB of HBM per device.

```python
import jax
import jax.numpy as jnp
from jax import lax

C = 400
HID = 1600
TE = 16
SLOTS = 2
TILES = 256
N_WIDE = 32
N_NARROW = 4


def tile_layout(key):
    devices = N_WIDE * N_NARROW
    grid_w = 2 * N_WIDE
    grid_n = 2 * N_NARROW
    counts = jax.random.randint(jax.random.fold_in(key, 11), (devices,), 1, 3)
    counts = counts.at[0].set(2)
    order_keys = jax.random.split(jax.random.fold_in(key, 12), devices)
    orders = jax.vmap(lambda item: jax.random.permutation(item, 4))(order_keys)
    chosen = orders[:, 0:SLOTS].astype(jnp.int32)
    slot_index = jnp.arange(SLOTS, dtype=jnp.int32)[None, :]
    filled = slot_index < counts[:, None]
    device_ids = jnp.arange(devices, dtype=jnp.int32)[:, None]
    wide_index = device_ids // N_NARROW
    narrow_index = device_ids % N_NARROW
    col_pos = 2 * wide_index + chosen % 2
    row_pos = 2 * narrow_index + chosen // 2
    global_ids = device_ids * SLOTS + slot_index
    flat_pos = jnp.where(filled, col_pos * grid_n + row_pos, grid_w * grid_n)
    table = jnp.full((grid_w * grid_n + 1,), -1, jnp.int32).at[flat_pos.reshape(-1)].set(global_ids.reshape(-1))
    table = table.at[grid_w * grid_n].set(-1)
    row_steps = jnp.array([-1, 1, 0, 0, -1, -1, 1, 1], jnp.int32)
    col_steps = jnp.array([0, 0, -1, 1, -1, 1, -1, 1], jnp.int32)
    near_col = (col_pos.reshape(-1, 1) + col_steps[None, :] + grid_w) % grid_w
    near_row = row_pos.reshape(-1, 1) + row_steps[None, :]
    inside = (near_row >= 0) & (near_row < grid_n) & filled.reshape(-1, 1)
    lookup = jnp.where(inside, near_col * grid_n + near_row, grid_w * grid_n)
    neighbour_ids = table[lookup]
    return (neighbour_ids.astype(jnp.int32), filled.reshape(-1))


def draw_neighbours(key, part):
    neighbour_ids, filled = tile_layout(key)
    return neighbour_ids


def draw_land(key, part):
    neighbour_ids, filled = tile_layout(key)
    key = jax.random.fold_in(key, 5)
    cells = jax.random.randint(key, (TILES, TE, TE), 0, 6)
    return jnp.where(filled[:, None, None] & (cells > 0), 1, 0).astype(jnp.int32)


def block_levels(stream_key, extent, shards, low, largest):
    gain = 1.0
    for dim, shards_of in shards:
        draws = jax.random.uniform(jax.random.fold_in(jax.random.fold_in(stream_key, 6), dim), (shards_of,), jnp.float32, low / len(shards), largest / len(shards))
        gain = gain * jnp.repeat(jnp.exp(draws), extent[dim] // shards_of).reshape((-1,) + (1,) * (len(extent) - 1 - dim))
    return gain


def normal_values(stream_key, dims, width, limit, pieces=(), held_as=jnp.bfloat16):
    loudness = block_levels(stream_key, dims, pieces, -0.22, 0.18) if pieces else 1.0
    values = jax.random.normal(stream_key, dims, jnp.float32) * width * loudness
    return jnp.minimum(jnp.maximum(values, -limit), limit).astype(held_as)


def setup_inputs(seed: int = 0) -> dict:
    seeds = jax.random.split(jax.random.key(seed), 12)
    return {
        "field": normal_values(seeds[0], (TILES, TE, TE, C), 1.0, 6.0, ((0, 128),)),
        "cotangent": normal_values(seeds[1], (TILES, TE, TE, C), 1.0, 6.0, ((0, 128),)),
        "land": draw_land(jax.random.fold_in(seeds[11], 71), 0),
        "neighbours": draw_neighbours(jax.random.fold_in(seeds[11], 71), 0),
        "depth_weight": normal_values(seeds[4], (49, C), 49 ** -0.5, 0.875, (), jnp.float32),
        "depth_bias": normal_values(seeds[5], (C,), 1.0, 5.0, (), jnp.float32),
        "ln_gain": jnp.clip(1.0 + 0.15 * jax.random.normal(seeds[6], (C,), jnp.float32), 0.25, 1.75),
        "ln_shift": normal_values(seeds[7], (C,), 0.5, 3.0, (), jnp.float32),
        "up_weight": normal_values(seeds[8], (C, HID), C ** -0.5, 0.3125),
        "up_bias": normal_values(seeds[9], (HID,), 0.5, 3.0, (), jnp.float32),
        "down_weight": normal_values(seeds[10], (HID, C), HID ** -0.5, 0.15625),
    }


epsilon = 1e-06
gelu_root = 0.7978845608028654
gelu_cubic = 0.044715
strip_pick = (1, 0, 3, 2, 1, 1, 0, 0)

def gelu_pair(hidden):
    inner = gelu_root * (hidden + gelu_cubic * hidden * hidden * hidden)
    bent = jnp.tanh(inner)
    value = 0.5 * hidden * (1.0 + bent)
    slope = 0.5 * (1.0 + bent) + 0.5 * hidden * (1.0 - bent * bent) * gelu_root * (1.0 + 3.0 * gelu_cubic * hidden * hidden)
    return (value, slope)

def make_strips(tiles):
    edge = tiles.shape[1]
    north = tiles[:, 0:3]
    south = tiles[:, edge - 3:]
    west = jnp.swapaxes(tiles[:, :, 0:3], 1, 2)
    east = jnp.swapaxes(tiles[:, :, edge - 3:], 1, 2)
    return jnp.stack([north, south, west, east], axis=1)

def pick_strips(flat_strips, strip_rows, present):
    safe_rows = jnp.clip(strip_rows, 0, flat_strips.shape[0] - 1).astype(jnp.int32)
    taken = jnp.take(flat_strips, safe_rows, axis=0, mode='clip')
    return jnp.where(present[..., None, None, None], taken, jnp.zeros((), flat_strips.dtype))

def assemble(tiles, nearby):
    edge = tiles.shape[1]
    upper = jnp.concatenate([nearby[:, 4, :, edge - 3:], nearby[:, 0], nearby[:, 5, :, 0:3]], axis=2)
    lower = jnp.concatenate([nearby[:, 6, :, edge - 3:], nearby[:, 1], nearby[:, 7, :, 0:3]], axis=2)
    middle = jnp.concatenate([jnp.swapaxes(nearby[:, 2], 1, 2), tiles, jnp.swapaxes(nearby[:, 3], 1, 2)], axis=2)
    return jnp.concatenate([upper, middle, lower], axis=1)

def contract_cells(left, right):
    return lax.dot_general(left, right, (((0,), (0,)), ((), ())), preferred_element_type=jnp.float32)

def window_at(wide_array, row_tap, col_tap, edge):
    zero = jnp.zeros((), jnp.int32)
    shape = (wide_array.shape[0], edge, edge, wide_array.shape[3])
    return lax.dynamic_slice(wide_array, (zero, row_tap, col_tap, zero), shape)

def front_back(padded, land, cotangent, depth_weight, depth_bias, ln_gain, ln_shift, up_weight, up_bias, down_weight):
    count = land.shape[0]
    edge = land.shape[1]
    chans = padded.shape[-1]
    wider = padded.astype(jnp.float32)

    def add_tap(tap, total):
        row_tap = (tap // 7).astype(jnp.int32)
        col_tap = (tap % 7).astype(jnp.int32)
        weight_row = lax.dynamic_index_in_dim(depth_weight, tap, 0, keepdims=False)
        return total + weight_row * window_at(wider, row_tap, col_tap, edge)
    conv_out = jnp.zeros((count, edge, edge, chans), jnp.float32) + depth_bias
    conv_out = lax.fori_loop(jnp.int32(0), jnp.int32(49), add_tap, conv_out)
    flat_out = conv_out.reshape(-1, chans)
    centre = lax.optimization_barrier(jnp.mean(flat_out, axis=1, keepdims=True))
    deviation = flat_out - centre
    spread = lax.optimization_barrier(jnp.mean(deviation * deviation, axis=1, keepdims=True))
    inv_std = lax.rsqrt(spread + epsilon)
    zhat = deviation * inv_std
    normed = (zhat * ln_gain + ln_shift).astype(jnp.bfloat16)
    hidden = jnp.dot(normed, up_weight, preferred_element_type=jnp.float32) + up_bias
    act_value, slope = gelu_pair(hidden)
    act_value = act_value.astype(jnp.bfloat16)
    gated = cotangent.reshape(-1, chans) * land.reshape(-1, 1).astype(jnp.bfloat16)
    down_grad = contract_cells(act_value, gated)
    down_bias_grad = lax.optimization_barrier(jnp.sum(gated.astype(jnp.float32), axis=0))
    act_grad = jnp.dot(gated, down_weight.T, preferred_element_type=jnp.float32)
    hidden_grad = (act_grad * slope).astype(jnp.bfloat16)
    up_grad = contract_cells(normed, hidden_grad)
    up_bias_grad = lax.optimization_barrier(jnp.sum(hidden_grad.astype(jnp.float32), axis=0))
    normed_grad = jnp.dot(hidden_grad, up_weight.T, preferred_element_type=jnp.float32)
    gain_grad = lax.optimization_barrier(jnp.sum(normed_grad * zhat, axis=0))
    shift_grad = lax.optimization_barrier(jnp.sum(normed_grad, axis=0))
    scaled = normed_grad * ln_gain
    conv_grad = inv_std * (scaled - lax.optimization_barrier(jnp.mean(scaled, axis=1, keepdims=True)) - zhat * lax.optimization_barrier(jnp.mean(scaled * zhat, axis=1, keepdims=True)))
    conv_grad = conv_grad.astype(jnp.bfloat16).reshape(count, edge, edge, chans)
    return (conv_grad, gated.reshape(count, edge, edge, chans), (up_grad, down_grad, up_bias_grad, down_bias_grad, gain_grad, shift_grad))

def conv_back(grad_padded, padded, land, gated, depth_weight):
    edge = land.shape[1]
    grad_wide = grad_padded.astype(jnp.float32)
    field_wide = padded.astype(jnp.float32)
    inner = grad_wide[:, 3:3 + edge, 3:3 + edge]

    def back_tap(tap, carry):
        spread_back, tap_grads = carry
        row_tap = (tap // 7).astype(jnp.int32)
        col_tap = (tap % 7).astype(jnp.int32)
        weight_row = lax.dynamic_index_in_dim(depth_weight, tap, 0, keepdims=False)
        spread_back = spread_back + weight_row * window_at(grad_wide, 6 - row_tap, 6 - col_tap, edge)
        tap_sum = lax.optimization_barrier(jnp.sum(window_at(field_wide, row_tap, col_tap, edge) * inner, axis=(0, 1, 2)))
        tap_grads = lax.dynamic_update_index_in_dim(tap_grads, tap_sum, tap, 0)
        return (spread_back, tap_grads)
    start = (gated.astype(jnp.float32), jnp.zeros(depth_weight.shape, jnp.float32))
    spread_back, depth_grad = lax.fori_loop(jnp.int32(0), jnp.int32(49), back_tap, start)
    depth_bias_grad = lax.optimization_barrier(jnp.sum(inner, axis=(0, 1, 2)))
    field_grad = (spread_back * land.astype(jnp.float32)[..., None]).astype(jnp.bfloat16)
    return (field_grad, depth_grad, depth_bias_grad)

def reference(field, cotangent, land, neighbours, depth_weight, depth_bias, ln_gain, ln_shift, up_weight, up_bias, down_weight):
    count = field.shape[0]
    masked = field * land.astype(field.dtype)[..., None]
    pick = jnp.array(strip_pick, jnp.int32)
    present = neighbours >= 0
    strip_rows = (jnp.maximum(neighbours, 0) * 4 + pick).astype(jnp.int32)
    field_strips = make_strips(masked).reshape((count * 4, 3) + masked.shape[2:])

    def first_pass(carry, item):
        tile, cot_tile, cells, tile_rows, tile_present = item
        padded = assemble(tile[None], pick_strips(field_strips, tile_rows[None], tile_present[None]))
        conv_grad, gated, sums = front_back(padded, cells[None], cot_tile[None], depth_weight, depth_bias, ln_gain, ln_shift, up_weight, up_bias, down_weight)
        return (jax.tree.map(jnp.add, carry, sums), (conv_grad[0], gated[0]))
    start = (jnp.zeros(up_weight.shape, jnp.float32), jnp.zeros(down_weight.shape, jnp.float32), jnp.zeros(up_bias.shape, jnp.float32), jnp.zeros(depth_bias.shape, jnp.float32), jnp.zeros(ln_gain.shape, jnp.float32), jnp.zeros(ln_shift.shape, jnp.float32))
    sums, (conv_grads, gateds) = lax.scan(first_pass, start, (masked, cotangent, land, strip_rows, present))
    grad_strips = make_strips(conv_grads).reshape(field_strips.shape)

    def second_pass(carry, item):
        tile, grad_tile, gated, cells, tile_rows, tile_present = item
        padded = assemble(tile[None], pick_strips(field_strips, tile_rows[None], tile_present[None]))
        grad_padded = assemble(grad_tile[None], pick_strips(grad_strips, tile_rows[None], tile_present[None]))
        field_grad, depth_grad, depth_bias_grad = conv_back(grad_padded, padded, cells[None], gated[None], depth_weight)
        return ((carry[0] + depth_grad, carry[1] + depth_bias_grad), field_grad[0])
    start_two = (jnp.zeros(depth_weight.shape, jnp.float32), jnp.zeros(depth_bias.shape, jnp.float32))
    (depth_grad, depth_bias_grad), field_grad = lax.scan(second_pass, start_two, (masked, conv_grads, gateds, land, strip_rows, present))
    up_grad, down_grad, up_bias_grad, down_bias_grad, gain_grad, shift_grad = sums
    return (field_grad, depth_grad, depth_bias_grad, gain_grad, shift_grad, up_grad, up_bias_grad, down_grad, down_bias_grad)
```

```python
import functools

import jax
import jax.numpy as jnp
from jax import lax
from jax.experimental import pallas as pl
from jax.experimental.pallas import tpu as pltpu
from jax.sharding import PartitionSpec as P

epsilon = 1e-06
gelu_root = 0.7978845608028654
gelu_cubic = 0.044715

C = 400
CP = 512
HID = 1600
TE = 16
CELLS = 512
GROUPS = 4
HT = 13
PITCH = 32
TILES = 696
EXTRA = 650
AXES = ("wide", "narrow")
f32 = jnp.float32
bf16 = jnp.bfloat16
VMEM = pl.BlockSpec(memory_space=pltpu.VMEM)
SMEM = pl.BlockSpec(memory_space=pltpu.SMEM)


def group_width(g):
    return min(128, C - 128 * g)


def lanes(g):
    return slice(128 * g, 128 * g + group_width(g))


def land_mask(land):
    spread = jnp.broadcast_to(land.astype(f32)[:, :, None], (2 * TE, TE, C))
    return spread.reshape(CELLS, C)


def zero_lanes(ref):
    ref[...] = jnp.zeros(ref.shape, ref.dtype)


def pack_narrow(tile_rows, even, first_ref, second_ref):
    for ref in (first_ref, second_ref):
        zero_lanes(ref)
    for s in range(2):
        north = tile_rows(s, 0)
        south = tile_rows(s, TE - 3)
        first_ref[s, :, 0:C] = jnp.where(even, south, north).astype(bf16)
        second_ref[s, :, 0:C] = jnp.where(even, north, south).astype(bf16)


def narrow_kernel(field_ref, land_ref, first_ref, second_ref, mask_ref):
    mask_ref[...] = land_mask(land_ref[...].reshape(2 * TE, TE))

    def tile_rows(s, row):
        cells = field_ref[s, row : row + 3].reshape(3 * TE, C).astype(f32)
        at = s * TE * TE + row * TE
        return cells * mask_ref[at : at + 3 * TE, :]

    pack_narrow(tile_rows, lax.axis_index("narrow") % 2 == 0, first_ref, second_ref)


def wide_kernel(masked, *refs):
    if masked:
        tiles_ref, land_ref, n1_ref, n2_ref, first_ref, second_ref, m_ref, r_ref, o_ref = refs
        mask = land_mask(land_ref[...].reshape(2 * TE, TE))
    else:
        tiles_ref, n1_ref, n2_ref, first_ref, second_ref, m_ref, r_ref, o_ref = refs
    n_even = lax.axis_index("narrow") % 2 == 0
    w_even = lax.axis_index("wide") % 2 == 0
    zero_lanes(o_ref)
    for s in range(2):
        cells = tiles_ref[s].reshape(TE * TE, C).astype(f32)
        if masked:
            cells = cells * mask[s * TE * TE : (s + 1) * TE * TE]
        one = n1_ref[s].astype(f32)
        two = n2_ref[s].astype(f32)
        from_north = jnp.where(n_even, two, one)
        from_south = jnp.where(n_even, one, two)
        for g in range(GROUPS):
            m_ref[s, g, :, 0 : group_width(g)] = cells[:, lanes(g)]
            r_ref[0, s, g] = from_north[:, 128 * g : 128 * g + 128]
            r_ref[1, s, g] = from_south[:, 128 * g : 128 * g + 128]
    for s in range(2):
        for g in range(GROUPS):
            w = group_width(g)
            for side in range(2):
                for c in range(3):
                    col = c + side * (TE - 3)
                    at = c * 22
                    o_ref[side, s, g, at : at + 3, :] = r_ref[0, s, g, pl.ds(col, 3, stride=TE), :]
                    o_ref[side, s, g, at + 3 : at + 19, 0:w] = m_ref[s, g, pl.ds(col, TE, stride=TE), 0:w]
                    o_ref[side, s, g, at + 19 : at + 22, :] = r_ref[1, s, g, pl.ds(col, 3, stride=TE), :]
            west = o_ref[0, s, g]
            east = o_ref[1, s, g]
            first_ref[s, :, 128 * g : 128 * g + 128] = jnp.where(w_even, east, west).astype(bf16)
            second_ref[s, :, 128 * g : 128 * g + 128] = jnp.where(w_even, west, east).astype(bf16)


def place_centre(cells, s, p_ref):
    for g in range(GROUPS):
        w = group_width(g)
        for r in range(TE):
            at = (r + 3) * PITCH + 8
            p_ref[s, g, at : at + TE, 0:w] = cells[r * TE : (r + 1) * TE, lanes(g)]


def place_borders(neighbours_ref, n1_ref, n2_ref, w1_ref, w2_ref, p_ref, rn_ref, rw_ref):
    here_w = lax.axis_index("wide")
    here_n = lax.axis_index("narrow")
    here = here_w * lax.axis_size("narrow") + here_n
    n_even = here_n % 2 == 0
    w_even = here_w % 2 == 0
    for s in range(2):
        one = n1_ref[s].astype(f32)
        two = n2_ref[s].astype(f32)
        north = jnp.where(n_even, two, one)
        south = jnp.where(n_even, one, two)
        one = w1_ref[s].astype(f32)
        two = w2_ref[s].astype(f32)
        west = jnp.where(w_even, two, one)
        east = jnp.where(w_even, one, two)
        for g in range(GROUPS):
            at = slice(128 * g, 128 * g + 128)
            rn_ref[0, s, g] = north[:, at]
            rn_ref[1, s, g] = south[:, at]
            rw_ref[0, s, g] = west[:, at]
            rw_ref[1, s, g] = east[:, at]

    def column(t, g):
        def entry(d):
            e = neighbours_ref[t, d]
            near = jnp.maximum(e, 0)
            return e >= 0, near // 2, near % 2

        def chosen(options, present):
            value = options[-1][1]
            for test, other in reversed(options[:-1]):
                value = jnp.where(test, other, value)
            return jnp.where(present, value, 0.0)

        for d in range(2):
            present, device, slot = entry(d)
            from_row = 3 + TE - 3 if d == 0 else 3
            to_row = 0 if d == 0 else 3 + TE
            for i in range(3):
                own = p_ref[slot, g, pl.ds((from_row + i) * PITCH + 8, TE), :]
                other = rn_ref[d, slot, g, pl.ds(i * TE, TE), :]
                p_ref[t, g, pl.ds((to_row + i) * PITCH + 8, TE), :] = chosen(
                    [(device == here, own), (None, other)], present
                )
        for d in range(2):
            present, device, slot = entry(2 + d)
            from_col = 8 + TE - 3 if d == 0 else 8
            to_col = 5 if d == 0 else 8 + TE
            for c in range(3):
                own = p_ref[slot, g, pl.ds(3 * PITCH + from_col + c, TE, stride=PITCH), :]
                other = rw_ref[d, slot, g, pl.ds(c * 22 + 3, TE), :]
                p_ref[t, g, pl.ds(3 * PITCH + to_col + c, TE, stride=PITCH), :] = chosen(
                    [(device == here, own), (None, other)], present
                )
        for d in range(4):
            south, east = d // 2, d % 2
            present, device, slot = entry(4 + d)
            same_w = device // lax.axis_size("narrow") == here_w
            same_n = device % lax.axis_size("narrow") == here_n
            from_row = 3 if south else 3 + TE - 3
            to_row = 3 + TE if south else 0
            from_col = 8 if east else 8 + TE - 3
            to_col = 8 + TE if east else 5
            for c in range(3):
                own = p_ref[slot, g, pl.ds(from_row * PITCH + from_col + c, 3, stride=PITCH), :]
                beyond = rn_ref[south, slot, g, pl.ds(from_col - 8 + c, 3, stride=TE), :]
                beside = rw_ref[east, slot, g, pl.ds(c * 22 + from_row, 3), :]
                across = rw_ref[east, slot, g, pl.ds(c * 22 + (19 if south else 0), 3), :]
                p_ref[t, g, pl.ds(to_row * PITCH + to_col + c, 3, stride=PITCH), :] = chosen(
                    [(device == here, own), (same_w, beyond), (same_n, beside), (None, across)], present
                )

    def step(i, _):
        column(i // GROUPS, i % GROUPS)
        return _

    lax.fori_loop(0, 2 * GROUPS, step, 0)


def weight_rows(weight_ref, g, taps):
    at = pl.ds(pl.multiple_of(g * 128, 128), 128)
    return [jnp.broadcast_to(weight_ref[pl.ds(k, 1), at], (8, 128)) for k in taps]


def convolve(p_ref, weight_ref, start, finish, flip):
    def step(i, _):
        t, g = i // GROUPS, i % GROUPS
        for h in range(2):
            total = start(t, g, h)
            for b in range(7):
                taps = [48 - (7 * a + b) if flip else 7 * a + b for a in range(7)]
                weights = weight_rows(weight_ref, g, taps)
                for row in range(22):
                    x = p_ref[t, g, pl.ds(row * PITCH + 5 + b + 8 * h, 8), :]
                    for a in range(7):
                        r = row - a
                        if 0 <= r < TE:
                            total[r] = total[r] + weights[a] * x
            finish(t, g, h, total)
        return _

    lax.fori_loop(0, 2 * GROUPS, step, 0)


def gelu_pair(hidden):
    square = hidden * hidden
    bent = jnp.tanh(gelu_root * hidden * (1.0 + gelu_cubic * square))
    half = 0.5 * (1.0 + bent)
    slope = half + 0.5 * hidden * (1.0 - bent * bent) * (gelu_root * (1.0 + 3.0 * gelu_cubic * square))
    return hidden * half, slope


def front_kernel(
    neighbours_ref,
    field_ref,
    land_ref,
    cot_ref,
    n1_ref,
    n2_ref,
    w1_ref,
    w2_ref,
    depth_weight_ref,
    depth_bias_ref,
    gain_ref,
    shift_ref,
    up_ref,
    up_bias_ref,
    down_ref,
    cg_ref,
    keep_ref,
    send_ref,
    g1_ref,
    g2_ref,
    p_ref,
    rn_ref,
    rw_ref,
    weight_ref,
    y_ref,
    z_ref,
    r_ref,
    normed_ref,
    normed_t_ref,
    gated_ref,
    gated_t_ref,
    ng_ref,
    dw_ref,
    up_bias_sum_ref,
):
    core0 = lax.axis_index("narrow") % 2 == 0
    p_ref[...] = jnp.zeros(p_ref.shape, f32)
    mask = land_mask(land_ref[...].reshape(2 * TE, TE))
    for s in range(2):
        cells = field_ref[s].reshape(TE * TE, C).astype(f32)
        place_centre(cells * mask[s * TE * TE : (s + 1) * TE * TE], s, p_ref)
    gated = cot_ref[...].reshape(CELLS, C).astype(f32) * mask
    gated_ref[...] = jnp.zeros(gated_ref.shape, bf16)
    gated_ref[:, 0:C] = gated.astype(bf16)
    gated_t_ref[...] = gated_ref[...].T
    down_bias = jnp.sum(gated, axis=0, keepdims=True)
    place_borders(neighbours_ref, n1_ref, n2_ref, w1_ref, w2_ref, p_ref, rn_ref, rw_ref)

    weight_ref[...] = jnp.zeros(weight_ref.shape, f32)
    weight_ref[0:49, 0:C] = depth_weight_ref[...]
    weight_ref[49:50, 0:C] = depth_bias_ref[...]

    def start(t, g, h):
        return weight_rows(weight_ref, g, [49]) * TE

    def finish(t, g, h, rows):
        for r in range(TE):
            at = pl.ds(t * TE * TE + r * TE + 8 * h, 8)
            y_ref[at, pl.ds(pl.multiple_of(g * 128, 128), 128)] = rows[r]

    convolve(p_ref, weight_ref, start, finish, False)

    normed_ref[...] = jnp.zeros(normed_ref.shape, bf16)
    step_rows = 64

    def norm(i, _):
        at = pl.ds(pl.multiple_of(i * step_rows, step_rows), step_rows)
        conv = y_ref[at, 0:C]
        mean = jnp.sum(conv, axis=1, keepdims=True) * (1.0 / C)
        dev = conv - mean
        var = jnp.sum(dev * dev, axis=1, keepdims=True) * (1.0 / C)
        rstd = lax.rsqrt(var + epsilon)
        zhat = dev * rstd
        z_ref[at, :] = zhat
        r_ref[at, :] = jnp.broadcast_to(rstd, (step_rows, 128))
        normed_ref[at, 0:C] = (zhat * gain_ref[...] + shift_ref[...]).astype(bf16)
        return _

    lax.fori_loop(0, CELLS // step_rows, norm, 0)
    normed_t_ref[...] = normed_ref[...].T

    for l in range(EXTRA, TILES):
        keep_ref[l] = jnp.zeros((8, 128), f32)
        send_ref[l] = jnp.zeros((8, 128), bf16)

    def hidden_chunk(lo, width, lane_tile, first):
        at = pl.ds(lo, width)
        up = up_ref[:, at]
        h = jnp.dot(normed_ref[:, 0:C], up, preferred_element_type=f32) + up_bias_ref[:, at]
        act, slope = gelu_pair(h)
        ag = jnp.dot(gated_ref[:, 0:C], down_ref[:, at], preferred_element_type=f32)
        hg = ag * slope
        hgb = hg.astype(bf16)
        dg = jnp.dot(gated_t_ref[0:C, :], act.astype(bf16), preferred_element_type=f32)
        ug = jnp.dot(normed_t_ref[0:C, :], hgb, preferred_element_type=f32)
        ng = lax.dot_general(hgb, up, (((1,), (1,)), ((), ())), preferred_element_type=f32)
        if first:
            ng_ref[...] = ng
        else:
            ng_ref[...] += ng
        up_bias_sum_ref[:, at] = jnp.sum(hgb.astype(f32), axis=0, keepdims=True)
        keep = jnp.where(core0, ug, dg)
        send = jnp.where(core0, dg, ug).astype(bf16)
        for k in range((width + 127) // 128):
            w = min(128, width - 128 * k)
            for i in range(C // 8):
                kt = keep[8 * i : 8 * i + 8, 128 * k : 128 * k + w]
                st = send[8 * i : 8 * i + 8, 128 * k : 128 * k + w]
                l = (lane_tile + k) * (C // 8) + i
                if w < 128:
                    keep_ref[l] = jnp.zeros((8, 128), f32)
                    send_ref[l] = jnp.zeros((8, 128), bf16)
                keep_ref[l, :, 0:w] = kt
                send_ref[l, :, 0:w] = st

    ng_ref[...] = jnp.zeros(ng_ref.shape, f32)

    def more(i, _):
        hidden_chunk(pl.multiple_of(i * 256, 256), 256, 2 * i, False)
        return _

    lax.fori_loop(0, 6, more, 0)
    hidden_chunk(1536, 64, 12, False)

    y_ref[...] = jnp.zeros(y_ref.shape, f32)

    def back(i, sums):
        at = pl.ds(pl.multiple_of(i * step_rows, step_rows), step_rows)
        ng = ng_ref[at, :]
        zhat = z_ref[at, :]
        rstd = r_ref[at, 0:1]
        q = ng * gain_ref[...]
        a = jnp.sum(q, axis=1, keepdims=True) * (1.0 / C)
        b = jnp.sum(q * zhat, axis=1, keepdims=True) * (1.0 / C)
        cg = (rstd * (q - a - zhat * b)).astype(bf16)
        t = i // 4
        cg_ref[t, pl.ds((i % 4) * 4, 4)] = cg.reshape(4, TE, C)
        wide = cg.astype(f32)
        y_ref[at, 0:C] = wide
        return (
            sums[0] + jnp.sum(ng * zhat, axis=0, keepdims=True),
            sums[1] + jnp.sum(ng, axis=0, keepdims=True),
            sums[2] + jnp.sum(wide, axis=0, keepdims=True),
        )

    zero = jnp.zeros((1, C), f32)
    gain_sum, shift_sum, bias_sum = lax.fori_loop(0, CELLS // step_rows, back, (zero, zero, zero))

    def tile_rows(s, row):
        at = s * TE * TE + row * TE
        return y_ref[at : at + 3 * TE, 0:C]

    pack_narrow(tile_rows, core0, g1_ref, g2_ref)

    dw_ref[...] = jnp.zeros(dw_ref.shape, f32)

    def taps(i, _):
        t, g = i // GROUPS, i % GROUPS
        for h in range(2):
            cg = [
                y_ref[
                    pl.ds(t * TE * TE + r * TE + 8 * h, 8),
                    pl.ds(pl.multiple_of(g * 128, 128), 128),
                ]
                for r in range(TE)
            ]
            for b in range(7):
                total = [None] * 7
                for row in range(22):
                    x = p_ref[t, g, pl.ds(row * PITCH + 5 + b + 8 * h, 8), :]
                    for a in range(7):
                        r = row - a
                        if 0 <= r < TE:
                            term = x * cg[r]
                            total[a] = term if total[a] is None else total[a] + term
                for a in range(7):
                    dw_ref[g, 7 * a + b] += total[a]
        return _

    lax.fori_loop(0, 2 * GROUPS, taps, 0)

    for g in range(GROUPS):
        w = group_width(g)
        tap_sums = jnp.sum(dw_ref[g], axis=1)
        for k in range(0, 48, 8):
            keep_ref[EXTRA + g * 8 + k // 8] = tap_sums[k : k + 8]
        tail = EXTRA + g * 8 + 6
        keep_ref[tail, 0:1, :] = tap_sums[48:49]
        keep_ref[tail, 1:2, 0:w] = bias_sum[:, lanes(g)]
        keep_ref[tail, 2:3, 0:w] = gain_sum[:, lanes(g)]
        keep_ref[tail, 3:4, 0:w] = shift_sum[:, lanes(g)]
        keep_ref[tail, 4:5, 0:w] = down_bias[:, lanes(g)]
    for l in range(HT):
        w = min(128, HID - 128 * l)
        keep_ref[EXTRA + 32 + l // 8, l % 8 : l % 8 + 1, 0:w] = up_bias_sum_ref[:, 128 * l : 128 * l + w]


def back_kernel(
    neighbours_ref,
    cg_ref,
    land_ref,
    cot_ref,
    n1_ref,
    n2_ref,
    w1_ref,
    w2_ref,
    depth_weight_ref,
    out_ref,
    p_ref,
    rn_ref,
    rw_ref,
    weight_ref,
    y_ref,
):
    p_ref[...] = jnp.zeros(p_ref.shape, f32)
    for s in range(2):
        place_centre(cg_ref[s].reshape(TE * TE, C).astype(f32), s, p_ref)
    mask = land_mask(land_ref[...].reshape(2 * TE, TE))
    place_borders(neighbours_ref, n1_ref, n2_ref, w1_ref, w2_ref, p_ref, rn_ref, rw_ref)
    weight_ref[...] = jnp.zeros(weight_ref.shape, f32)
    weight_ref[0:49, 0:C] = depth_weight_ref[...]
    y_ref[...] = jnp.zeros(y_ref.shape, f32)
    y_ref[:, 0:C] = cot_ref[...].reshape(CELLS, C).astype(f32) * mask

    def place(t, g, h, r):
        return (
            pl.ds(t * TE * TE + r * TE + 8 * h, 8),
            pl.ds(pl.multiple_of(g * 128, 128), 128),
        )

    def start(t, g, h):
        return [y_ref[place(t, g, h, r)] for r in range(TE)]

    def finish(t, g, h, rows):
        for r in range(TE):
            y_ref[place(t, g, h, r)] = rows[r]

    convolve(p_ref, weight_ref, start, finish, True)
    out_ref[...] = (y_ref[:, 0:C] * mask).astype(bf16).reshape(2, TE, TE, C)


def params():
    return pltpu.CompilerParams(vmem_limit_bytes=48 * 1024 * 1024)


P_SCRATCH = pltpu.VMEM((2, GROUPS, 22 * PITCH, 128), f32)
RN_SCRATCH = pltpu.VMEM((2, 2, GROUPS, 48, 128), f32)
RW_SCRATCH = pltpu.VMEM((2, 2, GROUPS, 80, 128), f32)
W_SCRATCH = pltpu.VMEM((56, CP), f32)
Y_SCRATCH = pltpu.VMEM((CELLS, CP), f32)


def swap_pairs(kind):
    axis, offset = kind
    pairs = []
    for w in range(32):
        for n in range(4):
            if axis == "narrow":
                up = (n - offset) % 2 == 0
                other = (w, (n + (1 if up else -1)) % 4)
            else:
                up = (w - offset) % 2 == 0
                other = ((w + (1 if up else -1)) % 32, n)
            pairs.append((w * 4 + n, other[0] * 4 + other[1]))
    return pairs


def swap(x, kind):
    return lax.ppermute(x, AXES, swap_pairs(kind))


def flip(x, mask):
    return lax.ppermute(x, AXES, [(i, i ^ mask) for i in range(128)])


STAGES = {
    "x1": (2, (1, 6)),
    "x2": (66, (6,)),
    "z1": (4, (2, 3)),
    "z2": (12, (3,)),
    "y1": (16, (4, 5)),
    "y2": (48, (5,)),
}
ORDERS = (
    ("x1", "y1", "z1", "x2", "y2", "z2"),
    ("y1", "z1", "x1", "y2", "z2", "x2"),
    ("z1", "x1", "y1", "z2", "x2", "y2"),
)
DEPTH = 2


def parity(me, bits):
    return sum((me >> bit) & 1 for bit in bits) & 1


def sum_over_chips(total, me, orders):
    size = total.shape[0] // len(orders)
    parts = [total[i * size : (i + 1) * size] for i in range(len(orders))]
    for stage in range(DEPTH):
        steps = []
        for order, part in zip(orders, parts):
            mask, bits = STAGES[order[stage]]
            high = parity(me, bits)
            half = part.shape[0] // 2
            send = lax.dynamic_slice_in_dim(part, (1 - high) * half, half, 0).astype(bf16)
            keep = lax.dynamic_slice_in_dim(part, high * half, half, 0)
            steps.append((keep, flip(send, mask)))
        parts = [keep + got.astype(f32) for keep, got in steps]
    for stage in range(DEPTH, 6):
        steps = []
        for order, part in zip(orders, parts):
            mine = part.astype(bf16)
            steps.append((mine, flip(mine, STAGES[order[stage]][0])))
        parts = [mine.astype(f32) + got.astype(f32) for mine, got in steps]
    parts = [part.astype(bf16) for part in parts]
    for stage in reversed(range(DEPTH)):
        steps = []
        for order, part in zip(orders, parts):
            mask, bits = STAGES[order[stage]]
            low = parity(me, bits) == 0
            got = flip(part, mask)
            steps.append(
                jnp.concatenate([jnp.where(low, part, got), jnp.where(low, got, part)], axis=0)
            )
        parts = steps
    return jnp.concatenate(parts, axis=0)


def local(
    field,
    cotangent,
    land,
    neighbours,
    depth_weight,
    depth_bias,
    ln_gain,
    ln_shift,
    up_weight,
    up_bias,
    down_weight,
):
    me = lax.axis_index("wide") * 4 + lax.axis_index("narrow")
    core = lax.axis_index("narrow") % 2
    narrow_shape = jax.ShapeDtypeStruct((2, 48, CP), bf16)
    wide_shape = jax.ShapeDtypeStruct((2, 80, CP), bf16)
    wide_scratch = [
        pltpu.VMEM((2, GROUPS, TE * TE, 128), f32),
        RN_SCRATCH,
        RW_SCRATCH,
    ]

    s1, s2 = pl.pallas_call(
        narrow_kernel,
        out_shape=(narrow_shape, narrow_shape),
        in_specs=[VMEM] * 2,
        out_specs=(VMEM, VMEM),
        scratch_shapes=[pltpu.VMEM((CELLS, C), f32)],
        compiler_params=params(),
        name="pack_rows",
    )(field, land)
    n1, n2 = swap(s1, ("narrow", 0)), swap(s2, ("narrow", 1))
    s1, s2 = pl.pallas_call(
        functools.partial(wide_kernel, True),
        out_shape=(wide_shape, wide_shape),
        in_specs=[VMEM] * 4,
        out_specs=(VMEM, VMEM),
        scratch_shapes=wide_scratch,
        compiler_params=params(),
        name="pack_columns",
    )(field, land, n1, n2)
    w1, w2 = swap(s1, ("wide", 0)), swap(s2, ("wide", 1))

    row = lambda v: v.reshape(1, -1)
    cg, keep, send, g1, g2 = pl.pallas_call(
        front_kernel,
        out_shape=(
            jax.ShapeDtypeStruct((2, TE, TE, C), bf16),
            jax.ShapeDtypeStruct((TILES, 8, 128), f32),
            jax.ShapeDtypeStruct((TILES, 8, 128), bf16),
            narrow_shape,
            narrow_shape,
        ),
        in_specs=[SMEM] + [VMEM] * 14,
        out_specs=(VMEM,) * 5,
        scratch_shapes=[
            P_SCRATCH,
            RN_SCRATCH,
            RW_SCRATCH,
            W_SCRATCH,
            Y_SCRATCH,
            pltpu.VMEM((CELLS, C), f32),
            pltpu.VMEM((CELLS, 128), f32),
            pltpu.VMEM((CELLS, CP), bf16),
            pltpu.VMEM((CP, CELLS), bf16),
            pltpu.VMEM((CELLS, CP), bf16),
            pltpu.VMEM((CP, CELLS), bf16),
            pltpu.VMEM((CELLS, C), f32),
            pltpu.VMEM((GROUPS, 49, 8, 128), f32),
            pltpu.VMEM((1, HID), f32),
        ],
        compiler_params=params(),
        name="front",
    )(
        neighbours,
        field,
        land,
        cotangent,
        n1,
        n2,
        w1,
        w2,
        depth_weight,
        row(depth_bias),
        row(ln_gain),
        row(ln_shift),
        up_weight,
        row(up_bias),
        down_weight.T,
    )

    got = flip(send, 1)
    n1, n2 = swap(g1, ("narrow", 0)), swap(g2, ("narrow", 1))
    s1, s2 = pl.pallas_call(
        functools.partial(wide_kernel, False),
        out_shape=(wide_shape, wide_shape),
        in_specs=[VMEM] * 3,
        out_specs=(VMEM, VMEM),
        scratch_shapes=wide_scratch,
        compiler_params=params(),
        name="pack_columns_back",
    )(cg, n1, n2)
    w1, w2 = swap(s1, ("wide", 0)), swap(s2, ("wide", 1))
    field_grad = pl.pallas_call(
        back_kernel,
        out_shape=jax.ShapeDtypeStruct((2, TE, TE, C), bf16),
        in_specs=[SMEM] + [VMEM] * 8,
        out_specs=VMEM,
        scratch_shapes=[P_SCRATCH, RN_SCRATCH, RW_SCRATCH, W_SCRATCH, Y_SCRATCH],
        compiler_params=params(),
        name="back",
    )(neighbours, cg, land, cotangent, n1, n2, w1, w2, depth_weight)

    mine = sum_over_chips(keep + got.astype(f32), me, ORDERS)
    theirs = flip(mine, 1)
    up_part = jnp.where(core == 0, mine, theirs)[0:EXTRA].astype(f32)
    down_part = jnp.where(core == 0, theirs, mine)[0:EXTRA].astype(f32)
    extra = mine[EXTRA:].astype(f32) + theirs[EXTRA:].astype(f32)

    def weight_grad(part):
        return jnp.transpose(part.reshape(HT, C, 128), (1, 0, 2)).reshape(C, HT * 128)[:, 0:HID]

    channel = jnp.transpose(extra[0:32].reshape(GROUPS, 64, 128), (1, 0, 2)).reshape(64, CP)[:, 0:C]
    up_bias_grad = extra[32:34].reshape(-1)[0:HID]
    return (
        field_grad,
        channel[0:49],
        channel[49],
        channel[50],
        channel[51],
        weight_grad(up_part),
        up_bias_grad,
        weight_grad(down_part).T,
        channel[52],
    )


def solution(mesh):
    return jax.shard_map(
        local,
        mesh=mesh,
        in_specs=(
            P(("wide", "narrow"), None, None, None),
            P(("wide", "narrow"), None, None, None),
            P(("wide", "narrow"), None, None),
            P(("wide", "narrow"), None),
            P(),
            P(),
            P(),
            P(),
            P(),
            P(),
            P(),
        ),
        out_specs=(P(("wide", "narrow"), None, None, None), P(), P(), P(), P(), P(), P(), P(), P()),
        check_vma=False,
    )
```

```python
import functools

import jax
import jax.numpy as jnp
from jax import lax
from jax.experimental import pallas as pl
from jax.experimental.pallas import tpu as pltpu
from jax.sharding import PartitionSpec as P

epsilon = 1e-06
gelu_root = 0.7978845608028654
gelu_cubic = 0.044715

C = 400
CP = 512
HID = 1600
TE = 16
CELLS = 512
GROUPS = 4
HT = 13
PITCH = 32
ROWS = HT * C
EXTRA = 368
PARTS = 3
AXES = ("wide", "narrow")
f32 = jnp.float32
bf16 = jnp.bfloat16
VMEM = pl.BlockSpec(memory_space=pltpu.VMEM)
SMEM = pl.BlockSpec(memory_space=pltpu.SMEM)
ANY = pl.BlockSpec(memory_space=pl.ANY)


def group_width(g):
    return min(128, C - 128 * g)


def lanes(g):
    return slice(128 * g, 128 * g + group_width(g))


def land_mask(land):
    spread = jnp.broadcast_to(land.astype(f32)[:, :, None], (2 * TE, TE, C))
    return spread.reshape(CELLS, C)


def zero_lanes(ref):
    ref[...] = jnp.zeros(ref.shape, ref.dtype)


def pack_narrow(tile_rows, even, first_ref, second_ref):
    for ref in (first_ref, second_ref):
        zero_lanes(ref)
    for s in range(2):
        north = tile_rows(s, 0)
        south = tile_rows(s, TE - 3)
        first_ref[s, :, 0:C] = jnp.where(even, south, north).astype(bf16)
        second_ref[s, :, 0:C] = jnp.where(even, north, south).astype(bf16)


def narrow_kernel(field_ref, land_ref, first_ref, second_ref, rows_ref, cells_ref, sems):
    copies = [pltpu.make_async_copy(land_ref, cells_ref, sems.at[4])]
    for s in range(2):
        for k, row in enumerate((0, TE - 3)):
            copies.append(
                pltpu.make_async_copy(field_ref.at[s, pl.ds(row, 3)], rows_ref.at[s, k], sems.at[2 * s + k])
            )
    for copy in copies:
        copy.start()
    for copy in copies:
        copy.wait()

    def tile_rows(s, row):
        cells = rows_ref[s, 1 if row else 0].reshape(3 * TE, C).astype(f32)
        land = cells_ref[s, row : row + 3].astype(f32)
        return cells * jnp.broadcast_to(land[:, :, None], (3, TE, C)).reshape(3 * TE, C)

    pack_narrow(tile_rows, lax.axis_index("narrow") % 2 == 0, first_ref, second_ref)


def wide_kernel(masked, *refs):
    if masked:
        tiles_ref, land_ref, n1_ref, n2_ref, first_ref, second_ref, m_ref, r_ref, o_ref = refs
        mask = land_mask(land_ref[...].reshape(2 * TE, TE))
    else:
        tiles_ref, n1_ref, n2_ref, first_ref, second_ref, m_ref, r_ref, o_ref = refs
    n_even = lax.axis_index("narrow") % 2 == 0
    w_even = lax.axis_index("wide") % 2 == 0
    zero_lanes(o_ref)
    for s in range(2):
        cells = tiles_ref[s].reshape(TE * TE, C).astype(f32)
        if masked:
            cells = cells * mask[s * TE * TE : (s + 1) * TE * TE]
        one = n1_ref[s].astype(f32)
        two = n2_ref[s].astype(f32)
        from_north = jnp.where(n_even, two, one)
        from_south = jnp.where(n_even, one, two)
        for g in range(GROUPS):
            m_ref[s, g, :, 0 : group_width(g)] = cells[:, lanes(g)]
            r_ref[0, s, g] = from_north[:, 128 * g : 128 * g + 128]
            r_ref[1, s, g] = from_south[:, 128 * g : 128 * g + 128]
    for s in range(2):
        for g in range(GROUPS):
            w = group_width(g)
            for side in range(2):
                for c in range(3):
                    col = c + side * (TE - 3)
                    at = c * 22
                    o_ref[side, s, g, at : at + 3, :] = r_ref[0, s, g, pl.ds(col, 3, stride=TE), :]
                    o_ref[side, s, g, at + 3 : at + 19, 0:w] = m_ref[s, g, pl.ds(col, TE, stride=TE), 0:w]
                    o_ref[side, s, g, at + 19 : at + 22, :] = r_ref[1, s, g, pl.ds(col, 3, stride=TE), :]
            west = o_ref[0, s, g]
            east = o_ref[1, s, g]
            first_ref[s, :, 128 * g : 128 * g + 128] = jnp.where(w_even, east, west).astype(bf16)
            second_ref[s, :, 128 * g : 128 * g + 128] = jnp.where(w_even, west, east).astype(bf16)


def place_centre(cells, s, p_ref):
    for g in range(GROUPS):
        w = group_width(g)
        for r in range(TE):
            at = (r + 3) * PITCH + 8
            p_ref[s, g, at : at + TE, 0:w] = cells[r * TE : (r + 1) * TE, lanes(g)]


def place_rows(n1_ref, n2_ref, rn_ref):
    n_even = lax.axis_index("narrow") % 2 == 0
    for s in range(2):
        one = n1_ref[s].astype(f32)
        two = n2_ref[s].astype(f32)
        north = jnp.where(n_even, two, one)
        south = jnp.where(n_even, one, two)
        for g in range(GROUPS):
            at = slice(128 * g, 128 * g + 128)
            rn_ref[0, s, g] = north[:, at]
            rn_ref[1, s, g] = south[:, at]


def place_columns(w1_ref, w2_ref, rw_ref):
    w_even = lax.axis_index("wide") % 2 == 0
    for s in range(2):
        one = w1_ref[s].astype(f32)
        two = w2_ref[s].astype(f32)
        west = jnp.where(w_even, two, one)
        east = jnp.where(w_even, one, two)
        for g in range(GROUPS):
            at = slice(128 * g, 128 * g + 128)
            rw_ref[0, s, g] = west[:, at]
            rw_ref[1, s, g] = east[:, at]


def entry_of(neighbours_ref, t, d):
    e = neighbours_ref[t, d]
    near = jnp.maximum(e, 0)
    return e >= 0, near // 2, near % 2


def chosen(options, present):
    value = options[-1][1]
    for test, other in reversed(options[:-1]):
        value = jnp.where(test, other, value)
    return jnp.where(present, value, 0.0)


def here():
    return lax.axis_index("wide") * lax.axis_size("narrow") + lax.axis_index("narrow")


def border_rows(neighbours_ref, p_ref, rn_ref, t, g):
    for d in range(2):
        present, device, slot = entry_of(neighbours_ref, t, d)
        from_row = 3 + TE - 3 if d == 0 else 3
        to_row = 0 if d == 0 else 3 + TE
        for i in range(3):
            own = p_ref[slot, g, pl.ds((from_row + i) * PITCH + 8, TE), :]
            other = rn_ref[d, slot, g, pl.ds(i * TE, TE), :]
            p_ref[t, g, pl.ds((to_row + i) * PITCH + 8, TE), :] = chosen(
                [(device == here(), own), (None, other)], present
            )


def border_columns(neighbours_ref, p_ref, rn_ref, rw_ref, t, g, put):
    narrow = lax.axis_size("narrow")
    for d in range(2):
        present, device, slot = entry_of(neighbours_ref, t, 2 + d)
        from_col = 8 + TE - 3 if d == 0 else 8
        for c in range(3):
            own = p_ref[slot, g, pl.ds(3 * PITCH + from_col + c, TE, stride=PITCH), :]
            other = rw_ref[d, slot, g, pl.ds(c * 22 + 3, TE), :]
            put(d, c, 3, TE, chosen([(device == here(), own), (None, other)], present))
    for d in range(4):
        south, east = d // 2, d % 2
        present, device, slot = entry_of(neighbours_ref, t, 4 + d)
        same_w = device // narrow == lax.axis_index("wide")
        same_n = device % narrow == lax.axis_index("narrow")
        from_row = 3 if south else 3 + TE - 3
        to_row = 3 + TE if south else 0
        from_col = 8 if east else 8 + TE - 3
        for c in range(3):
            own = p_ref[slot, g, pl.ds(from_row * PITCH + from_col + c, 3, stride=PITCH), :]
            beyond = rn_ref[south, slot, g, pl.ds(from_col - 8 + c, 3, stride=TE), :]
            beside = rw_ref[east, slot, g, pl.ds(c * 22 + from_row, 3), :]
            across = rw_ref[east, slot, g, pl.ds(c * 22 + (19 if south else 0), 3), :]
            put(
                east,
                c,
                to_row,
                3,
                chosen(
                    [(device == here(), own), (same_w, beyond), (same_n, beside), (None, across)], present
                ),
            )


def column_in(p_ref, t, g):
    def put(side, c, row, count, value):
        at = row * PITCH + (8 + TE if side else 5) + c
        p_ref[t, g, pl.ds(at, count, stride=PITCH), :] = value

    return put


def each_group(body):
    def step(i, _):
        body(i // GROUPS, i % GROUPS)
        return _

    lax.fori_loop(0, 2 * GROUPS, step, 0)


def weight_rows(weight_ref, g, taps):
    at = pl.ds(pl.multiple_of(g * 128, 128), 128)
    return [jnp.broadcast_to(weight_ref[pl.ds(k, 1), at], (8, 128)) for k in taps]


def convolve(p_ref, weight_ref, start, finish, flip):
    def body(t, g):
        for h in range(2):
            total = start(t, g, h)
            for b in range(7):
                taps = [48 - (7 * a + b) if flip else 7 * a + b for a in range(7)]
                weights = weight_rows(weight_ref, g, taps)
                for row in range(22):
                    x = p_ref[t, g, pl.ds(row * PITCH + 5 + b + 8 * h, 8), :]
                    for a in range(7):
                        r = row - a
                        if 0 <= r < TE:
                            total[r] = total[r] + weights[a] * x
            finish(t, g, h, total)

    each_group(body)


def gelu_pair(hidden):
    square = hidden * hidden
    bent = jnp.tanh(gelu_root * hidden * (1.0 + gelu_cubic * square))
    half = 0.5 * (1.0 + bent)
    slope = half + 0.5 * hidden * (1.0 - bent * bent) * (gelu_root * (1.0 + 3.0 * gelu_cubic * square))
    return hidden * half, slope


def take_weights(weight_ref, depth_weight_ref):
    weight_ref[...] = jnp.zeros(weight_ref.shape, f32)
    weight_ref[0:49, 0:C] = depth_weight_ref[...]


def prep_kernel(
    neighbours_ref,
    field_ref,
    land_ref,
    cot_ref,
    n1_ref,
    n2_ref,
    depth_weight_ref,
    small_ref,
    up_ref,
    down_ref,
    p_ref,
    y_ref,
    gated_ref,
    gated_t_ref,
    down_bias_ref,
    up_out_ref,
    down_out_ref,
    rn_ref,
    weight_ref,
    taps_ref,
    cot_in_ref,
    sems,
):
    copies = [
        pltpu.make_async_copy(depth_weight_ref, taps_ref, sems.at[0]),
        pltpu.make_async_copy(cot_ref, cot_in_ref, sems.at[1]),
        pltpu.make_async_copy(up_ref, up_out_ref, sems.at[2]),
        pltpu.make_async_copy(down_ref, down_out_ref, sems.at[3]),
    ]
    for copy in copies:
        copy.start()
    p_ref[...] = jnp.zeros(p_ref.shape, f32)
    mask = land_mask(land_ref[...].reshape(2 * TE, TE))
    for s in range(2):
        cells = field_ref[s].reshape(TE * TE, C).astype(f32)
        place_centre(cells * mask[s * TE * TE : (s + 1) * TE * TE], s, p_ref)
    place_rows(n1_ref, n2_ref, rn_ref)
    each_group(lambda t, g: border_rows(neighbours_ref, p_ref, rn_ref, t, g))
    copies[0].wait()
    take_weights(weight_ref, taps_ref)
    weight_ref[49:50, 0:C] = small_ref[0:1, 0:C]

    def start(t, g, h):
        return weight_rows(weight_ref, g, [49]) * TE

    def finish(t, g, h, rows):
        for r in range(TE):
            y_ref[t, g, pl.ds(r * TE + 8 * h, 8), :] = rows[r]

    convolve(p_ref, weight_ref, start, finish, False)

    copies[1].wait()
    gated = cot_in_ref[...].reshape(CELLS, C).astype(f32) * mask
    gated_ref[...] = jnp.zeros(gated_ref.shape, bf16)
    gated_ref[:, 0:C] = gated.astype(bf16)
    gated_t_ref[...] = gated_ref[...].T
    down_bias_ref[...] = jnp.sum(gated, axis=0, keepdims=True)
    copies[2].wait()
    copies[3].wait()


def front_kernel(
    neighbours_ref,
    n1_ref,
    n2_ref,
    w1_ref,
    w2_ref,
    p_ref,
    y_in_ref,
    gated_ref,
    gated_t_ref,
    depth_weight_ref,
    small_ref,
    up_ref,
    down_ref,
    keep_ref,
    send_ref,
    ng_ref,
    z_ref,
    r_ref,
    up_bias_sum_ref,
    border_ref,
    rn_ref,
    rw_ref,
    weight_ref,
    y_ref,
    normed_ref,
    normed_t_ref,
):
    core0 = lax.axis_index("narrow") % 2 == 0
    place_rows(n1_ref, n2_ref, rn_ref)
    place_columns(w1_ref, w2_ref, rw_ref)
    take_weights(weight_ref, depth_weight_ref)
    y_ref[...] = y_in_ref[...]

    def sides(t, g):
        def put(side, c, row, count, value):
            border_ref[t, g, pl.ds((side * 3 + c) * 24 + row, count), :] = value

        border_columns(neighbours_ref, p_ref, rn_ref, rw_ref, t, g, put)
        at = pl.ds(pl.multiple_of(g * 128, 128), 128)
        for side in range(2):
            for out in range(3):
                col = out + side * (TE - 3)
                total = y_ref[t, g, pl.ds(col, TE, stride=TE), :]
                for c in range(3):
                    b = (19 + c if side else c) - col
                    if 0 <= b < 7:
                        for a in range(7):
                            cells = border_ref[t, g, pl.ds((side * 3 + c) * 24 + a, TE), :]
                            total = total + weight_ref[pl.ds(7 * a + b, 1), at] * cells
                y_ref[t, g, pl.ds(col, TE, stride=TE), :] = total

    each_group(sides)

    normed_ref[...] = jnp.zeros(normed_ref.shape, bf16)
    step_rows = 64

    def norm(i, _):
        at = pl.ds(pl.multiple_of(i * step_rows, step_rows), step_rows)
        inside = pl.ds(pl.multiple_of((i % 4) * step_rows, step_rows), step_rows)
        conv = jnp.concatenate([y_ref[i // 4, g, inside, :] for g in range(GROUPS)], axis=1)[:, 0:C]
        mean = jnp.sum(conv, axis=1, keepdims=True) * (1.0 / C)
        dev = conv - mean
        var = jnp.sum(dev * dev, axis=1, keepdims=True) * (1.0 / C)
        rstd = lax.rsqrt(var + epsilon)
        zhat = dev * rstd
        z_ref[at, :] = zhat
        r_ref[at, :] = jnp.broadcast_to(rstd, (step_rows, 128))
        normed_ref[at, 0:C] = (zhat * small_ref[1:2, 0:C] + small_ref[2:3, 0:C]).astype(bf16)
        return _

    lax.fori_loop(0, CELLS // step_rows, norm, 0)
    normed_t_ref[...] = normed_ref[...].T

    def hidden_chunk(lo, width, lane_tile):
        at = pl.ds(lo, width)
        up = up_ref[:, at]
        h = jnp.dot(normed_ref[:, 0:C], up, preferred_element_type=f32) + small_ref[3:4, at]
        act, slope = gelu_pair(h)
        ag = jnp.dot(gated_ref[:, 0:C], down_ref[:, at], preferred_element_type=f32)
        hg = ag * slope
        hgb = hg.astype(bf16)
        dg = jnp.dot(gated_t_ref[0:C, :], act.astype(bf16), preferred_element_type=f32)
        ug = jnp.dot(normed_t_ref[0:C, :], hgb, preferred_element_type=f32)
        ng_ref[...] += lax.dot_general(hgb, up, (((1,), (1,)), ((), ())), preferred_element_type=f32)
        up_bias_sum_ref[:, at] = jnp.sum(hgb.astype(f32), axis=0, keepdims=True)
        keep = jnp.where(core0, ug, dg)
        send = jnp.where(core0, dg, ug).astype(bf16)
        for k in range((width + 127) // 128):
            w = min(128, width - 128 * k)
            rows = pl.ds(pl.multiple_of((lane_tile + k) * C, C), C)
            if w < 128:
                keep_ref[rows, :] = jnp.zeros((C, 128), f32)
                send_ref[rows, :] = jnp.zeros((C, 128), bf16)
            keep_ref[rows, 0:w] = keep[:, 128 * k : 128 * k + w]
            send_ref[rows, 0:w] = send[:, 128 * k : 128 * k + w]

    ng_ref[...] = jnp.zeros(ng_ref.shape, f32)

    def more(i, _):
        hidden_chunk(pl.multiple_of(i * 256, 256), 256, 2 * i)
        return _

    lax.fori_loop(0, 6, more, 0)
    hidden_chunk(1536, 64, 12)


def grad_kernel(
    ng_ref,
    z_ref,
    r_ref,
    small_ref,
    p_in_ref,
    border_ref,
    up_bias_sum_ref,
    down_bias_ref,
    cg_ref,
    g1_ref,
    g2_ref,
    extra_ref,
    p_ref,
    y_ref,
    dw_ref,
):
    y_ref[...] = jnp.zeros(y_ref.shape, f32)
    step_rows = 64

    def back(i, sums):
        at = pl.ds(pl.multiple_of(i * step_rows, step_rows), step_rows)
        ng = ng_ref[at, :]
        zhat = z_ref[at, :]
        rstd = r_ref[at, 0:1]
        q = ng * small_ref[1:2, 0:C]
        a = jnp.sum(q, axis=1, keepdims=True) * (1.0 / C)
        b = jnp.sum(q * zhat, axis=1, keepdims=True) * (1.0 / C)
        cg = (rstd * (q - a - zhat * b)).astype(bf16)
        cg_ref[i // 4, pl.ds((i % 4) * 4, 4)] = cg.reshape(4, TE, C)
        wide = cg.astype(f32)
        y_ref[at, 0:C] = wide
        return (
            sums[0] + jnp.sum(ng * zhat, axis=0, keepdims=True),
            sums[1] + jnp.sum(ng, axis=0, keepdims=True),
            sums[2] + jnp.sum(wide, axis=0, keepdims=True),
        )

    zero = jnp.zeros((1, C), f32)
    gain_sum, shift_sum, bias_sum = lax.fori_loop(0, CELLS // step_rows, back, (zero, zero, zero))

    def tile_rows(s, row):
        at = s * TE * TE + row * TE
        return y_ref[at : at + 3 * TE, 0:C]

    pack_narrow(tile_rows, lax.axis_index("narrow") % 2 == 0, g1_ref, g2_ref)

    p_ref[...] = p_in_ref[...]
    dw_ref[...] = jnp.zeros(dw_ref.shape, f32)

    def taps(t, g):
        put = column_in(p_ref, t, g)
        for side in range(2):
            for c in range(3):
                put(side, c, 0, 22, border_ref[t, g, pl.ds((side * 3 + c) * 24, 22), :])
        for h in range(2):
            cg = [
                y_ref[
                    pl.ds(t * TE * TE + r * TE + 8 * h, 8),
                    pl.ds(pl.multiple_of(g * 128, 128), 128),
                ]
                for r in range(TE)
            ]
            for b in range(7):
                total = [None] * 7
                for row in range(22):
                    x = p_ref[t, g, pl.ds(row * PITCH + 5 + b + 8 * h, 8), :]
                    for a in range(7):
                        r = row - a
                        if 0 <= r < TE:
                            term = x * cg[r]
                            total[a] = term if total[a] is None else total[a] + term
                for a in range(7):
                    dw_ref[g, 7 * a + b] += total[a]

    each_group(taps)

    extra_ref[...] = jnp.zeros(extra_ref.shape, f32)
    for g in range(GROUPS):
        w = group_width(g)
        extra_ref[g * 64 : g * 64 + 49, :] = jnp.sum(dw_ref[g], axis=1)
        extra_ref[g * 64 + 49 : g * 64 + 50, 0:w] = bias_sum[:, lanes(g)]
        extra_ref[g * 64 + 50 : g * 64 + 51, 0:w] = gain_sum[:, lanes(g)]
        extra_ref[g * 64 + 51 : g * 64 + 52, 0:w] = shift_sum[:, lanes(g)]
        extra_ref[g * 64 + 52 : g * 64 + 53, 0:w] = down_bias_ref[:, lanes(g)]
    for l in range(HT):
        w = min(128, HID - 128 * l)
        extra_ref[256 + l : 257 + l, 0:w] = up_bias_sum_ref[:, 128 * l : 128 * l + w]


def split_kernel(keep_ref, got_ref, extra_ref, *refs):
    me = here()
    size = (ROWS + EXTRA) // PARTS
    half = size // 2
    for i in range(PARTS):
        send_ref, mine_ref = refs[i], refs[PARTS + i]
        high = parity(me, STAGES[ORDERS[i][0]][1])
        for j in range(2):
            lo = i * size + j * half
            inner = min(half, ROWS - lo)

            def value(a, b):
                return keep_ref[a:b, :] + got_ref[a:b, :].astype(f32)

            def store(ref):
                ref[0:inner, :] = value(lo, lo + inner).astype(ref.dtype)
                if inner < half:
                    ref[inner:half, :] = extra_ref[0 : half - inner, :].astype(ref.dtype)

            pl.when(high == j)(functools.partial(store, mine_ref))
            pl.when(high != j)(functools.partial(store, send_ref))


def unpack_kernel(mine_ref, theirs_ref, up_ref, down_ref, channel_ref, up_bias_ref):
    core0 = lax.axis_index("narrow") % 2 == 0
    for l in range(HT):
        w = min(128, HID - 128 * l)
        rows = slice(l * C, l * C + C)
        one = mine_ref[rows, :].astype(f32)
        two = theirs_ref[rows, :].astype(f32)
        up_ref[:, 128 * l : 128 * l + w] = jnp.where(core0, one, two)[:, 0:w]
        down_ref[:, 128 * l : 128 * l + w] = jnp.where(core0, two, one)[:, 0:w]
    extra = mine_ref[ROWS:, :].astype(f32) + theirs_ref[ROWS:, :].astype(f32)
    for g in range(GROUPS):
        channel_ref[:, lanes(g)] = extra[g * 64 : g * 64 + 56, 0 : group_width(g)]
    up_bias_ref[...] = extra[256:272]


def back_kernel(
    neighbours_ref,
    cg_ref,
    land_ref,
    cot_ref,
    n1_ref,
    n2_ref,
    w1_ref,
    w2_ref,
    depth_weight_ref,
    out_ref,
    p_ref,
    rn_ref,
    rw_ref,
    weight_ref,
    y_ref,
):
    p_ref[...] = jnp.zeros(p_ref.shape, f32)
    for s in range(2):
        place_centre(cg_ref[s].reshape(TE * TE, C).astype(f32), s, p_ref)
    mask = land_mask(land_ref[...].reshape(2 * TE, TE))
    place_rows(n1_ref, n2_ref, rn_ref)
    place_columns(w1_ref, w2_ref, rw_ref)

    def borders(t, g):
        border_rows(neighbours_ref, p_ref, rn_ref, t, g)
        border_columns(neighbours_ref, p_ref, rn_ref, rw_ref, t, g, column_in(p_ref, t, g))

    each_group(borders)
    take_weights(weight_ref, depth_weight_ref)
    y_ref[...] = jnp.zeros(y_ref.shape, f32)
    y_ref[:, 0:C] = cot_ref[...].reshape(CELLS, C).astype(f32) * mask

    def place(t, g, h, r):
        return (
            pl.ds(t * TE * TE + r * TE + 8 * h, 8),
            pl.ds(pl.multiple_of(g * 128, 128), 128),
        )

    def start(t, g, h):
        return [y_ref[place(t, g, h, r)] for r in range(TE)]

    def finish(t, g, h, rows):
        for r in range(TE):
            y_ref[place(t, g, h, r)] = rows[r]

    convolve(p_ref, weight_ref, start, finish, True)
    out_ref[...] = (y_ref[:, 0:C] * mask).astype(bf16).reshape(2, TE, TE, C)


def params(size=16):
    return pltpu.CompilerParams(vmem_limit_bytes=size * 1024 * 1024)


P_SCRATCH = pltpu.VMEM((2, GROUPS, 22 * PITCH, 128), f32)
RN_SCRATCH = pltpu.VMEM((2, 2, GROUPS, 48, 128), f32)
RW_SCRATCH = pltpu.VMEM((2, 2, GROUPS, 80, 128), f32)
W_SCRATCH = pltpu.VMEM((56, CP), f32)
Y_SCRATCH = pltpu.VMEM((CELLS, CP), f32)


def swap_pairs(kind):
    axis, offset = kind
    pairs = []
    for w in range(32):
        for n in range(4):
            if axis == "narrow":
                up = (n - offset) % 2 == 0
                other = (w, (n + (1 if up else -1)) % 4)
            else:
                up = (w - offset) % 2 == 0
                other = ((w + (1 if up else -1)) % 32, n)
            pairs.append((w * 4 + n, other[0] * 4 + other[1]))
    return pairs


def swap(x, kind):
    return lax.ppermute(x, AXES, swap_pairs(kind))


def flip(x, mask):
    return lax.ppermute(x, AXES, [(i, i ^ mask) for i in range(128)])


STAGES = {
    "x1": (2, (1, 6)),
    "x2": (66, (6,)),
    "z1": (4, (2, 3)),
    "z2": (12, (3,)),
    "y1": (16, (4, 5)),
    "y2": (48, (5,)),
}
ORDERS = (
    ("x1", "y1", "z1", "x2", "y2", "z2"),
    ("y1", "z1", "x1", "y2", "z2", "x2"),
    ("z1", "x1", "y1", "z2", "x2", "y2"),
)
DEPTH = 2


def parity(me, bits):
    return sum((me >> bit) & 1 for bit in bits) & 1


def halved(part, order, stage, me):
    mask, bits = STAGES[order[stage]]
    high = parity(me, bits)
    half = part.shape[0] // 2
    send = lax.dynamic_slice_in_dim(part, (1 - high) * half, half, 0).astype(bf16)
    keep = lax.dynamic_slice_in_dim(part, high * half, half, 0)
    return keep + flip(send, mask).astype(f32)


def doubled(part, order, stage):
    mine = part.astype(bf16)
    return mine.astype(f32) + flip(mine, STAGES[order[stage]][0]).astype(f32)


def joined(part, order, stage, me):
    mask, bits = STAGES[order[stage]]
    low = parity(me, bits) == 0
    got = flip(part, mask)
    return jnp.concatenate([jnp.where(low, part, got), jnp.where(low, got, part)], axis=0)


def together(*values):
    return lax.optimization_barrier(values)


def local(
    field,
    cotangent,
    land,
    neighbours,
    depth_weight,
    depth_bias,
    ln_gain,
    ln_shift,
    up_weight,
    up_bias,
    down_weight,
):
    me = here()
    shape = jax.ShapeDtypeStruct
    narrow_shape = shape((2, 48, CP), bf16)
    wide_shape = shape((2, 80, CP), bf16)
    wide_scratch = [
        pltpu.VMEM((2, GROUPS, TE * TE, 128), f32),
        RN_SCRATCH,
        RW_SCRATCH,
    ]
    p_shape = shape((2, GROUPS, 22 * PITCH, 128), f32)
    small = jnp.stack(
        [jnp.pad(v, (0, HID - C)) for v in (depth_bias, ln_gain, ln_shift)] + [up_bias]
    )

    s1, s2 = pl.pallas_call(
        narrow_kernel,
        out_shape=(narrow_shape, narrow_shape),
        in_specs=[ANY] * 2,
        out_specs=(VMEM, VMEM),
        scratch_shapes=[
            pltpu.VMEM((2, 2, 3, TE, C), bf16),
            pltpu.VMEM((2, TE, TE), jnp.int32),
            pltpu.SemaphoreType.DMA((5,)),
        ],
        compiler_params=params(),
        name="pack_rows",
    )(field, land)
    n1, n2 = swap(s1, ("narrow", 0)), swap(s2, ("narrow", 1))
    s1, s2 = pl.pallas_call(
        functools.partial(wide_kernel, True),
        out_shape=(wide_shape, wide_shape),
        in_specs=[VMEM] * 4,
        out_specs=(VMEM, VMEM),
        scratch_shapes=wide_scratch,
        compiler_params=params(),
        name="pack_columns",
    )(field, land, n1, n2)
    s1, s2, n1, n2 = together(s1, s2, n1, n2)
    w2, w1 = swap(s2, ("wide", 1)), swap(s1, ("wide", 0))
    p, y, gated, gated_t, down_bias_sum, up_held, down_held = pl.pallas_call(
        prep_kernel,
        out_shape=(
            p_shape,
            shape((2, GROUPS, TE * TE, 128), f32),
            shape((CELLS, CP), bf16),
            shape((CP, CELLS), bf16),
            shape((1, C), f32),
            shape((C, HID), bf16),
            shape((C, HID), bf16),
        ),
        in_specs=[SMEM, VMEM, VMEM, ANY, VMEM, VMEM, ANY, VMEM, ANY, ANY],
        out_specs=(VMEM,) * 7,
        scratch_shapes=[
            RN_SCRATCH,
            W_SCRATCH,
            pltpu.VMEM((49, C), f32),
            pltpu.VMEM((2, TE, TE, C), bf16),
            pltpu.SemaphoreType.DMA((4,)),
        ],
        compiler_params=params(),
        cost_estimate=pl.CostEstimate(flops=10**9, bytes_accessed=16 * 10**6, transcendentals=0),
        name="prep",
    )(neighbours, field, land, cotangent, n1, n2, depth_weight, small, up_weight, down_weight.T)

    keep, send, ng, z, r, up_bias_sum, border = pl.pallas_call(
        front_kernel,
        out_shape=(
            shape((ROWS, 128), f32),
            shape((ROWS, 128), bf16),
            shape((CELLS, C), f32),
            shape((CELLS, C), f32),
            shape((CELLS, 128), f32),
            shape((1, HID), f32),
            shape((2, GROUPS, 6 * 24, 128), f32),
        ),
        in_specs=[SMEM] + [VMEM] * 12,
        out_specs=(VMEM,) * 7,
        scratch_shapes=[
            RN_SCRATCH,
            RW_SCRATCH,
            W_SCRATCH,
            pltpu.VMEM((2, GROUPS, TE * TE, 128), f32),
            pltpu.VMEM((CELLS, CP), bf16),
            pltpu.VMEM((CP, CELLS), bf16),
        ],
        compiler_params=params(20),
        name="front",
    )(
        neighbours,
        n1,
        n2,
        w1,
        w2,
        p,
        y,
        gated,
        gated_t,
        depth_weight,
        small,
        up_held,
        down_held,
    )

    got = flip(send, 1)
    cg, g1, g2, extra = pl.pallas_call(
        grad_kernel,
        out_shape=(
            shape((2, TE, TE, C), bf16),
            narrow_shape,
            narrow_shape,
            shape((EXTRA, 128), f32),
        ),
        in_specs=[VMEM] * 8,
        out_specs=(VMEM,) * 4,
        scratch_shapes=[
            pltpu.VMEM(p_shape.shape, f32),
            Y_SCRATCH,
            pltpu.VMEM((GROUPS, 49, 8, 128), f32),
        ],
        compiler_params=params(),
        cost_estimate=pl.CostEstimate(flops=10**9, bytes_accessed=16 * 10**6, transcendentals=0),
        name="grad",
    )(ng, z, r, small, p, border, up_bias_sum, down_bias_sum)

    half = (ROWS + EXTRA) // PARTS // 2
    pieces = pl.pallas_call(
        split_kernel,
        out_shape=(shape((half, 128), bf16),) * PARTS + (shape((half, 128), f32),) * PARTS,
        in_specs=[VMEM] * 3,
        out_specs=(VMEM,) * (2 * PARTS),
        compiler_params=params(),
        name="split",
    )(keep, got, extra)

    orders = list(enumerate(ORDERS))
    n1, n2 = swap(g1, ("narrow", 0)), swap(g2, ("narrow", 1))
    parts = [
        pieces[PARTS + i] + flip(pieces[i], STAGES[order[0]][0]).astype(f32) for i, order in orders
    ]
    parts, n1, n2 = together(parts, n1, n2)
    s1, s2 = pl.pallas_call(
        functools.partial(wide_kernel, False),
        out_shape=(wide_shape, wide_shape),
        in_specs=[VMEM] * 3,
        out_specs=(VMEM, VMEM),
        scratch_shapes=wide_scratch,
        compiler_params=params(),
        name="pack_columns_back",
    )(cg, n1, n2)
    parts, s1, s2 = together(parts, s1, s2)
    w2, w1 = swap(s2, ("wide", 1)), swap(s1, ("wide", 0))
    for stage in range(1, DEPTH):
        parts = [halved(parts[i], order, stage, me) for i, order in orders]
    for stage in range(DEPTH, 6):
        parts = [doubled(parts[i], order, stage) for i, order in orders]
        if stage == 4:
            parts, w1, w2 = together(parts, w1, w2)
    parts = [part.astype(bf16) for part in parts]
    for stage in reversed(range(1, DEPTH)):
        parts = [joined(parts[i], order, stage, me) for i, order in orders]
    parts, w1, w2 = together(parts, w1, w2)
    field_grad = pl.pallas_call(
        back_kernel,
        out_shape=shape((2, TE, TE, C), bf16),
        in_specs=[SMEM] + [VMEM] * 8,
        out_specs=VMEM,
        scratch_shapes=[P_SCRATCH, RN_SCRATCH, RW_SCRATCH, W_SCRATCH, Y_SCRATCH],
        compiler_params=params(),
        cost_estimate=pl.CostEstimate(flops=10**9, bytes_accessed=16 * 10**6, transcendentals=0),
        name="back",
    )(neighbours, cg, land, cotangent, n1, n2, w1, w2, depth_weight)
    parts = [joined(parts[i], order, 0, me) for i, order in orders]
    mine = jnp.concatenate(parts, axis=0)
    theirs = flip(mine, 1)
    up_grad, down_grad, channel, up_bias_grad = pl.pallas_call(
        unpack_kernel,
        out_shape=(
            shape((C, HID), f32),
            shape((C, HID), f32),
            shape((56, C), f32),
            shape((16, 128), f32),
        ),
        in_specs=[VMEM] * 2,
        out_specs=(VMEM,) * 4,
        compiler_params=params(),
        name="unpack",
    )(mine, theirs)
    return (
        field_grad,
        channel[0:49],
        channel[49],
        channel[50],
        channel[51],
        up_grad,
        up_bias_grad.reshape(-1)[0:HID],
        down_grad.T,
        channel[52],
    )


def solution(mesh):
    return jax.shard_map(
        local,
        mesh=mesh,
        in_specs=(
            P(("wide", "narrow"), None, None, None),
            P(("wide", "narrow"), None, None, None),
            P(("wide", "narrow"), None, None),
            P(("wide", "narrow"), None),
            P(),
            P(),
            P(),
            P(),
            P(),
            P(),
            P(),
        ),
        out_specs=(P(("wide", "narrow"), None, None, None), P(), P(), P(), P(), P(), P(), P(), P()),
        check_vma=False,
    )
```

```python
import functools

import jax
import jax.numpy as jnp
from jax import lax
from jax.experimental import pallas as pl
from jax.experimental.pallas import tpu as pltpu
from jax.sharding import PartitionSpec as P

epsilon = 1e-06
gelu_root = 0.7978845608028654
gelu_cubic = 0.044715

C = 400
CP = 512
HID = 1600
TE = 16
CELLS = 512
GROUPS = 4
HT = 13
PITCH = 32
ROWS = HT * C + 16
EXTRA = 272
SIZES = (1856, 1856, 1504)
AXES = ("wide", "narrow")
f32 = jnp.float32
bf16 = jnp.bfloat16
VMEM = pl.BlockSpec(memory_space=pltpu.VMEM)
SMEM = pl.BlockSpec(memory_space=pltpu.SMEM)
HBM = pl.BlockSpec(memory_space=pltpu.HBM)


def group_width(g):
    return min(128, C - 128 * g)


def lanes(g):
    return slice(128 * g, 128 * g + group_width(g))


def land_mask(land, tiles=2):
    spread = jnp.broadcast_to(land.astype(f32)[:, :, None], (tiles * TE, TE, C))
    return spread.reshape(tiles * TE * TE, C)


def zero_lanes(ref):
    ref[...] = jnp.zeros(ref.shape, ref.dtype)


def pack_narrow(tile_rows, even, first_ref, second_ref):
    for ref in (first_ref, second_ref):
        zero_lanes(ref)
    for s in range(2):
        north = tile_rows(s, 0)
        south = tile_rows(s, TE - 3)
        first_ref[s, :, 0:C] = jnp.where(even, south, north).astype(bf16)
        second_ref[s, :, 0:C] = jnp.where(even, north, south).astype(bf16)


def narrow_kernel(field_ref, land_ref, first_ref, second_ref, held_ref, cells_ref, sems):
    copies = [
        pltpu.make_async_copy(field_ref, held_ref, sems.at[0]),
        pltpu.make_async_copy(land_ref, cells_ref, sems.at[1]),
    ]
    for copy in copies:
        copy.start()
    for copy in copies:
        copy.wait()

    def tile_rows(s, row):
        cells = held_ref[s, row : row + 3].reshape(3 * TE, C).astype(f32)
        land = cells_ref[s, row : row + 3].astype(f32)
        return cells * jnp.broadcast_to(land[:, :, None], (3, TE, C)).reshape(3 * TE, C)

    pack_narrow(tile_rows, lax.axis_index("narrow") % 2 == 0, first_ref, second_ref)


def wide_kernel(masked, *refs):
    if masked:
        tiles_ref, land_ref, n1_ref, n2_ref, first_ref, second_ref, m_ref, r_ref, o_ref = refs
        mask = land_mask(land_ref[...].reshape(2 * TE, TE))
    else:
        tiles_ref, n1_ref, n2_ref, first_ref, second_ref, m_ref, r_ref, o_ref = refs
    n_even = lax.axis_index("narrow") % 2 == 0
    w_even = lax.axis_index("wide") % 2 == 0
    zero_lanes(o_ref)
    for s in range(2):
        cells = tiles_ref[s].reshape(TE * TE, C).astype(f32)
        if masked:
            cells = cells * mask[s * TE * TE : (s + 1) * TE * TE]
        one = n1_ref[s].astype(f32)
        two = n2_ref[s].astype(f32)
        from_north = jnp.where(n_even, two, one)
        from_south = jnp.where(n_even, one, two)
        for g in range(GROUPS):
            m_ref[s, g, :, 0 : group_width(g)] = cells[:, lanes(g)]
            r_ref[0, s, g] = from_north[:, 128 * g : 128 * g + 128]
            r_ref[1, s, g] = from_south[:, 128 * g : 128 * g + 128]
    for s in range(2):
        for g in range(GROUPS):
            w = group_width(g)
            for side in range(2):
                for c in range(3):
                    col = c + side * (TE - 3)
                    at = c * 22
                    o_ref[side, s, g, at : at + 3, :] = r_ref[0, s, g, pl.ds(col, 3, stride=TE), :]
                    o_ref[side, s, g, at + 3 : at + 19, 0:w] = m_ref[s, g, pl.ds(col, TE, stride=TE), 0:w]
                    o_ref[side, s, g, at + 19 : at + 22, :] = r_ref[1, s, g, pl.ds(col, 3, stride=TE), :]
            west = o_ref[0, s, g]
            east = o_ref[1, s, g]
            first_ref[s, :, 128 * g : 128 * g + 128] = jnp.where(w_even, east, west).astype(bf16)
            second_ref[s, :, 128 * g : 128 * g + 128] = jnp.where(w_even, west, east).astype(bf16)


def place_centre(cells, s, p_ref):
    for g in range(GROUPS):
        w = group_width(g)
        for r in range(TE):
            at = (r + 3) * PITCH + 8
            p_ref[s, g, at : at + TE, 0:w] = cells[r * TE : (r + 1) * TE, lanes(g)]


def place_rows(n1_ref, n2_ref, rn_ref):
    n_even = lax.axis_index("narrow") % 2 == 0
    for s in range(2):
        one = n1_ref[s].astype(f32)
        two = n2_ref[s].astype(f32)
        north = jnp.where(n_even, two, one)
        south = jnp.where(n_even, one, two)
        for g in range(GROUPS):
            at = slice(128 * g, 128 * g + 128)
            rn_ref[0, s, g] = north[:, at]
            rn_ref[1, s, g] = south[:, at]


def place_columns(w1_ref, w2_ref, rw_ref):
    w_even = lax.axis_index("wide") % 2 == 0
    for s in range(2):
        one = w1_ref[s].astype(f32)
        two = w2_ref[s].astype(f32)
        west = jnp.where(w_even, two, one)
        east = jnp.where(w_even, one, two)
        for g in range(GROUPS):
            at = slice(128 * g, 128 * g + 128)
            rw_ref[0, s, g] = west[:, at]
            rw_ref[1, s, g] = east[:, at]


def entry_of(neighbours_ref, t, d):
    e = neighbours_ref[t, d]
    near = jnp.maximum(e, 0)
    return e >= 0, near // 2, near % 2


def chosen(options, present):
    value = options[-1][1]
    for test, other in reversed(options[:-1]):
        value = jnp.where(test, other, value)
    return jnp.where(present, value, 0.0)


def here():
    return lax.axis_index("wide") * lax.axis_size("narrow") + lax.axis_index("narrow")


def border_rows(neighbours_ref, p_ref, rn_ref, t, g):
    for d in range(2):
        present, device, slot = entry_of(neighbours_ref, t, d)
        from_row = 3 + TE - 3 if d == 0 else 3
        to_row = 0 if d == 0 else 3 + TE
        for i in range(3):
            own = p_ref[slot, g, pl.ds((from_row + i) * PITCH + 8, TE), :]
            other = rn_ref[d, slot, g, pl.ds(i * TE, TE), :]
            p_ref[t, g, pl.ds((to_row + i) * PITCH + 8, TE), :] = chosen(
                [(device == here(), own), (None, other)], present
            )


def border_columns(neighbours_ref, p_ref, rn_ref, rw_ref, t, g, put):
    narrow = lax.axis_size("narrow")
    for d in range(2):
        present, device, slot = entry_of(neighbours_ref, t, 2 + d)
        from_col = 8 + TE - 3 if d == 0 else 8
        for c in range(3):
            own = p_ref[slot, g, pl.ds(3 * PITCH + from_col + c, TE, stride=PITCH), :]
            other = rw_ref[d, slot, g, pl.ds(c * 22 + 3, TE), :]
            put(d, c, 3, TE, chosen([(device == here(), own), (None, other)], present))
    for d in range(4):
        south, east = d // 2, d % 2
        present, device, slot = entry_of(neighbours_ref, t, 4 + d)
        same_w = device // narrow == lax.axis_index("wide")
        same_n = device % narrow == lax.axis_index("narrow")
        from_row = 3 if south else 3 + TE - 3
        to_row = 3 + TE if south else 0
        from_col = 8 if east else 8 + TE - 3
        for c in range(3):
            own = p_ref[slot, g, pl.ds(from_row * PITCH + from_col + c, 3, stride=PITCH), :]
            beyond = rn_ref[south, slot, g, pl.ds(from_col - 8 + c, 3, stride=TE), :]
            beside = rw_ref[east, slot, g, pl.ds(c * 22 + from_row, 3), :]
            across = rw_ref[east, slot, g, pl.ds(c * 22 + (19 if south else 0), 3), :]
            put(
                east,
                c,
                to_row,
                3,
                chosen(
                    [(device == here(), own), (same_w, beyond), (same_n, beside), (None, across)], present
                ),
            )


def column_in(p_ref, t, g):
    def put(side, c, row, count, value):
        at = row * PITCH + (8 + TE if side else 5) + c
        p_ref[t, g, pl.ds(at, count, stride=PITCH), :] = value

    return put


def each_group(body, tiles=(0, 1)):
    def step(i, _):
        body(tiles[0] + i // GROUPS, i % GROUPS)
        return _

    lax.fori_loop(0, len(tiles) * GROUPS, step, 0)


def weight_rows(weight_ref, g, taps):
    at = pl.ds(pl.multiple_of(g * 128, 128), 128)
    return [jnp.broadcast_to(weight_ref[pl.ds(k, 1), at], (8, 128)) for k in taps]


def convolve(p_ref, weight_ref, start, finish, flip, tiles=(0, 1)):
    def body(t, g):
        for h in range(2):
            total = start(t, g, h)
            for b in range(7):
                taps = [48 - (7 * a + b) if flip else 7 * a + b for a in range(7)]
                weights = weight_rows(weight_ref, g, taps)
                for row in range(22):
                    x = p_ref[t, g, pl.ds(row * PITCH + 5 + b + 8 * h, 8), :]
                    for a in range(7):
                        r = row - a
                        if 0 <= r < TE:
                            total[r] = total[r] + weights[a] * x
            finish(t, g, h, total)

    each_group(body, tiles)


def gelu_pair(hidden):
    square = hidden * hidden
    bent = jnp.tanh(gelu_root * hidden * (1.0 + gelu_cubic * square))
    half = 0.5 * (1.0 + bent)
    slope = half + 0.5 * hidden * (1.0 - bent * bent) * (gelu_root * (1.0 + 3.0 * gelu_cubic * square))
    return hidden * half, slope


def take_weights(weight_ref, depth_weight_ref):
    weight_ref[...] = jnp.zeros(weight_ref.shape, f32)
    weight_ref[0:49, 0:C] = depth_weight_ref[...]


def prep_kernel(
    beside_ref,
    field_ref,
    land_ref,
    cot_ref,
    n1_ref,
    n2_ref,
    depth_weight_ref,
    depth_bias_ref,
    gain_ref,
    shift_ref,
    up_bias_ref,
    up_ref,
    down_ref,
    p_ref,
    y_ref,
    gated_ref,
    gated_t_ref,
    down_bias_ref,
    up_out_ref,
    down_out_ref,
    taps_ref,
    small_ref,
    rn_ref,
    weight_ref,
    cot_in_ref,
    bias_in_ref,
    gain_in_ref,
    shift_in_ref,
    up_bias_in_ref,
    neighbours_ref,
    sems,
):
    copies = [
        pltpu.make_async_copy(depth_weight_ref, taps_ref, sems.at[0]),
        pltpu.make_async_copy(cot_ref, cot_in_ref, sems.at[1]),
        pltpu.make_async_copy(up_ref, up_out_ref, sems.at[2]),
        pltpu.make_async_copy(down_ref, down_out_ref, sems.at[3]),
        pltpu.make_async_copy(depth_bias_ref, bias_in_ref, sems.at[4]),
        pltpu.make_async_copy(gain_ref, gain_in_ref, sems.at[5]),
        pltpu.make_async_copy(shift_ref, shift_in_ref, sems.at[6]),
        pltpu.make_async_copy(up_bias_ref, up_bias_in_ref, sems.at[7]),
        pltpu.make_async_copy(beside_ref, neighbours_ref, sems.at[8]),
    ]
    for copy in copies:
        copy.start()
    p_ref[...] = jnp.zeros(p_ref.shape, f32)
    mask = land_mask(land_ref[...].reshape(2 * TE, TE))
    for s in range(2):
        cells = field_ref[s].reshape(TE * TE, C).astype(f32)
        place_centre(cells * mask[s * TE * TE : (s + 1) * TE * TE], s, p_ref)
    place_rows(n1_ref, n2_ref, rn_ref)
    copies[8].wait()
    each_group(lambda t, g: border_rows(neighbours_ref, p_ref, rn_ref, t, g))
    for k in (0, 4, 5, 6, 7):
        copies[k].wait()
    small_ref[0:1, 0:C] = bias_in_ref[...].reshape(1, C)
    small_ref[1:2, 0:C] = gain_in_ref[...].reshape(1, C)
    small_ref[2:3, 0:C] = shift_in_ref[...].reshape(1, C)
    small_ref[3:4, :] = up_bias_in_ref[...].reshape(1, HID)
    take_weights(weight_ref, taps_ref)
    weight_ref[49:50, 0:C] = small_ref[0:1, 0:C]

    def start(t, g, h):
        return weight_rows(weight_ref, g, [49]) * TE

    def finish(t, g, h, rows):
        for r in range(TE):
            y_ref[t, g, pl.ds(r * TE + 8 * h, 8), :] = rows[r]

    convolve(p_ref, weight_ref, start, finish, False)

    copies[1].wait()
    gated = cot_in_ref[...].reshape(CELLS, C).astype(f32) * mask
    gated_ref[...] = jnp.zeros(gated_ref.shape, bf16)
    gated_ref[:, 0:C] = gated.astype(bf16)
    gated_t_ref[...] = gated_ref[...].T
    down_bias_ref[...] = jnp.sum(gated, axis=0, keepdims=True)
    copies[2].wait()
    copies[3].wait()


def front_kernel(
    beside_ref,
    n1_ref,
    n2_ref,
    w1_ref,
    w2_ref,
    p_ref,
    y_in_ref,
    gated_ref,
    gated_t_ref,
    depth_weight_ref,
    small_ref,
    up_ref,
    down_ref,
    keep_ref,
    send_ref,
    ng_ref,
    z_ref,
    r_ref,
    up_bias_sum_ref,
    border_ref,
    rn_ref,
    rw_ref,
    weight_ref,
    y_ref,
    normed_ref,
    normed_t_ref,
    neighbours_ref,
    sem,
):
    core0 = lax.axis_index("narrow") % 2 == 0
    copy = pltpu.make_async_copy(beside_ref, neighbours_ref, sem)
    copy.start()
    place_rows(n1_ref, n2_ref, rn_ref)
    place_columns(w1_ref, w2_ref, rw_ref)
    take_weights(weight_ref, depth_weight_ref)
    y_ref[...] = y_in_ref[...]
    copy.wait()

    def sides(t, g):
        def put(side, c, row, count, value):
            border_ref[t, g, pl.ds((side * 3 + c) * 24 + row, count), :] = value

        border_columns(neighbours_ref, p_ref, rn_ref, rw_ref, t, g, put)
        at = pl.ds(pl.multiple_of(g * 128, 128), 128)
        for side in range(2):
            for out in range(3):
                col = out + side * (TE - 3)
                total = y_ref[t, g, pl.ds(col, TE, stride=TE), :]
                for c in range(3):
                    b = (19 + c if side else c) - col
                    if 0 <= b < 7:
                        for a in range(7):
                            cells = border_ref[t, g, pl.ds((side * 3 + c) * 24 + a, TE), :]
                            total = total + weight_ref[pl.ds(7 * a + b, 1), at] * cells
                y_ref[t, g, pl.ds(col, TE, stride=TE), :] = total

    each_group(sides)

    normed_ref[...] = jnp.zeros(normed_ref.shape, bf16)
    step_rows = 64

    def norm(i, _):
        at = pl.ds(pl.multiple_of(i * step_rows, step_rows), step_rows)
        inside = pl.ds(pl.multiple_of((i % 4) * step_rows, step_rows), step_rows)
        conv = jnp.concatenate([y_ref[i // 4, g, inside, :] for g in range(GROUPS)], axis=1)[:, 0:C]
        mean = jnp.sum(conv, axis=1, keepdims=True) * (1.0 / C)
        dev = conv - mean
        var = jnp.sum(dev * dev, axis=1, keepdims=True) * (1.0 / C)
        rstd = lax.rsqrt(var + epsilon)
        zhat = dev * rstd
        z_ref[at, :] = zhat
        r_ref[at, :] = jnp.broadcast_to(rstd, (step_rows, 128))
        normed_ref[at, 0:C] = (zhat * small_ref[1:2, 0:C] + small_ref[2:3, 0:C]).astype(bf16)
        return _

    lax.fori_loop(0, CELLS // step_rows, norm, 0)
    normed_t_ref[...] = normed_ref[...].T

    def products(lo, width):
        at = slice(lo, lo + width)
        h = jnp.dot(normed_ref[:, 0:C], up_ref[:, at], preferred_element_type=f32) + small_ref[3:4, at]
        ag = jnp.dot(gated_ref[:, 0:C], down_ref[:, at], preferred_element_type=f32)
        return h, ag

    def hidden_chunk(lo, width, h, ag):
        at = slice(lo, lo + width)
        act, slope = gelu_pair(h)
        hg = ag * slope
        hgb = hg.astype(bf16)
        dg = jnp.dot(gated_t_ref[0:C, :], act.astype(bf16), preferred_element_type=f32)
        ug = jnp.dot(normed_t_ref[0:C, :], hgb, preferred_element_type=f32)
        ng = lax.dot_general(hgb, up_ref[:, at], (((1,), (1,)), ((), ())), preferred_element_type=f32)
        if lo == 0:
            ng_ref[...] = ng
        else:
            ng_ref[...] += ng
        up_bias_sum_ref[:, at] = jnp.sum(hgb.astype(f32), axis=0, keepdims=True)
        keep = jnp.where(core0, ug, dg)
        send = jnp.where(core0, dg, ug).astype(bf16)
        for k in range((width + 127) // 128):
            w = min(128, width - 128 * k)
            rows = slice((lo // 128 + k) * C, (lo // 128 + k + 1) * C)
            if w < 128:
                keep_ref[rows, :] = jnp.zeros((C, 128), f32)
                send_ref[rows, :] = jnp.zeros((C, 128), bf16)
            keep_ref[rows, 0:w] = keep[:, 128 * k : 128 * k + w]
            send_ref[rows, 0:w] = send[:, 128 * k : 128 * k + w]

    keep_ref[HT * C :, :] = jnp.zeros((16, 128), f32)
    send_ref[HT * C :, :] = jnp.zeros((16, 128), bf16)
    chunks = ((0, 512), (512, 512), (1024, 576))
    ready = products(*chunks[0])
    for i, chunk in enumerate(chunks):
        current = ready
        if i + 1 < len(chunks):
            ready = products(*chunks[i + 1])
        hidden_chunk(*chunk, *current)


def grad_kernel(
    ng_ref,
    z_ref,
    r_ref,
    small_ref,
    cg_ref,
    g1_ref,
    g2_ref,
    y_ref,
    sums_ref,
):
    y_ref[...] = jnp.zeros(y_ref.shape, f32)
    step_rows = 64

    def back(i, sums):
        at = pl.ds(pl.multiple_of(i * step_rows, step_rows), step_rows)
        ng = ng_ref[at, :]
        zhat = z_ref[at, :]
        rstd = r_ref[at, 0:1]
        q = ng * small_ref[1:2, 0:C]
        a = jnp.sum(q, axis=1, keepdims=True) * (1.0 / C)
        b = jnp.sum(q * zhat, axis=1, keepdims=True) * (1.0 / C)
        cg = (rstd * (q - a - zhat * b)).astype(bf16)
        cg_ref[i // 4, pl.ds((i % 4) * 4, 4)] = cg.reshape(4, TE, C)
        wide = cg.astype(f32)
        y_ref[at, 0:C] = wide
        return (
            sums[0] + jnp.sum(ng * zhat, axis=0, keepdims=True),
            sums[1] + jnp.sum(ng, axis=0, keepdims=True),
            sums[2] + jnp.sum(wide, axis=0, keepdims=True),
        )

    zero = jnp.zeros((1, C), f32)
    gain_sum, shift_sum, bias_sum = lax.fori_loop(0, CELLS // step_rows, back, (zero, zero, zero))
    sums_ref[0:1, :] = bias_sum
    sums_ref[1:2, :] = gain_sum
    sums_ref[2:3, :] = shift_sum

    def tile_rows(s, row):
        at = s * TE * TE + row * TE
        return y_ref[at : at + 3 * TE, 0:C]

    pack_narrow(tile_rows, lax.axis_index("narrow") % 2 == 0, g1_ref, g2_ref)

def taps_kernel(
    after_ref, y_ref, p_in_ref, border_ref, sums_ref, up_bias_sum_ref, down_bias_ref, extra_ref, p_ref, dw_ref
):
    p_ref[...] = p_in_ref[...]
    dw_ref[...] = jnp.zeros(dw_ref.shape, f32)

    def taps(t, g):
        put = column_in(p_ref, t, g)
        for side in range(2):
            for c in range(3):
                put(side, c, 0, 22, border_ref[t, g, pl.ds((side * 3 + c) * 24, 22), :])
        for h in range(2):
            cg = [
                y_ref[
                    pl.ds(t * TE * TE + r * TE + 8 * h, 8),
                    pl.ds(pl.multiple_of(g * 128, 128), 128),
                ]
                for r in range(TE)
            ]
            for b in range(7):
                total = [None] * 7
                for row in range(22):
                    x = p_ref[t, g, pl.ds(row * PITCH + 5 + b + 8 * h, 8), :]
                    for a in range(7):
                        r = row - a
                        if 0 <= r < TE:
                            term = x * cg[r]
                            total[a] = term if total[a] is None else total[a] + term
                for a in range(7):
                    dw_ref[g, 7 * a + b] += total[a]

    each_group(taps)

    extra_ref[...] = jnp.zeros(extra_ref.shape, f32)
    for g in range(GROUPS):
        w = group_width(g)
        extra_ref[g * 64 : g * 64 + 49, :] = jnp.sum(dw_ref[g], axis=1)
        extra_ref[g * 64 + 49 : g * 64 + 50, 0:w] = sums_ref[0:1, lanes(g)]
        extra_ref[g * 64 + 50 : g * 64 + 51, 0:w] = sums_ref[1:2, lanes(g)]
        extra_ref[g * 64 + 51 : g * 64 + 52, 0:w] = sums_ref[2:3, lanes(g)]
        extra_ref[g * 64 + 52 : g * 64 + 53, 0:w] = down_bias_ref[:, lanes(g)]
    for l in range(HT):
        w = min(128, HID - 128 * l)
        extra_ref[256 + l : 257 + l, 0:w] = up_bias_sum_ref[:, 128 * l : 128 * l + w]


def split_kernel(keep_ref, got_ref, after_ref, *refs):
    me = here()
    refs[-1][...] = jnp.zeros((8, 128), f32)
    lo = 0
    for i, size in enumerate(SIZES):
        send_ref, mine_ref = refs[i], refs[len(SIZES) + i]
        high = parity(me, STAGES[ORDERS[i][0]][1])
        half = size // 2
        for j in range(2):

            def store(ref, lo=lo):
                total = keep_ref[lo : lo + half, :] + got_ref[lo : lo + half, :].astype(f32)
                ref[...] = total.astype(ref.dtype)

            pl.when(high == j)(functools.partial(store, mine_ref))
            pl.when(high != j)(functools.partial(store, send_ref))
            lo += half


def unpack_kernel(mine_ref, theirs_ref, up_ref, down_ref, taps_ref, bias_ref, gain_ref, shift_ref, up_bias_ref, down_bias_ref):
    core0 = lax.axis_index("narrow") % 2 == 0
    for l in range(HT):
        w = min(128, HID - 128 * l)
        rows = slice(l * C, l * C + C)
        one = mine_ref[rows, :].astype(f32)
        two = theirs_ref[rows, :].astype(f32)
        up_ref[:, 128 * l : 128 * l + w] = jnp.where(core0, one, two)[:, 0:w]
        down_ref[:, 128 * l : 128 * l + w] = jnp.where(core0, two, one)[:, 0:w]
    extra = mine_ref[ROWS:, :].astype(f32) + theirs_ref[ROWS:, :].astype(f32)
    for g in range(GROUPS):
        taps_ref[:, lanes(g)] = extra[g * 64 : g * 64 + 49, 0 : group_width(g)]
    for k, ref in enumerate((bias_ref, gain_ref, shift_ref, down_bias_ref)):
        at = 49 + k
        vector = jnp.concatenate([extra[g * 64 + at : g * 64 + at + 1] for g in range(GROUPS)], axis=1)
        ref[...] = vector[:, 0:C].reshape(C)
    vector = jnp.concatenate([extra[256 + l : 257 + l] for l in range(HT)], axis=1)
    up_bias_ref[...] = vector[:, 0:HID].reshape(HID)


def back_kernel(
    t,
    beside_ref,
    cg_ref,
    land_ref,
    gated_ref,
    n1_ref,
    n2_ref,
    w1_ref,
    w2_ref,
    depth_weight_ref,
    *refs,
):
    out_ref, p_ref, rn_ref, rw_ref, weight_ref, y_ref, tile_ref, neighbours_ref, sem = refs[-9:]
    copy = pltpu.make_async_copy(beside_ref, neighbours_ref, sem)
    copy.start()
    p_ref[t] = jnp.zeros(p_ref.shape[1:], f32)
    for s in range(2):
        place_centre(cg_ref[s].reshape(TE * TE, C).astype(f32), s, p_ref)
    mask = land_mask(land_ref[t], 1)
    place_rows(n1_ref, n2_ref, rn_ref)
    place_columns(w1_ref, w2_ref, rw_ref)
    copy.wait()

    def borders(g, _):
        border_rows(neighbours_ref, p_ref, rn_ref, t, g)
        border_columns(neighbours_ref, p_ref, rn_ref, rw_ref, t, g, column_in(p_ref, t, g))
        return _

    lax.fori_loop(0, GROUPS, borders, 0)
    take_weights(weight_ref, depth_weight_ref)
    y_ref[...] = gated_ref[t * TE * TE : (t + 1) * TE * TE, :].astype(f32)

    def place(g, h, r):
        return (pl.ds(r * TE + 8 * h, 8), pl.ds(pl.multiple_of(g * 128, 128), 128))

    def start(t, g, h):
        return [y_ref[place(g, h, r)] for r in range(TE)]

    def finish(t, g, h, rows):
        for r in range(TE):
            y_ref[place(g, h, r)] = rows[r]

    convolve(p_ref, weight_ref, start, finish, True, (t,))
    tile_ref[...] = (y_ref[:, 0:C] * mask).astype(bf16).reshape(TE, TE, C)
    copy = pltpu.make_async_copy(tile_ref, out_ref.at[t], sem)
    copy.start()
    copy.wait()


def params(size=16):
    return pltpu.CompilerParams(vmem_limit_bytes=size * 1024 * 1024)


def estimate():
    return pl.CostEstimate(flops=10**9, bytes_accessed=16 * 10**6, transcendentals=0)


NEIGHBOURS = pltpu.SMEM((2, 8), jnp.int32)
P_SCRATCH = pltpu.VMEM((2, GROUPS, 22 * PITCH, 128), f32)
RN_SCRATCH = pltpu.VMEM((2, 2, GROUPS, 48, 128), f32)
RW_SCRATCH = pltpu.VMEM((2, 2, GROUPS, 80, 128), f32)
W_SCRATCH = pltpu.VMEM((56, CP), f32)
Y_SCRATCH = pltpu.VMEM((CELLS, CP), f32)


def swap_pairs(kind):
    axis, offset = kind
    pairs = []
    for w in range(32):
        for n in range(4):
            if axis == "narrow":
                up = (n - offset) % 2 == 0
                other = (w, (n + (1 if up else -1)) % 4)
            else:
                up = (w - offset) % 2 == 0
                other = ((w + (1 if up else -1)) % 32, n)
            pairs.append((w * 4 + n, other[0] * 4 + other[1]))
    return pairs


def swap(x, kind):
    return lax.ppermute(x, AXES, swap_pairs(kind))


def flip(x, mask):
    return lax.ppermute(x, AXES, [(i, i ^ mask) for i in range(128)])


STAGES = {
    "x1": (2, (1, 6)),
    "x2": (66, (6,)),
    "z1": (4, (2, 3)),
    "z2": (12, (3,)),
    "y1": (16, (4, 5)),
    "y2": (48, (5,)),
}
ORDERS = (
    ("x1", "y1", "z1", "x2", "y2", "z2"),
    ("y1", "z1", "x1", "y2", "z2", "x2"),
    ("z1", "x1", "y1", "z2", "x2", "y2"),
)
DEPTH = 2


def parity(me, bits):
    return sum((me >> bit) & 1 for bit in bits) & 1


def halved(part, step, high):
    half = part.shape[0] // 2
    low_rows, high_rows = part[0:half], part[half:]
    send = jnp.where(high, low_rows, high_rows).astype(bf16)
    keep = jnp.where(high, high_rows, low_rows)
    return keep + flip(send, STAGES[step][0]).astype(f32)


def doubled(part, step):
    mine = part.astype(bf16)
    return mine.astype(f32) + flip(mine, STAGES[step][0]).astype(f32)


def joined(part, step, high):
    got = flip(part, STAGES[step][0])
    return jnp.concatenate([jnp.where(high, got, part), jnp.where(high, part, got)], axis=0)


def together(*values):
    return lax.optimization_barrier(values)


def local(
    field,
    cotangent,
    land,
    neighbours,
    depth_weight,
    depth_bias,
    ln_gain,
    ln_shift,
    up_weight,
    up_bias,
    down_weight,
):
    me = here()
    shape = jax.ShapeDtypeStruct
    stay = lambda v: pltpu.with_memory_space_constraint(v, pltpu.HBM)
    steps = sorted({order[stage] for order in ORDERS for stage in range(DEPTH)})
    highs = [parity(me, STAGES[step][1]) == 1 for step in steps]
    highs, field = together(highs, field)
    high = dict(zip(steps, highs))
    neighbours = stay(neighbours)
    narrow_shape = shape((2, 48, CP), bf16)
    wide_shape = shape((2, 80, CP), bf16)
    wide_scratch = [
        pltpu.VMEM((2, GROUPS, TE * TE, 128), f32),
        RN_SCRATCH,
        RW_SCRATCH,
    ]
    p_shape = shape((2, GROUPS, 22 * PITCH, 128), f32)

    s1, s2, field, land = pl.pallas_call(
        narrow_kernel,
        out_shape=(
            narrow_shape,
            narrow_shape,
            shape((2, TE, TE, C), bf16),
            shape((2, TE, TE), jnp.int32),
        ),
        in_specs=[HBM] * 2,
        out_specs=(VMEM,) * 4,
        scratch_shapes=[pltpu.SemaphoreType.DMA((2,))],
        compiler_params=params(4),
        name="pack_rows",
    )(stay(field), stay(land))
    n1, n2 = swap(s1, ("narrow", 0)), swap(s2, ("narrow", 1))
    s1, s2 = pl.pallas_call(
        functools.partial(wide_kernel, True),
        out_shape=(wide_shape, wide_shape),
        in_specs=[VMEM] * 4,
        out_specs=(VMEM, VMEM),
        scratch_shapes=wide_scratch,
        compiler_params=params(8),
        name="pack_columns",
    )(field, land, n1, n2)
    s1, s2, n1, n2 = together(s1, s2, n1, n2)
    w2, w1 = swap(s2, ("wide", 1)), swap(s1, ("wide", 0))
    p, y, gated, gated_t, down_bias_sum, up_held, down_held, taps, small = pl.pallas_call(
        prep_kernel,
        out_shape=(
            p_shape,
            shape((2, GROUPS, TE * TE, 128), f32),
            shape((CELLS, CP), bf16),
            shape((CP, CELLS), bf16),
            shape((1, C), f32),
            shape((C, HID), bf16),
            shape((C, HID), bf16),
            shape((49, C), f32),
            shape((4, HID), f32),
        ),
        in_specs=[HBM, VMEM, VMEM, HBM, VMEM, VMEM] + [HBM] * 7,
        out_specs=(VMEM,) * 9,
        scratch_shapes=[
            RN_SCRATCH,
            W_SCRATCH,
            pltpu.VMEM((2, TE, TE, C), bf16),
            pltpu.VMEM((C,), f32),
            pltpu.VMEM((C,), f32),
            pltpu.VMEM((C,), f32),
            pltpu.VMEM((HID,), f32),
            NEIGHBOURS,
            pltpu.SemaphoreType.DMA((9,)),
        ],
        compiler_params=params(8),
        cost_estimate=estimate(),
        name="prep",
    )(
        neighbours,
        field,
        land,
        stay(cotangent),
        n1,
        n2,
        stay(depth_weight),
        stay(depth_bias),
        stay(ln_gain),
        stay(ln_shift),
        stay(up_bias),
        stay(up_weight),
        stay(down_weight.T),
    )

    keep, send, ng, z, r, up_bias_sum, border = pl.pallas_call(
        front_kernel,
        out_shape=(
            shape((ROWS, 128), f32),
            shape((ROWS, 128), bf16),
            shape((CELLS, C), f32),
            shape((CELLS, C), f32),
            shape((CELLS, 128), f32),
            shape((1, HID), f32),
            shape((2, GROUPS, 6 * 24, 128), f32),
        ),
        in_specs=[HBM] + [VMEM] * 12,
        out_specs=(VMEM,) * 7,
        scratch_shapes=[
            RN_SCRATCH,
            RW_SCRATCH,
            W_SCRATCH,
            pltpu.VMEM((2, GROUPS, TE * TE, 128), f32),
            pltpu.VMEM((CELLS, CP), bf16),
            pltpu.VMEM((CP, CELLS), bf16),
            NEIGHBOURS,
            pltpu.SemaphoreType.DMA,
        ],
        compiler_params=params(14),
        name="front",
    )(
        neighbours,
        n1,
        n2,
        w1,
        w2,
        p,
        y,
        gated,
        gated_t,
        taps,
        small,
        up_held,
        down_held,
    )

    got = flip(send, 1)
    cg, g1, g2, cg_wide, sums = pl.pallas_call(
        grad_kernel,
        out_shape=(
            shape((2, TE, TE, C), bf16),
            narrow_shape,
            narrow_shape,
            shape((CELLS, CP), f32),
            shape((3, C), f32),
        ),
        in_specs=[VMEM] * 4,
        out_specs=(VMEM,) * 5,
        compiler_params=params(4),
        cost_estimate=estimate(),
        name="grad",
    )(ng, z, r, small)

    halves = [size // 2 for size in SIZES]
    pieces = pl.pallas_call(
        split_kernel,
        out_shape=tuple(shape((half, 128), bf16) for half in halves)
        + tuple(shape((half, 128), f32) for half in halves)
        + (shape((8, 128), f32),),
        in_specs=[VMEM] * 3,
        out_specs=(VMEM,) * (2 * len(SIZES) + 1),
        compiler_params=params(4),
        name="split",
    )(keep, got, sums)

    orders = list(enumerate(ORDERS))
    got = [flip(pieces[i], STAGES[order[0]][0]) for i, order in orders]
    n1, n2 = swap(g1, ("narrow", 0)), swap(g2, ("narrow", 1))
    extra = pl.pallas_call(
        taps_kernel,
        out_shape=shape((EXTRA, 128), f32),
        in_specs=[VMEM] * 7,
        out_specs=VMEM,
        scratch_shapes=[
            pltpu.VMEM(p_shape.shape, f32),
            pltpu.VMEM((GROUPS, 49, 8, 128), f32),
        ],
        compiler_params=params(8),
        cost_estimate=estimate(),
        name="taps",
    )(pieces[-1], cg_wide, p, border, sums, up_bias_sum, down_bias_sum)
    parts = [pieces[len(SIZES) + i] + got[i].astype(f32) for i, order in orders]
    parts[-1] = jnp.concatenate([parts[-1], extra], axis=0)
    parts, n1, n2 = together(parts, n1, n2)
    s1, s2 = pl.pallas_call(
        functools.partial(wide_kernel, False),
        out_shape=(wide_shape, wide_shape),
        in_specs=[VMEM] * 3,
        out_specs=(VMEM, VMEM),
        scratch_shapes=wide_scratch,
        compiler_params=params(8),
        name="pack_columns_back",
    )(cg, n1, n2)
    parts, s1, s2 = together(parts, s1, s2)
    w2, w1 = swap(s2, ("wide", 1)), swap(s1, ("wide", 0))
    for stage in range(1, DEPTH):
        parts = [halved(parts[i], order[stage], high[order[stage]]) for i, order in orders]
    for stage in range(DEPTH, 6):
        parts = [doubled(parts[i], order[stage]) for i, order in orders]
        if stage == 4:
            parts, w1, w2 = together(parts, w1, w2)
    parts = [part.astype(bf16) for part in parts]
    for stage in reversed(range(1, DEPTH)):
        parts = [joined(parts[i], order[stage], high[order[stage]]) for i, order in orders]
    parts, w1, w2 = together(parts, w1, w2)

    def back(t, *before):
        operands = (neighbours, cg, land, gated, n1, n2, w1, w2, taps)
        return pl.pallas_call(
            functools.partial(back_kernel, t),
            out_shape=shape((2, TE, TE, C), bf16),
            in_specs=[HBM] + [VMEM] * 8 + [HBM] * len(before),
            out_specs=HBM,
            scratch_shapes=[
                P_SCRATCH,
                RN_SCRATCH,
                RW_SCRATCH,
                W_SCRATCH,
                pltpu.VMEM((TE * TE, CP), f32),
                pltpu.VMEM((TE, TE, C), bf16),
                NEIGHBOURS,
                pltpu.SemaphoreType.DMA,
            ],
            input_output_aliases={len(operands): 0} if before else {},
            compiler_params=params(10),
            cost_estimate=estimate(),
            name=f"back_{t}",
        )(*operands, *before)

    field_grad = back(0)
    matrix = [joined(parts[i], order[0], high[order[0]]) for i, order in orders[:-1]]
    last = parts[-1]
    order = ORDERS[-1]
    got = flip(last, STAGES[order[0]][0])
    one, two = last[0 : halves[-1]], got[0 : halves[-1]]
    upper = high[order[0]]
    extra = (last[halves[-1] :].astype(f32) + got[halves[-1] :].astype(f32)).astype(bf16)
    mine = jnp.concatenate(
        matrix + [jnp.where(upper, two, one), jnp.where(upper, one, two), extra], axis=0
    )
    mine, field_grad = together(mine, field_grad)
    theirs = flip(mine, 1)
    field_grad = back(1, field_grad)
    theirs, field_grad = together(theirs, field_grad)
    up_grad, down_grad, *rest = pl.pallas_call(
        unpack_kernel,
        out_shape=(
            shape((C, HID), f32),
            shape((C, HID), f32),
            shape((49, C), f32),
            shape((C,), f32),
            shape((C,), f32),
            shape((C,), f32),
            shape((HID,), f32),
            shape((C,), f32),
        ),
        in_specs=[VMEM] * 2,
        out_specs=(VMEM,) * 8,
        compiler_params=params(12),
        name="unpack",
    )(mine, theirs)
    depth_grad, depth_bias_grad, gain_grad, shift_grad, up_bias_grad, down_bias_grad = rest
    return (
        field_grad,
        depth_grad,
        depth_bias_grad,
        gain_grad,
        shift_grad,
        up_grad,
        up_bias_grad,
        down_grad.T,
        down_bias_grad,
    )


def solution(mesh):
    return jax.shard_map(
        local,
        mesh=mesh,
        in_specs=(
            P(("wide", "narrow"), None, None, None),
            P(("wide", "narrow"), None, None, None),
            P(("wide", "narrow"), None, None),
            P(("wide", "narrow"), None),
            P(),
            P(),
            P(),
            P(),
            P(),
            P(),
            P(),
        ),
        out_specs=(P(("wide", "narrow"), None, None, None), P(), P(), P(), P(), P(), P(), P(), P()),
        check_vma=False,
    )
```

```python
import functools

import jax
import jax.numpy as jnp
from jax import lax
from jax.experimental import pallas as pl
from jax.experimental.pallas import tpu as pltpu
from jax.sharding import PartitionSpec as P

epsilon = 1e-06
gelu_root = 0.7978845608028654
gelu_cubic = 0.044715

C = 400
CP = 512
HID = 1600
TE = 16
CELLS = 512
GROUPS = 4
HT = 13
PITCH = 32
ROWS = HT * C + 16
EXTRA = 272
SIZES = (1856, 1856, 1504)
AXES = ("wide", "narrow")
f32 = jnp.float32
bf16 = jnp.bfloat16
VMEM = pl.BlockSpec(memory_space=pltpu.VMEM)
SMEM = pl.BlockSpec(memory_space=pltpu.SMEM)
HBM = pl.BlockSpec(memory_space=pltpu.HBM)


def group_width(g):
    return min(128, C - 128 * g)


def lanes(g):
    return slice(128 * g, 128 * g + group_width(g))


def land_mask(land, tiles=2):
    spread = jnp.broadcast_to(land.astype(f32)[:, :, None], (tiles * TE, TE, C))
    return spread.reshape(tiles * TE * TE, C)


def zero_lanes(ref):
    ref[...] = jnp.zeros(ref.shape, ref.dtype)


def pack_narrow(tile_rows, even, first_ref, second_ref):
    for ref in (first_ref, second_ref):
        zero_lanes(ref)
    for s in range(2):
        north = tile_rows(s, 0)
        south = tile_rows(s, TE - 3)
        first_ref[s, :, 0:C] = jnp.where(even, south, north).astype(bf16)
        second_ref[s, :, 0:C] = jnp.where(even, north, south).astype(bf16)


def narrow_kernel(field_ref, land_ref, first_ref, second_ref, held_ref, cells_ref, sems):
    copies = [
        pltpu.make_async_copy(field_ref, held_ref, sems.at[0]),
        pltpu.make_async_copy(land_ref, cells_ref, sems.at[1]),
    ]
    for copy in copies:
        copy.start()
    for copy in copies:
        copy.wait()

    def tile_rows(s, row):
        cells = held_ref[s, row : row + 3].reshape(3 * TE, C).astype(f32)
        land = cells_ref[s, row : row + 3].astype(f32)
        return cells * jnp.broadcast_to(land[:, :, None], (3, TE, C)).reshape(3 * TE, C)

    pack_narrow(tile_rows, lax.axis_index("narrow") % 2 == 0, first_ref, second_ref)


def wide_kernel(masked, *refs):
    if masked:
        tiles_ref, mask_ref, n1_ref, n2_ref, first_ref, second_ref, m_ref, r_ref, o_ref = refs
    else:
        tiles_ref, n1_ref, n2_ref, first_ref, second_ref, m_ref, r_ref, o_ref = refs
    n_even = lax.axis_index("narrow") % 2 == 0
    w_even = lax.axis_index("wide") % 2 == 0
    zero_lanes(o_ref)
    for s in range(2):
        cells = tiles_ref[s].reshape(TE * TE, C).astype(f32)
        if masked:
            cells = cells * mask_ref[s * TE * TE : (s + 1) * TE * TE, :]
        one = n1_ref[s].astype(f32)
        two = n2_ref[s].astype(f32)
        from_north = jnp.where(n_even, two, one)
        from_south = jnp.where(n_even, one, two)
        for g in range(GROUPS):
            m_ref[s, g, :, 0 : group_width(g)] = cells[:, lanes(g)]
            r_ref[0, s, g] = from_north[:, 128 * g : 128 * g + 128]
            r_ref[1, s, g] = from_south[:, 128 * g : 128 * g + 128]
    for s in range(2):
        for g in range(GROUPS):
            w = group_width(g)
            for side in range(2):
                for c in range(3):
                    col = c + side * (TE - 3)
                    at = c * 22
                    o_ref[side, s, g, at : at + 3, :] = r_ref[0, s, g, pl.ds(col, 3, stride=TE), :]
                    o_ref[side, s, g, at + 3 : at + 19, 0:w] = m_ref[s, g, pl.ds(col, TE, stride=TE), 0:w]
                    o_ref[side, s, g, at + 19 : at + 22, :] = r_ref[1, s, g, pl.ds(col, 3, stride=TE), :]
            west = o_ref[0, s, g]
            east = o_ref[1, s, g]
            first_ref[s, :, 128 * g : 128 * g + 128] = jnp.where(w_even, east, west).astype(bf16)
            second_ref[s, :, 128 * g : 128 * g + 128] = jnp.where(w_even, west, east).astype(bf16)


def place_centre(cells, s, p_ref):
    for g in range(GROUPS):
        for r in range(TE):
            at = (r + 3) * PITCH + 8
            p_ref[s, g, at : at + TE, :] = cells[r * TE : (r + 1) * TE, 128 * g : 128 * g + 128]


def padded_lanes(cells):
    return jnp.concatenate([cells, jnp.zeros((cells.shape[0], CP - C), cells.dtype)], axis=1)


def place_rows(n1_ref, n2_ref, rn_ref):
    n_even = lax.axis_index("narrow") % 2 == 0
    for s in range(2):
        one = n1_ref[s].astype(f32)
        two = n2_ref[s].astype(f32)
        north = jnp.where(n_even, two, one)
        south = jnp.where(n_even, one, two)
        for g in range(GROUPS):
            at = slice(128 * g, 128 * g + 128)
            rn_ref[0, s, g] = north[:, at]
            rn_ref[1, s, g] = south[:, at]


def place_columns(w1_ref, w2_ref, rw_ref):
    w_even = lax.axis_index("wide") % 2 == 0
    for s in range(2):
        one = w1_ref[s].astype(f32)
        two = w2_ref[s].astype(f32)
        west = jnp.where(w_even, two, one)
        east = jnp.where(w_even, one, two)
        for g in range(GROUPS):
            at = slice(128 * g, 128 * g + 128)
            rw_ref[0, s, g] = west[:, at]
            rw_ref[1, s, g] = east[:, at]


def entry_of(neighbours_ref, t, d):
    e = neighbours_ref[t, d]
    near = jnp.maximum(e, 0)
    return e >= 0, near // 2, near % 2


def chosen(options, present):
    value = options[-1][1]
    for test, other in reversed(options[:-1]):
        value = jnp.where(test, other, value)
    return jnp.where(present, value, 0.0)


def here():
    return lax.axis_index("wide") * lax.axis_size("narrow") + lax.axis_index("narrow")


def border_rows(neighbours_ref, p_ref, rn_ref, t, g):
    for d in range(2):
        present, device, slot = entry_of(neighbours_ref, t, d)
        from_row = 3 + TE - 3 if d == 0 else 3
        to_row = 0 if d == 0 else 3 + TE
        for i in range(3):
            own = p_ref[slot, g, pl.ds((from_row + i) * PITCH + 8, TE), :]
            other = rn_ref[d, slot, g, pl.ds(i * TE, TE), :]
            p_ref[t, g, pl.ds((to_row + i) * PITCH + 8, TE), :] = chosen(
                [(device == here(), own), (None, other)], present
            )


def border_columns(neighbours_ref, p_ref, rn_ref, rw_ref, t, g, put):
    narrow = lax.axis_size("narrow")
    for d in range(2):
        present, device, slot = entry_of(neighbours_ref, t, 2 + d)
        from_col = 8 + TE - 3 if d == 0 else 8
        for c in range(3):
            own = p_ref[slot, g, pl.ds(3 * PITCH + from_col + c, TE, stride=PITCH), :]
            other = rw_ref[d, slot, g, pl.ds(c * 22 + 3, TE), :]
            put(d, c, 3, TE, chosen([(device == here(), own), (None, other)], present))
    for d in range(4):
        south, east = d // 2, d % 2
        present, device, slot = entry_of(neighbours_ref, t, 4 + d)
        same_w = device // narrow == lax.axis_index("wide")
        same_n = device % narrow == lax.axis_index("narrow")
        from_row = 3 if south else 3 + TE - 3
        to_row = 3 + TE if south else 0
        from_col = 8 if east else 8 + TE - 3
        for c in range(3):
            own = p_ref[slot, g, pl.ds(from_row * PITCH + from_col + c, 3, stride=PITCH), :]
            beyond = rn_ref[south, slot, g, pl.ds(from_col - 8 + c, 3, stride=TE), :]
            beside = rw_ref[east, slot, g, pl.ds(c * 22 + from_row, 3), :]
            across = rw_ref[east, slot, g, pl.ds(c * 22 + (19 if south else 0), 3), :]
            put(
                east,
                c,
                to_row,
                3,
                chosen(
                    [(device == here(), own), (same_w, beyond), (same_n, beside), (None, across)], present
                ),
            )


def column_in(p_ref, t, g):
    def put(side, c, row, count, value):
        at = row * PITCH + (8 + TE if side else 5) + c
        p_ref[t, g, pl.ds(at, count, stride=PITCH), :] = value

    return put


def each_group(body, tiles=(0, 1)):
    def step(i, _):
        body(tiles[0] + i // GROUPS, i % GROUPS)
        return _

    lax.fori_loop(0, len(tiles) * GROUPS, step, 0)


def weight_rows(weight_ref, g, taps):
    at = pl.ds(pl.multiple_of(g * 128, 128), 128)
    return [jnp.broadcast_to(weight_ref[pl.ds(k, 1), at], (8, 128)) for k in taps]


def convolve(p_ref, weight_ref, start, finish, flip, tiles=(0, 1)):
    def body(t, g):
        for h in range(2):
            total = start(t, g, h)
            for b in range(7):
                taps = [48 - (7 * a + b) if flip else 7 * a + b for a in range(7)]
                weights = weight_rows(weight_ref, g, taps)
                for row in range(22):
                    x = p_ref[t, g, pl.ds(row * PITCH + 5 + b + 8 * h, 8), :]
                    for a in range(7):
                        r = row - a
                        if 0 <= r < TE:
                            total[r] = total[r] + weights[a] * x
            finish(t, g, h, total)

    each_group(body, tiles)


def gelu_pair(hidden):
    square = hidden * hidden
    bent = jnp.tanh(gelu_root * hidden * (1.0 + gelu_cubic * square))
    half = 0.5 * (1.0 + bent)
    slope = half + 0.5 * hidden * (1.0 - bent * bent) * (gelu_root * (1.0 + 3.0 * gelu_cubic * square))
    return hidden * half, slope


def take_weights(weight_ref, depth_weight_ref):
    weight_ref[...] = jnp.zeros(weight_ref.shape, f32)
    weight_ref[0:49, 0:C] = depth_weight_ref[...]


def hold_kernel(
    land_ref,
    cot_ref,
    depth_weight_ref,
    depth_bias_ref,
    gain_ref,
    shift_ref,
    up_bias_ref,
    up_ref,
    down_ref,
    mask_ref,
    gated_ref,
    gated_t_ref,
    down_bias_ref,
    up_out_ref,
    down_out_ref,
    taps_ref,
    small_ref,
    cot_in_ref,
    bias_in_ref,
    gain_in_ref,
    shift_in_ref,
    up_bias_in_ref,
    sems,
):
    pairs = (
        (cot_ref, cot_in_ref),
        (depth_weight_ref, taps_ref),
        (depth_bias_ref, bias_in_ref),
        (gain_ref, gain_in_ref),
        (shift_ref, shift_in_ref),
        (up_bias_ref, up_bias_in_ref),
        (up_ref, up_out_ref),
        (down_ref, down_out_ref),
    )
    copies = [pltpu.make_async_copy(a, b, sems.at[k]) for k, (a, b) in enumerate(pairs)]
    for copy in copies:
        copy.start()
    mask_ref[...] = land_mask(land_ref[...].reshape(2 * TE, TE))
    copies[0].wait()
    gated = cot_in_ref[...].reshape(CELLS, C).astype(f32) * mask_ref[...]
    gated_ref[...] = padded_lanes(gated).astype(bf16)
    gated_t_ref[...] = gated_ref[...].T
    down_bias_ref[...] = jnp.sum(gated, axis=0, keepdims=True)
    for copy in copies[1:]:
        copy.wait()
    small_ref[0:1, 0:C] = bias_in_ref[...].reshape(1, C)
    small_ref[1:2, 0:C] = gain_in_ref[...].reshape(1, C)
    small_ref[2:3, 0:C] = shift_in_ref[...].reshape(1, C)
    small_ref[3:4, :] = up_bias_in_ref[...].reshape(1, HID)


def prep_kernel(
    beside_ref,
    field_ref,
    mask_ref,
    n1_ref,
    n2_ref,
    taps_ref,
    small_ref,
    p_ref,
    y_ref,
    rn_ref,
    weight_ref,
    neighbours_ref,
    sem,
):
    copy = pltpu.make_async_copy(beside_ref, neighbours_ref, sem)
    copy.start()
    p_ref[...] = jnp.zeros(p_ref.shape, f32)
    for s in range(2):
        cells = field_ref[s].reshape(TE * TE, C).astype(f32)
        place_centre(padded_lanes(cells * mask_ref[s * TE * TE : (s + 1) * TE * TE, :]), s, p_ref)
    place_rows(n1_ref, n2_ref, rn_ref)
    take_weights(weight_ref, taps_ref)
    weight_ref[49:50, 0:C] = small_ref[0:1, 0:C]
    copy.wait()
    each_group(lambda t, g: border_rows(neighbours_ref, p_ref, rn_ref, t, g))

    def start(t, g, h):
        return weight_rows(weight_ref, g, [49]) * TE

    def finish(t, g, h, rows):
        for r in range(TE):
            y_ref[t, g, pl.ds(r * TE + 8 * h, 8), :] = rows[r]

    convolve(p_ref, weight_ref, start, finish, False)


def front_kernel(
    beside_ref,
    n1_ref,
    n2_ref,
    w1_ref,
    w2_ref,
    p_ref,
    y_in_ref,
    gated_ref,
    gated_t_ref,
    depth_weight_ref,
    small_ref,
    up_ref,
    down_ref,
    keep_ref,
    send_ref,
    ng_ref,
    z_ref,
    r_ref,
    up_bias_sum_ref,
    border_ref,
    rn_ref,
    rw_ref,
    weight_ref,
    y_ref,
    normed_ref,
    normed_t_ref,
    neighbours_ref,
    sem,
):
    core0 = lax.axis_index("narrow") % 2 == 0
    copy = pltpu.make_async_copy(beside_ref, neighbours_ref, sem)
    copy.start()
    place_rows(n1_ref, n2_ref, rn_ref)
    place_columns(w1_ref, w2_ref, rw_ref)
    take_weights(weight_ref, depth_weight_ref)
    y_ref[...] = y_in_ref[...]
    copy.wait()

    def sides(t, g):
        def put(side, c, row, count, value):
            border_ref[t, g, pl.ds((side * 3 + c) * 24 + row, count), :] = value

        border_columns(neighbours_ref, p_ref, rn_ref, rw_ref, t, g, put)
        at = pl.ds(pl.multiple_of(g * 128, 128), 128)
        for side in range(2):
            for out in range(3):
                col = out + side * (TE - 3)
                total = y_ref[t, g, pl.ds(col, TE, stride=TE), :]
                for c in range(3):
                    b = (19 + c if side else c) - col
                    if 0 <= b < 7:
                        for a in range(7):
                            cells = border_ref[t, g, pl.ds((side * 3 + c) * 24 + a, TE), :]
                            total = total + weight_ref[pl.ds(7 * a + b, 1), at] * cells
                y_ref[t, g, pl.ds(col, TE, stride=TE), :] = total

    each_group(sides)

    normed_ref[...] = jnp.zeros(normed_ref.shape, bf16)
    step_rows = 64

    def norm(i, _):
        at = pl.ds(pl.multiple_of(i * step_rows, step_rows), step_rows)
        inside = pl.ds(pl.multiple_of((i % 4) * step_rows, step_rows), step_rows)
        conv = jnp.concatenate([y_ref[i // 4, g, inside, :] for g in range(GROUPS)], axis=1)[:, 0:C]
        mean = jnp.sum(conv, axis=1, keepdims=True) * (1.0 / C)
        dev = conv - mean
        var = jnp.sum(dev * dev, axis=1, keepdims=True) * (1.0 / C)
        rstd = lax.rsqrt(var + epsilon)
        zhat = dev * rstd
        z_ref[at, :] = zhat
        r_ref[at, :] = jnp.broadcast_to(rstd, (step_rows, 128))
        normed_ref[at, 0:C] = (zhat * small_ref[1:2, 0:C] + small_ref[2:3, 0:C]).astype(bf16)
        return _

    lax.fori_loop(0, CELLS // step_rows, norm, 0)
    normed_t_ref[...] = normed_ref[...].T

    def products(lo, width):
        at = slice(lo, lo + width)
        h = jnp.dot(normed_ref[:, 0:C], up_ref[:, at], preferred_element_type=f32) + small_ref[3:4, at]
        ag = jnp.dot(gated_ref[:, 0:C], down_ref[:, at], preferred_element_type=f32)
        return h, ag

    def hidden_chunk(lo, width, h, ag):
        at = slice(lo, lo + width)
        act, slope = gelu_pair(h)
        hg = ag * slope
        hgb = hg.astype(bf16)
        dg = jnp.dot(gated_t_ref[0:C, :], act.astype(bf16), preferred_element_type=f32)
        ug = jnp.dot(normed_t_ref[0:C, :], hgb, preferred_element_type=f32)
        ng = lax.dot_general(hgb, up_ref[:, at], (((1,), (1,)), ((), ())), preferred_element_type=f32)
        if lo == 0:
            ng_ref[...] = ng
        else:
            ng_ref[...] += ng
        up_bias_sum_ref[:, at] = jnp.sum(hgb.astype(f32), axis=0, keepdims=True)
        keep = jnp.where(core0, ug, dg)
        send = jnp.where(core0, dg, ug).astype(bf16)
        for k in range((width + 127) // 128):
            w = min(128, width - 128 * k)
            rows = slice((lo // 128 + k) * C, (lo // 128 + k + 1) * C)
            if w < 128:
                keep_ref[rows, :] = jnp.zeros((C, 128), f32)
                send_ref[rows, :] = jnp.zeros((C, 128), bf16)
            keep_ref[rows, 0:w] = keep[:, 128 * k : 128 * k + w]
            send_ref[rows, 0:w] = send[:, 128 * k : 128 * k + w]

    keep_ref[HT * C :, :] = jnp.zeros((16, 128), f32)
    send_ref[HT * C :, :] = jnp.zeros((16, 128), bf16)
    chunks = ((0, 512), (512, 512), (1024, 576))
    ready = products(*chunks[0])
    for i, chunk in enumerate(chunks):
        current = ready
        if i + 1 < len(chunks):
            ready = products(*chunks[i + 1])
        hidden_chunk(*chunk, *current)


def grad_kernel(
    ng_ref,
    z_ref,
    r_ref,
    small_ref,
    cg_ref,
    g1_ref,
    g2_ref,
    y_ref,
    sums_ref,
):
    y_ref[...] = jnp.zeros(y_ref.shape, f32)
    step_rows = 64

    def back(i, sums):
        at = pl.ds(pl.multiple_of(i * step_rows, step_rows), step_rows)
        ng = ng_ref[at, :]
        zhat = z_ref[at, :]
        rstd = r_ref[at, 0:1]
        q = ng * small_ref[1:2, 0:C]
        a = jnp.sum(q, axis=1, keepdims=True) * (1.0 / C)
        b = jnp.sum(q * zhat, axis=1, keepdims=True) * (1.0 / C)
        cg = (rstd * (q - a - zhat * b)).astype(bf16)
        cg_ref[i // 4, pl.ds((i % 4) * 4, 4)] = cg.reshape(4, TE, C)
        wide = cg.astype(f32)
        y_ref[at, 0:C] = wide
        return (
            sums[0] + jnp.sum(ng * zhat, axis=0, keepdims=True),
            sums[1] + jnp.sum(ng, axis=0, keepdims=True),
            sums[2] + jnp.sum(wide, axis=0, keepdims=True),
        )

    zero = jnp.zeros((1, C), f32)
    gain_sum, shift_sum, bias_sum = lax.fori_loop(0, CELLS // step_rows, back, (zero, zero, zero))
    sums_ref[0:1, :] = bias_sum
    sums_ref[1:2, :] = gain_sum
    sums_ref[2:3, :] = shift_sum

    def tile_rows(s, row):
        at = s * TE * TE + row * TE
        return y_ref[at : at + 3 * TE, 0:C]

    pack_narrow(tile_rows, lax.axis_index("narrow") % 2 == 0, g1_ref, g2_ref)

def taps_kernel(
    after_ref, y_ref, p_in_ref, border_ref, sums_ref, up_bias_sum_ref, down_bias_ref, extra_ref, p_ref, dw_ref
):
    p_ref[...] = p_in_ref[...]
    dw_ref[...] = jnp.zeros(dw_ref.shape, f32)

    def taps(t, g):
        put = column_in(p_ref, t, g)
        for side in range(2):
            for c in range(3):
                put(side, c, 0, 22, border_ref[t, g, pl.ds((side * 3 + c) * 24, 22), :])
        for h in range(2):
            cg = [
                y_ref[
                    pl.ds(t * TE * TE + r * TE + 8 * h, 8),
                    pl.ds(pl.multiple_of(g * 128, 128), 128),
                ]
                for r in range(TE)
            ]
            for b in range(7):
                total = [None] * 7
                for row in range(22):
                    x = p_ref[t, g, pl.ds(row * PITCH + 5 + b + 8 * h, 8), :]
                    for a in range(7):
                        r = row - a
                        if 0 <= r < TE:
                            term = x * cg[r]
                            total[a] = term if total[a] is None else total[a] + term
                for a in range(7):
                    dw_ref[g, 7 * a + b] += total[a]

    each_group(taps)

    extra_ref[...] = jnp.zeros(extra_ref.shape, f32)
    for g in range(GROUPS):
        w = group_width(g)
        extra_ref[g * 64 : g * 64 + 49, :] = jnp.sum(dw_ref[g], axis=1)
        extra_ref[g * 64 + 49 : g * 64 + 50, 0:w] = sums_ref[0:1, lanes(g)]
        extra_ref[g * 64 + 50 : g * 64 + 51, 0:w] = sums_ref[1:2, lanes(g)]
        extra_ref[g * 64 + 51 : g * 64 + 52, 0:w] = sums_ref[2:3, lanes(g)]
        extra_ref[g * 64 + 52 : g * 64 + 53, 0:w] = down_bias_ref[:, lanes(g)]
    for l in range(HT):
        w = min(128, HID - 128 * l)
        extra_ref[256 + l : 257 + l, 0:w] = up_bias_sum_ref[:, 128 * l : 128 * l + w]


def split_kernel(keep_ref, got_ref, after_ref, *refs):
    me = here()
    refs[-1][...] = jnp.zeros((8, 128), f32)
    lo = 0
    for i, size in enumerate(SIZES):
        send_ref, mine_ref = refs[i], refs[len(SIZES) + i]
        high = parity(me, STAGES[ORDERS[i][0]][1])
        half = size // 2
        for j in range(2):

            def store(ref, lo=lo):
                total = keep_ref[lo : lo + half, :] + got_ref[lo : lo + half, :].astype(f32)
                ref[...] = total.astype(ref.dtype)

            pl.when(high == j)(functools.partial(store, mine_ref))
            pl.when(high != j)(functools.partial(store, send_ref))
            lo += half


def unpack_kernel(mine_ref, theirs_ref, up_ref, down_ref, taps_ref, bias_ref, gain_ref, shift_ref, up_bias_ref, down_bias_ref):
    core0 = lax.axis_index("narrow") % 2 == 0
    for l in range(HT):
        w = min(128, HID - 128 * l)
        rows = slice(l * C, l * C + C)
        one = mine_ref[rows, :].astype(f32)
        two = theirs_ref[rows, :].astype(f32)
        up_ref[:, 128 * l : 128 * l + w] = jnp.where(core0, one, two)[:, 0:w]
        down_ref[:, 128 * l : 128 * l + w] = jnp.where(core0, two, one)[:, 0:w]
    extra = mine_ref[ROWS:, :].astype(f32) + theirs_ref[ROWS:, :].astype(f32)
    for g in range(GROUPS):
        taps_ref[:, lanes(g)] = extra[g * 64 : g * 64 + 49, 0 : group_width(g)]
    for k, ref in enumerate((bias_ref, gain_ref, shift_ref, down_bias_ref)):
        at = 49 + k
        vector = jnp.concatenate([extra[g * 64 + at : g * 64 + at + 1] for g in range(GROUPS)], axis=1)
        ref[...] = vector[:, 0:C].reshape(C)
    vector = jnp.concatenate([extra[256 + l : 257 + l] for l in range(HT)], axis=1)
    up_bias_ref[...] = vector[:, 0:HID].reshape(HID)


def back_tile(t, p_ref, weight_ref, y_ref, tile_ref, gated_ref, mask_ref, out_ref, sem):
    at = slice(t * TE * TE, (t + 1) * TE * TE)
    y_ref[...] = gated_ref[at, :].astype(f32)

    def place(g, h, r):
        return (pl.ds(r * TE + 8 * h, 8), pl.ds(pl.multiple_of(g * 128, 128), 128))

    def start(t, g, h):
        return [y_ref[place(g, h, r)] for r in range(TE)]

    def finish(t, g, h, rows):
        for r in range(TE):
            y_ref[place(g, h, r)] = rows[r]

    convolve(p_ref, weight_ref, start, finish, True, (t,))
    tile_ref[...] = (y_ref[:, 0:C] * mask_ref[at, :]).astype(bf16).reshape(TE, TE, C)
    copy = pltpu.make_async_copy(tile_ref, out_ref.at[t], sem)
    copy.start()
    copy.wait()


def back_first_kernel(
    beside_ref,
    cg_ref,
    mask_ref,
    gated_ref,
    n1_ref,
    n2_ref,
    w1_ref,
    w2_ref,
    taps_ref,
    out_ref,
    p_ref,
    rn_ref,
    rw_ref,
    weight_ref,
    y_ref,
    tile_ref,
    neighbours_ref,
    sem,
):
    copy = pltpu.make_async_copy(beside_ref, neighbours_ref, sem)
    copy.start()
    for s in range(2):
        place_centre(padded_lanes(cg_ref[s].reshape(TE * TE, C).astype(f32)), s, p_ref)
    place_rows(n1_ref, n2_ref, rn_ref)
    place_columns(w1_ref, w2_ref, rw_ref)
    take_weights(weight_ref, taps_ref)
    copy.wait()

    def borders(t, g):
        border_rows(neighbours_ref, p_ref, rn_ref, t, g)
        border_columns(neighbours_ref, p_ref, rn_ref, rw_ref, t, g, column_in(p_ref, t, g))

    each_group(borders)
    back_tile(0, p_ref, weight_ref, y_ref, tile_ref, gated_ref, mask_ref, out_ref, sem)


def back_second_kernel(
    p_ref, mask_ref, gated_ref, taps_ref, before_ref, out_ref, weight_ref, y_ref, tile_ref, sem
):
    take_weights(weight_ref, taps_ref)
    back_tile(1, p_ref, weight_ref, y_ref, tile_ref, gated_ref, mask_ref, out_ref, sem)


def params(size=16):
    return pltpu.CompilerParams(vmem_limit_bytes=size * 1024 * 1024)


def estimate():
    return pl.CostEstimate(flops=10**9, bytes_accessed=16 * 10**6, transcendentals=0)


NEIGHBOURS = pltpu.SMEM((2, 8), jnp.int32)
P_SCRATCH = pltpu.VMEM((2, GROUPS, 22 * PITCH, 128), f32)
RN_SCRATCH = pltpu.VMEM((2, 2, GROUPS, 48, 128), f32)
RW_SCRATCH = pltpu.VMEM((2, 2, GROUPS, 80, 128), f32)
W_SCRATCH = pltpu.VMEM((56, CP), f32)
Y_SCRATCH = pltpu.VMEM((CELLS, CP), f32)


def swap_pairs(kind):
    axis, offset = kind
    pairs = []
    for w in range(32):
        for n in range(4):
            if axis == "narrow":
                up = (n - offset) % 2 == 0
                other = (w, (n + (1 if up else -1)) % 4)
            else:
                up = (w - offset) % 2 == 0
                other = ((w + (1 if up else -1)) % 32, n)
            pairs.append((w * 4 + n, other[0] * 4 + other[1]))
    return pairs


def swap(x, kind):
    return lax.ppermute(x, AXES, swap_pairs(kind))


def flip(x, mask):
    return lax.ppermute(x, AXES, [(i, i ^ mask) for i in range(128)])


STAGES = {
    "x1": (2, (1, 6)),
    "x2": (66, (6,)),
    "z1": (4, (2, 3)),
    "z2": (12, (3,)),
    "y1": (16, (4, 5)),
    "y2": (48, (5,)),
}
ORDERS = (
    ("x1", "y1", "z1", "x2", "y2", "z2"),
    ("y1", "z1", "x1", "y2", "z2", "x2"),
    ("z1", "x1", "y1", "z2", "x2", "y2"),
)
DEPTH = 2


def parity(me, bits):
    return sum((me >> bit) & 1 for bit in bits) & 1


def halved(part, step, high):
    half = part.shape[0] // 2
    low_rows, high_rows = part[0:half], part[half:]
    send = jnp.where(high, low_rows, high_rows).astype(bf16)
    keep = jnp.where(high, high_rows, low_rows)
    return keep + flip(send, STAGES[step][0]).astype(f32)


def doubled(part, step):
    mine = part.astype(bf16)
    return mine.astype(f32) + flip(mine, STAGES[step][0]).astype(f32)


def joined(part, step, high):
    got = flip(part, STAGES[step][0])
    return jnp.concatenate([jnp.where(high, got, part), jnp.where(high, part, got)], axis=0)


def together(*values):
    return lax.optimization_barrier(values)


def local(
    field,
    cotangent,
    land,
    neighbours,
    depth_weight,
    depth_bias,
    ln_gain,
    ln_shift,
    up_weight,
    up_bias,
    down_weight,
):
    me = here()
    shape = jax.ShapeDtypeStruct
    stay = lambda v: pltpu.with_memory_space_constraint(v, pltpu.HBM)
    steps = sorted({order[stage] for order in ORDERS for stage in range(DEPTH)})
    highs = [parity(me, STAGES[step][1]) == 1 for step in steps]
    highs, field = together(highs, field)
    high = dict(zip(steps, highs))
    neighbours = stay(neighbours)
    narrow_shape = shape((2, 48, CP), bf16)
    wide_shape = shape((2, 80, CP), bf16)
    wide_scratch = [
        pltpu.VMEM((2, GROUPS, TE * TE, 128), f32),
        RN_SCRATCH,
        RW_SCRATCH,
    ]
    p_shape = shape((2, GROUPS, 22 * PITCH, 128), f32)

    s1, s2, field, land = pl.pallas_call(
        narrow_kernel,
        out_shape=(
            narrow_shape,
            narrow_shape,
            shape((2, TE, TE, C), bf16),
            shape((2, TE, TE), jnp.int32),
        ),
        in_specs=[HBM] * 2,
        out_specs=(VMEM,) * 4,
        scratch_shapes=[pltpu.SemaphoreType.DMA((2,))],
        compiler_params=params(4),
        name="pack_rows",
    )(stay(field), stay(land))
    n1, n2 = swap(s1, ("narrow", 0)), swap(s2, ("narrow", 1))
    mask, gated, gated_t, down_bias_sum, up_held, down_held, taps, small = pl.pallas_call(
        hold_kernel,
        out_shape=(
            shape((CELLS, C), f32),
            shape((CELLS, CP), bf16),
            shape((CP, CELLS), bf16),
            shape((1, C), f32),
            shape((C, HID), bf16),
            shape((C, HID), bf16),
            shape((49, C), f32),
            shape((4, HID), f32),
        ),
        in_specs=[VMEM] + [HBM] * 8,
        out_specs=(VMEM,) * 8,
        scratch_shapes=[
            pltpu.VMEM((2, TE, TE, C), bf16),
            pltpu.VMEM((C,), f32),
            pltpu.VMEM((C,), f32),
            pltpu.VMEM((C,), f32),
            pltpu.VMEM((HID,), f32),
            pltpu.SemaphoreType.DMA((8,)),
        ],
        compiler_params=params(8),
        cost_estimate=estimate(),
        name="hold",
    )(
        land,
        stay(cotangent),
        stay(depth_weight),
        stay(depth_bias),
        stay(ln_gain),
        stay(ln_shift),
        stay(up_bias),
        stay(up_weight),
        stay(down_weight.T),
    )
    s1, s2 = pl.pallas_call(
        functools.partial(wide_kernel, True),
        out_shape=(wide_shape, wide_shape),
        in_specs=[VMEM] * 4,
        out_specs=(VMEM, VMEM),
        scratch_shapes=wide_scratch,
        compiler_params=params(8),
        name="pack_columns",
    )(field, mask, n1, n2)
    s1, s2, n1, n2 = together(s1, s2, n1, n2)
    w2, w1 = swap(s2, ("wide", 1)), swap(s1, ("wide", 0))
    p, y = pl.pallas_call(
        prep_kernel,
        out_shape=(p_shape, shape((2, GROUPS, TE * TE, 128), f32)),
        in_specs=[HBM] + [VMEM] * 6,
        out_specs=(VMEM,) * 2,
        scratch_shapes=[RN_SCRATCH, W_SCRATCH, NEIGHBOURS, pltpu.SemaphoreType.DMA],
        compiler_params=params(8),
        cost_estimate=estimate(),
        name="prep",
    )(neighbours, field, mask, n1, n2, taps, small)

    keep, send, ng, z, r, up_bias_sum, border = pl.pallas_call(
        front_kernel,
        out_shape=(
            shape((ROWS, 128), f32),
            shape((ROWS, 128), bf16),
            shape((CELLS, C), f32),
            shape((CELLS, C), f32),
            shape((CELLS, 128), f32),
            shape((1, HID), f32),
            shape((2, GROUPS, 6 * 24, 128), f32),
        ),
        in_specs=[HBM] + [VMEM] * 12,
        out_specs=(VMEM,) * 7,
        scratch_shapes=[
            RN_SCRATCH,
            RW_SCRATCH,
            W_SCRATCH,
            pltpu.VMEM((2, GROUPS, TE * TE, 128), f32),
            pltpu.VMEM((CELLS, CP), bf16),
            pltpu.VMEM((CP, CELLS), bf16),
            NEIGHBOURS,
            pltpu.SemaphoreType.DMA,
        ],
        compiler_params=params(14),
        name="front",
    )(
        neighbours,
        n1,
        n2,
        w1,
        w2,
        p,
        y,
        gated,
        gated_t,
        taps,
        small,
        up_held,
        down_held,
    )

    got = flip(send, 1)
    cg, g1, g2, cg_wide, sums = pl.pallas_call(
        grad_kernel,
        out_shape=(
            shape((2, TE, TE, C), bf16),
            narrow_shape,
            narrow_shape,
            shape((CELLS, CP), f32),
            shape((3, C), f32),
        ),
        in_specs=[VMEM] * 4,
        out_specs=(VMEM,) * 5,
        compiler_params=params(4),
        cost_estimate=estimate(),
        name="grad",
    )(ng, z, r, small)

    halves = [size // 2 for size in SIZES]
    pieces = pl.pallas_call(
        split_kernel,
        out_shape=tuple(shape((half, 128), bf16) for half in halves)
        + tuple(shape((half, 128), f32) for half in halves)
        + (shape((8, 128), f32),),
        in_specs=[VMEM] * 3,
        out_specs=(VMEM,) * (2 * len(SIZES) + 1),
        compiler_params=params(4),
        name="split",
    )(keep, got, sums)

    orders = list(enumerate(ORDERS))
    got = [flip(pieces[i], STAGES[order[0]][0]) for i, order in orders]
    n1, n2 = swap(g1, ("narrow", 0)), swap(g2, ("narrow", 1))
    extra = pl.pallas_call(
        taps_kernel,
        out_shape=shape((EXTRA, 128), f32),
        in_specs=[VMEM] * 7,
        out_specs=VMEM,
        scratch_shapes=[
            pltpu.VMEM(p_shape.shape, f32),
            pltpu.VMEM((GROUPS, 49, 8, 128), f32),
        ],
        compiler_params=params(8),
        cost_estimate=estimate(),
        name="taps",
    )(pieces[-1], cg_wide, p, border, sums, up_bias_sum, down_bias_sum)
    parts = [pieces[len(SIZES) + i] + got[i].astype(f32) for i, order in orders]
    parts[-1] = jnp.concatenate([parts[-1], extra], axis=0)
    parts[-1], n1, n2 = together(parts[-1], n1, n2)
    s1, s2 = pl.pallas_call(
        functools.partial(wide_kernel, False),
        out_shape=(wide_shape, wide_shape),
        in_specs=[VMEM] * 3,
        out_specs=(VMEM, VMEM),
        scratch_shapes=wide_scratch,
        compiler_params=params(8),
        name="pack_columns_back",
    )(cg, n1, n2)
    parts, s1, s2 = together(parts, s1, s2)
    w2, w1 = swap(s2, ("wide", 1)), swap(s1, ("wide", 0))
    for stage in range(1, DEPTH):
        parts = [halved(parts[i], order[stage], high[order[stage]]) for i, order in orders]
    for stage in range(DEPTH, 6):
        parts = [doubled(parts[i], order[stage]) for i, order in orders]
        if stage == 4:
            parts[-1], w1, w2 = together(parts[-1], w1, w2)
    parts = [part.astype(bf16) for part in parts]
    for stage in reversed(range(1, DEPTH)):
        parts = [joined(parts[i], order[stage], high[order[stage]]) for i, order in orders]
    parts[-1], w1, w2 = together(parts[-1], w1, w2)

    tile_scratch = [
        W_SCRATCH,
        pltpu.VMEM((TE * TE, CP), f32),
        pltpu.VMEM((TE, TE, C), bf16),
    ]
    field_grad, grad_p = pl.pallas_call(
        back_first_kernel,
        out_shape=(shape((2, TE, TE, C), bf16), p_shape),
        in_specs=[HBM] + [VMEM] * 8,
        out_specs=(HBM, VMEM),
        scratch_shapes=[RN_SCRATCH, RW_SCRATCH]
        + tile_scratch
        + [NEIGHBOURS, pltpu.SemaphoreType.DMA],
        compiler_params=params(8),
        cost_estimate=estimate(),
        name="back_first",
    )(neighbours, cg, mask, gated, n1, n2, w1, w2, taps)
    matrix = [joined(parts[i], order[0], high[order[0]]) for i, order in orders[:-1]]
    last = parts[-1]
    order = ORDERS[-1]
    got = flip(last, STAGES[order[0]][0])
    one, two = last[0 : halves[-1]], got[0 : halves[-1]]
    upper = high[order[0]]
    extra = (last[halves[-1] :].astype(f32) + got[halves[-1] :].astype(f32)).astype(bf16)
    mine = jnp.concatenate(
        matrix + [jnp.where(upper, two, one), jnp.where(upper, one, two), extra], axis=0
    )
    mine, field_grad = together(mine, field_grad)
    theirs = flip(mine, 1)
    field_grad = pl.pallas_call(
        back_second_kernel,
        out_shape=shape((2, TE, TE, C), bf16),
        in_specs=[VMEM] * 4 + [HBM],
        out_specs=HBM,
        scratch_shapes=tile_scratch + [pltpu.SemaphoreType.DMA],
        input_output_aliases={4: 0},
        compiler_params=params(8),
        cost_estimate=estimate(),
        name="back_second",
    )(grad_p, mask, gated, taps, field_grad)
    theirs, field_grad = together(theirs, field_grad)
    up_grad, down_grad, *rest = pl.pallas_call(
        unpack_kernel,
        out_shape=(
            shape((C, HID), f32),
            shape((C, HID), f32),
            shape((49, C), f32),
            shape((C,), f32),
            shape((C,), f32),
            shape((C,), f32),
            shape((HID,), f32),
            shape((C,), f32),
        ),
        in_specs=[VMEM] * 2,
        out_specs=(VMEM,) * 8,
        compiler_params=params(12),
        name="unpack",
    )(mine, theirs)
    depth_grad, depth_bias_grad, gain_grad, shift_grad, up_bias_grad, down_bias_grad = rest
    return (
        field_grad,
        depth_grad,
        depth_bias_grad,
        gain_grad,
        shift_grad,
        up_grad,
        up_bias_grad,
        down_grad.T,
        down_bias_grad,
    )


def solution(mesh):
    return jax.shard_map(
        local,
        mesh=mesh,
        in_specs=(
            P(("wide", "narrow"), None, None, None),
            P(("wide", "narrow"), None, None, None),
            P(("wide", "narrow"), None, None),
            P(("wide", "narrow"), None),
            P(),
            P(),
            P(),
            P(),
            P(),
            P(),
            P(),
        ),
        out_specs=(P(("wide", "narrow"), None, None, None), P(), P(), P(), P(), P(), P(), P(), P()),
        check_vma=False,
    )
```

```python
import functools

import jax
import jax.numpy as jnp
from jax import lax
from jax.experimental import pallas as pl
from jax.experimental.pallas import tpu as pltpu
from jax.sharding import PartitionSpec as P

epsilon = 1e-06
gelu_root = 0.7978845608028654
gelu_cubic = 0.044715

C = 400
CP = 512
HID = 1600
TE = 16
CELLS = 512
GROUPS = 4
HT = 13
PITCH = 32
ROWS = HT * C + 16
PIECES = ((0, 1024, 8 * C), (1024, 576, 5 * C + 16))
EXTRA = 272
SIZES = (1856, 1856, 1504)
AXES = ("wide", "narrow")
SLOT_ROWS = 3 * 72 + 16
SIDE_ROWS = 2 * SLOT_ROWS
f32 = jnp.float32
bf16 = jnp.bfloat16
VMEM = pl.BlockSpec(memory_space=pltpu.VMEM)
SMEM = pl.BlockSpec(memory_space=pltpu.SMEM)
HBM = pl.BlockSpec(memory_space=pltpu.HBM)


def group_width(g):
    return min(128, C - 128 * g)


def lanes(g):
    return slice(128 * g, 128 * g + group_width(g))


def land_mask(land, tiles=2):
    spread = jnp.broadcast_to(land.astype(f32)[:, :, None], (tiles * TE, TE, C))
    return spread.reshape(tiles * TE * TE, C)


def zero_lanes(ref):
    ref[...] = jnp.zeros(ref.shape, ref.dtype)


def pack_narrow(tile_rows, even, first_ref, second_ref):
    for ref in (first_ref, second_ref):
        zero_lanes(ref)
    for s in range(2):
        north = tile_rows(s, 0)
        south = tile_rows(s, TE - 3)
        first_ref[s, :, 0:C] = jnp.where(even, south, north).astype(bf16)
        second_ref[s, :, 0:C] = jnp.where(even, north, south).astype(bf16)


def narrow_kernel(field_ref, land_ref, first_ref, second_ref, held_ref, cells_ref, sems):
    copies = [
        pltpu.make_async_copy(field_ref, held_ref, sems.at[0]),
        pltpu.make_async_copy(land_ref, cells_ref, sems.at[1]),
    ]
    for copy in copies:
        copy.start()
    for copy in copies:
        copy.wait()

    def tile_rows(s, row):
        cells = held_ref[s, row : row + 3].reshape(3 * TE, C).astype(f32)
        land = cells_ref[s, row : row + 3].astype(f32)
        return cells * jnp.broadcast_to(land[:, :, None], (3, TE, C)).reshape(3 * TE, C)

    pack_narrow(tile_rows, lax.axis_index("narrow") % 2 == 0, first_ref, second_ref)


def wide_kernel(masked, *refs):
    if masked:
        tiles_ref, mask_ref, n1_ref, n2_ref, first_ref, second_ref, m_ref, r_ref, o_ref, q_ref = refs
    else:
        tiles_ref, n1_ref, n2_ref, first_ref, second_ref, m_ref, r_ref, o_ref, q_ref = refs
    n_even = lax.axis_index("narrow") % 2 == 0
    w_even = lax.axis_index("wide") % 2 == 0
    zero_lanes(o_ref)
    for s in range(2):
        cells = tiles_ref[s].reshape(TE * TE, C).astype(f32)
        if masked:
            cells = cells * mask_ref[s * TE * TE : (s + 1) * TE * TE, :]
        one = n1_ref[s].astype(f32)
        two = n2_ref[s].astype(f32)
        from_north = jnp.where(n_even, two, one)
        from_south = jnp.where(n_even, one, two)
        for g in range(GROUPS):
            m_ref[s, g, :, 0 : group_width(g)] = cells[:, lanes(g)]
            r_ref[0, s, g] = from_north[:, 128 * g : 128 * g + 128]
            r_ref[1, s, g] = from_south[:, 128 * g : 128 * g + 128]
    for s in range(2):
        for g in range(GROUPS):
            w = group_width(g)
            for side in range(2):
                for c in range(3):
                    col = c + side * (TE - 3)
                    at = c * 22
                    o_ref[side, s, g, at : at + 3, :] = r_ref[0, s, g, pl.ds(col, 3, stride=TE), :]
                    o_ref[side, s, g, at + 3 : at + 19, 0:w] = m_ref[s, g, pl.ds(col, TE, stride=TE), 0:w]
                    o_ref[side, s, g, at + 19 : at + 22, :] = r_ref[1, s, g, pl.ds(col, 3, stride=TE), :]
            west = o_ref[0, s, g, 0:72, :]
            east = o_ref[1, s, g, 0:72, :]
            at = s * SLOT_ROWS + g * 72
            for k, value in enumerate((jnp.where(w_even, east, west), jnp.where(w_even, west, east))):
                if g < GROUPS - 1:
                    q_ref[k, at : at + 72, :] = value
                else:
                    blocks = [value[8 * j : 8 * j + 8, 0:16] for j in range(9)]
                    q_ref[k, at : at + 8, :] = jnp.concatenate(blocks[0:8], axis=1)
                    q_ref[k, at + 8 : at + 16, :] = jnp.concatenate(
                        [blocks[8], jnp.zeros((8, 112), f32)], axis=1
                    )
    first_ref[...] = q_ref[0].astype(bf16)
    second_ref[...] = q_ref[1].astype(bf16)


def place_centre(cells, s, p_ref):
    for g in range(GROUPS):
        for r in range(TE):
            at = (r + 3) * PITCH + 8
            p_ref[s, g, at : at + TE, :] = cells[r * TE : (r + 1) * TE, 128 * g : 128 * g + 128]


def padded_lanes(cells):
    return jnp.concatenate([cells, jnp.zeros((cells.shape[0], CP - C), cells.dtype)], axis=1)


def place_rows(n1_ref, n2_ref, rn_ref):
    n_even = lax.axis_index("narrow") % 2 == 0
    for s in range(2):
        one = n1_ref[s].astype(f32)
        two = n2_ref[s].astype(f32)
        north = jnp.where(n_even, two, one)
        south = jnp.where(n_even, one, two)
        for g in range(GROUPS):
            at = slice(128 * g, 128 * g + 128)
            rn_ref[0, s, g] = north[:, at]
            rn_ref[1, s, g] = south[:, at]


def place_columns(w1_ref, w2_ref, rw_ref):
    w_even = lax.axis_index("wide") % 2 == 0
    one = w1_ref[...].astype(f32)
    two = w2_ref[...].astype(f32)
    for side, value in enumerate((jnp.where(w_even, two, one), jnp.where(w_even, one, two))):
        for s in range(2):
            for g in range(GROUPS):
                at = s * SLOT_ROWS + g * 72
                if g < GROUPS - 1:
                    rw_ref[side, s, g, 0:72, :] = value[at : at + 72]
                else:
                    for j in range(9):
                        rows = value[at : at + 8] if j < 8 else value[at + 8 : at + 16]
                        lane = 16 * j % 128
                        block = jnp.concatenate(
                            [rows[:, lane : lane + 16], jnp.zeros((8, 112), f32)], axis=1
                        )
                        rw_ref[side, s, g, 8 * j : 8 * j + 8, :] = block


def entry_of(neighbours_ref, t, d):
    e = neighbours_ref[t, d]
    near = jnp.maximum(e, 0)
    return e >= 0, near // 2, near % 2


def chosen(options, present):
    value = options[-1][1]
    for test, other in reversed(options[:-1]):
        value = jnp.where(test, other, value)
    return jnp.where(present, value, 0.0)


def here():
    return lax.axis_index("wide") * lax.axis_size("narrow") + lax.axis_index("narrow")


def border_rows(neighbours_ref, p_ref, rn_ref, t, g):
    for d in range(2):
        present, device, slot = entry_of(neighbours_ref, t, d)
        from_row = 3 + TE - 3 if d == 0 else 3
        to_row = 0 if d == 0 else 3 + TE
        for i in range(3):
            own = p_ref[slot, g, pl.ds((from_row + i) * PITCH + 8, TE), :]
            other = rn_ref[d, slot, g, pl.ds(i * TE, TE), :]
            p_ref[t, g, pl.ds((to_row + i) * PITCH + 8, TE), :] = chosen(
                [(device == here(), own), (None, other)], present
            )


def border_columns(neighbours_ref, p_ref, rn_ref, rw_ref, t, g, put):
    narrow = lax.axis_size("narrow")
    for d in range(2):
        present, device, slot = entry_of(neighbours_ref, t, 2 + d)
        from_col = 8 + TE - 3 if d == 0 else 8
        for c in range(3):
            own = p_ref[slot, g, pl.ds(3 * PITCH + from_col + c, TE, stride=PITCH), :]
            other = rw_ref[d, slot, g, pl.ds(c * 22 + 3, TE), :]
            put(d, c, 3, TE, chosen([(device == here(), own), (None, other)], present))
    for d in range(4):
        south, east = d // 2, d % 2
        present, device, slot = entry_of(neighbours_ref, t, 4 + d)
        same_w = device // narrow == lax.axis_index("wide")
        same_n = device % narrow == lax.axis_index("narrow")
        from_row = 3 if south else 3 + TE - 3
        to_row = 3 + TE if south else 0
        from_col = 8 if east else 8 + TE - 3
        for c in range(3):
            own = p_ref[slot, g, pl.ds(from_row * PITCH + from_col + c, 3, stride=PITCH), :]
            beyond = rn_ref[south, slot, g, pl.ds(from_col - 8 + c, 3, stride=TE), :]
            beside = rw_ref[east, slot, g, pl.ds(c * 22 + from_row, 3), :]
            across = rw_ref[east, slot, g, pl.ds(c * 22 + (19 if south else 0), 3), :]
            put(
                east,
                c,
                to_row,
                3,
                chosen(
                    [(device == here(), own), (same_w, beyond), (same_n, beside), (None, across)], present
                ),
            )


def column_in(p_ref, t, g):
    def put(side, c, row, count, value):
        at = row * PITCH + (8 + TE if side else 5) + c
        p_ref[t, g, pl.ds(at, count, stride=PITCH), :] = value

    return put


def each_group(body, tiles=(0, 1)):
    def step(i, _):
        body(tiles[0] + i // GROUPS, i % GROUPS)
        return _

    lax.fori_loop(0, len(tiles) * GROUPS, step, 0)


def weight_rows(weight_ref, g, taps):
    at = pl.ds(pl.multiple_of(g * 128, 128), 128)
    return [jnp.broadcast_to(weight_ref[pl.ds(k, 1), at], (8, 128)) for k in taps]


def convolve(p_ref, weight_ref, start, finish, flip, tiles=(0, 1)):
    def body(t, g):
        for h in range(2):
            total = start(t, g, h)
            for b in range(7):
                taps = [48 - (7 * a + b) if flip else 7 * a + b for a in range(7)]
                weights = weight_rows(weight_ref, g, taps)
                for row in range(22):
                    x = p_ref[t, g, pl.ds(row * PITCH + 5 + b + 8 * h, 8), :]
                    for a in range(7):
                        r = row - a
                        if 0 <= r < TE:
                            total[r] = total[r] + weights[a] * x
            finish(t, g, h, total)

    each_group(body, tiles)


def gelu_pair(hidden):
    square = hidden * hidden
    bent = jnp.tanh(gelu_root * hidden * (1.0 + gelu_cubic * square))
    half = 0.5 * (1.0 + bent)
    slope = half + 0.5 * hidden * (1.0 - bent * bent) * (gelu_root * (1.0 + 3.0 * gelu_cubic * square))
    return hidden * half, slope


def take_weights(weight_ref, depth_weight_ref):
    weight_ref[...] = jnp.zeros(weight_ref.shape, f32)
    weight_ref[0:49, 0:C] = depth_weight_ref[...]


def hold_kernel(
    land_ref,
    cot_ref,
    depth_weight_ref,
    depth_bias_ref,
    gain_ref,
    shift_ref,
    up_bias_ref,
    up_ref,
    down_ref,
    mask_ref,
    gated_ref,
    gated_t_ref,
    down_bias_ref,
    up_out_ref,
    down_out_ref,
    taps_ref,
    small_ref,
    cot_in_ref,
    bias_in_ref,
    gain_in_ref,
    shift_in_ref,
    up_bias_in_ref,
    sems,
):
    pairs = (
        (cot_ref, cot_in_ref),
        (depth_weight_ref, taps_ref),
        (depth_bias_ref, bias_in_ref),
        (gain_ref, gain_in_ref),
        (shift_ref, shift_in_ref),
        (up_bias_ref, up_bias_in_ref),
        (up_ref, up_out_ref),
        (down_ref, down_out_ref),
    )
    copies = [pltpu.make_async_copy(a, b, sems.at[k]) for k, (a, b) in enumerate(pairs)]
    for copy in copies:
        copy.start()
    mask_ref[...] = land_mask(land_ref[...].reshape(2 * TE, TE))
    copies[0].wait()
    gated = cot_in_ref[...].reshape(CELLS, C).astype(f32) * mask_ref[...]
    gated_ref[...] = padded_lanes(gated).astype(bf16)
    gated_t_ref[...] = gated_ref[...].T
    down_bias_ref[...] = jnp.sum(gated, axis=0, keepdims=True)
    for copy in copies[1:]:
        copy.wait()
    small_ref[0:1, 0:C] = bias_in_ref[...].reshape(1, C)
    small_ref[1:2, 0:C] = gain_in_ref[...].reshape(1, C)
    small_ref[2:3, 0:C] = shift_in_ref[...].reshape(1, C)
    small_ref[3:4, :] = up_bias_in_ref[...].reshape(1, HID)


def prep_kernel(
    beside_ref,
    field_ref,
    mask_ref,
    n1_ref,
    n2_ref,
    taps_ref,
    small_ref,
    p_ref,
    y_ref,
    rn_ref,
    weight_ref,
    neighbours_ref,
    sem,
):
    copy = pltpu.make_async_copy(beside_ref, neighbours_ref, sem)
    copy.start()
    p_ref[...] = jnp.zeros(p_ref.shape, f32)
    for s in range(2):
        cells = field_ref[s].reshape(TE * TE, C).astype(f32)
        place_centre(padded_lanes(cells * mask_ref[s * TE * TE : (s + 1) * TE * TE, :]), s, p_ref)
    place_rows(n1_ref, n2_ref, rn_ref)
    take_weights(weight_ref, taps_ref)
    weight_ref[49:50, 0:C] = small_ref[0:1, 0:C]
    copy.wait()
    each_group(lambda t, g: border_rows(neighbours_ref, p_ref, rn_ref, t, g))

    def start(t, g, h):
        return weight_rows(weight_ref, g, [49]) * TE

    def finish(t, g, h, rows):
        for r in range(TE):
            y_ref[t, g, pl.ds(r * TE + 8 * h, 8), :] = rows[r]

    convolve(p_ref, weight_ref, start, finish, False)


def front_kernel(
    beside_ref,
    n1_ref,
    n2_ref,
    w1_ref,
    w2_ref,
    p_ref,
    y_in_ref,
    gated_ref,
    gated_t_ref,
    depth_weight_ref,
    small_ref,
    up_ref,
    down_ref,
    keep_ref,
    send_ref,
    ng_ref,
    up_bias_sum_ref,
    z_ref,
    r_ref,
    border_ref,
    normed_ref,
    normed_t_ref,
    rn_ref,
    rw_ref,
    weight_ref,
    y_ref,
    neighbours_ref,
    sem,
):
    copy = pltpu.make_async_copy(beside_ref, neighbours_ref, sem)
    copy.start()
    place_rows(n1_ref, n2_ref, rn_ref)
    place_columns(w1_ref, w2_ref, rw_ref)
    take_weights(weight_ref, depth_weight_ref)
    y_ref[...] = y_in_ref[...]
    copy.wait()

    def sides(t, g):
        def put(side, c, row, count, value):
            border_ref[t, g, pl.ds((side * 3 + c) * 24 + row, count), :] = value

        border_columns(neighbours_ref, p_ref, rn_ref, rw_ref, t, g, put)
        at = pl.ds(pl.multiple_of(g * 128, 128), 128)
        for side in range(2):
            for out in range(3):
                col = out + side * (TE - 3)
                total = y_ref[t, g, pl.ds(col, TE, stride=TE), :]
                for c in range(3):
                    b = (19 + c if side else c) - col
                    if 0 <= b < 7:
                        for a in range(7):
                            cells = border_ref[t, g, pl.ds((side * 3 + c) * 24 + a, TE), :]
                            total = total + weight_ref[pl.ds(7 * a + b, 1), at] * cells
                y_ref[t, g, pl.ds(col, TE, stride=TE), :] = total

    each_group(sides)

    normed_ref[...] = jnp.zeros(normed_ref.shape, bf16)
    step_rows = 128

    def norm(i, _):
        at = pl.ds(pl.multiple_of(i * step_rows, step_rows), step_rows)
        inside = pl.ds(pl.multiple_of((i % 2) * step_rows, step_rows), step_rows)
        conv = jnp.concatenate([y_ref[i // 2, g, inside, :] for g in range(GROUPS)], axis=1)[:, 0:C]
        mean = jnp.sum(conv, axis=1, keepdims=True) * (1.0 / C)
        dev = conv - mean
        var = jnp.sum(dev * dev, axis=1, keepdims=True) * (1.0 / C)
        rstd = lax.rsqrt(var + epsilon)
        zhat = dev * rstd
        z_ref[at, :] = zhat
        r_ref[at, :] = jnp.broadcast_to(rstd, (step_rows, 128))
        normed_ref[at, 0:C] = (zhat * small_ref[1:2, 0:C] + small_ref[2:3, 0:C]).astype(bf16)
        return _

    lax.fori_loop(0, CELLS // step_rows, norm, 0)
    normed_t_ref[...] = normed_ref[...].T

    hidden(
        0,
        normed_ref,
        normed_t_ref,
        gated_ref,
        gated_t_ref,
        small_ref,
        up_ref,
        down_ref,
        keep_ref,
        send_ref,
        ng_ref,
        up_bias_sum_ref,
    )


def hidden(
    piece,
    normed_ref,
    normed_t_ref,
    gated_ref,
    gated_t_ref,
    small_ref,
    up_ref,
    down_ref,
    keep_ref,
    send_ref,
    ng_ref,
    up_bias_sum_ref,
):
    core0 = lax.axis_index("narrow") % 2 == 0
    first, count, rows = PIECES[piece]
    used = (count + 127) // 128 * C
    if used < rows:
        keep_ref[used:, :] = jnp.zeros((rows - used, 128), f32)
        send_ref[used:, :] = jnp.zeros((rows - used, 128), bf16)

    def products(lo, width):
        at = slice(first + lo, first + lo + width)
        h = jnp.dot(normed_ref[:, 0:C], up_ref[:, at], preferred_element_type=f32) + small_ref[3:4, at]
        ag = jnp.dot(gated_ref[:, 0:C], down_ref[:, at], preferred_element_type=f32)
        return h, ag

    def gradients(lo, width, h, ag):
        at = slice(first + lo, first + lo + width)
        act, slope = gelu_pair(h)
        hg = ag * slope
        hgb = hg.astype(bf16)
        dg = jnp.dot(gated_t_ref[0:C, :], act.astype(bf16), preferred_element_type=f32)
        ug = jnp.dot(normed_t_ref[0:C, :], hgb, preferred_element_type=f32)
        ng = lax.dot_general(hgb, up_ref[:, at], (((1,), (1,)), ((), ())), preferred_element_type=f32)
        if lo == 0:
            ng_ref[...] = ng
        else:
            ng_ref[...] += ng
        up_bias_sum_ref[:, lo : lo + width] = jnp.sum(hgb.astype(f32), axis=0, keepdims=True)
        keep = jnp.where(core0, ug, dg)
        send = jnp.where(core0, dg, ug).astype(bf16)
        for k in range((width + 127) // 128):
            w = min(128, width - 128 * k)
            at = slice((lo // 128 + k) * C, (lo // 128 + k + 1) * C)
            if w < 128:
                keep_ref[at, :] = jnp.zeros((C, 128), f32)
                send_ref[at, :] = jnp.zeros((C, 128), bf16)
            keep_ref[at, 0:w] = keep[:, 128 * k : 128 * k + w]
            send_ref[at, 0:w] = send[:, 128 * k : 128 * k + w]

    cut = 512 if piece == 0 else 256
    chunks = ((0, cut), (cut, count - cut))
    ready = products(*chunks[0])
    for i, chunk in enumerate(chunks):
        current = ready
        if i + 1 < len(chunks):
            ready = products(*chunks[i + 1])
        gradients(*chunk, *current)


def grad_kernel(
    ng0_ref,
    ng1_ref,
    z_ref,
    r_ref,
    small_ref,
    cg_ref,
    g1_ref,
    g2_ref,
    y_ref,
    sums_ref,
):
    y_ref[...] = jnp.zeros(y_ref.shape, f32)
    step_rows = 64

    def back(i, sums):
        at = pl.ds(pl.multiple_of(i * step_rows, step_rows), step_rows)
        ng = ng0_ref[at, :] + ng1_ref[at, :]
        zhat = z_ref[at, :]
        rstd = r_ref[at, 0:1]
        q = ng * small_ref[1:2, 0:C]
        a = jnp.sum(q, axis=1, keepdims=True) * (1.0 / C)
        b = jnp.sum(q * zhat, axis=1, keepdims=True) * (1.0 / C)
        cg = (rstd * (q - a - zhat * b)).astype(bf16)
        cg_ref[i // 4, pl.ds((i % 4) * 4, 4)] = cg.reshape(4, TE, C)
        wide = cg.astype(f32)
        y_ref[at, 0:C] = wide
        return (
            sums[0] + jnp.sum(ng * zhat, axis=0, keepdims=True),
            sums[1] + jnp.sum(ng, axis=0, keepdims=True),
            sums[2] + jnp.sum(wide, axis=0, keepdims=True),
        )

    zero = jnp.zeros((1, C), f32)
    gain_sum, shift_sum, bias_sum = lax.fori_loop(0, CELLS // step_rows, back, (zero, zero, zero))
    sums_ref[0:1, :] = bias_sum
    sums_ref[1:2, :] = gain_sum
    sums_ref[2:3, :] = shift_sum

    def tile_rows(s, row):
        at = s * TE * TE + row * TE
        return y_ref[at : at + 3 * TE, 0:C]

    pack_narrow(tile_rows, lax.axis_index("narrow") % 2 == 0, g1_ref, g2_ref)

def taps_kernel(
    after_ref, y_ref, p_in_ref, border_ref, sums_ref, ub0_ref, ub1_ref, down_bias_ref, extra_ref, p_ref, dw_ref
):
    p_ref[...] = p_in_ref[...]
    dw_ref[...] = jnp.zeros(dw_ref.shape, f32)

    def taps(t, g):
        put = column_in(p_ref, t, g)
        for side in range(2):
            for c in range(3):
                put(side, c, 0, 22, border_ref[t, g, pl.ds((side * 3 + c) * 24, 22), :])
        for h in range(2):
            cg = [
                y_ref[
                    pl.ds(t * TE * TE + r * TE + 8 * h, 8),
                    pl.ds(pl.multiple_of(g * 128, 128), 128),
                ]
                for r in range(TE)
            ]
            for b in range(7):
                total = [None] * 7
                for row in range(22):
                    x = p_ref[t, g, pl.ds(row * PITCH + 5 + b + 8 * h, 8), :]
                    for a in range(7):
                        r = row - a
                        if 0 <= r < TE:
                            term = x * cg[r]
                            total[a] = term if total[a] is None else total[a] + term
                for a in range(7):
                    dw_ref[g, 7 * a + b] += total[a]

    each_group(taps)

    extra_ref[...] = jnp.zeros(extra_ref.shape, f32)
    for g in range(GROUPS):
        w = group_width(g)
        extra_ref[g * 64 : g * 64 + 49, :] = jnp.sum(dw_ref[g], axis=1)
        extra_ref[g * 64 + 49 : g * 64 + 50, 0:w] = sums_ref[0:1, lanes(g)]
        extra_ref[g * 64 + 50 : g * 64 + 51, 0:w] = sums_ref[1:2, lanes(g)]
        extra_ref[g * 64 + 51 : g * 64 + 52, 0:w] = sums_ref[2:3, lanes(g)]
        extra_ref[g * 64 + 52 : g * 64 + 53, 0:w] = down_bias_ref[:, lanes(g)]
    for (first, count, _), ref in zip(PIECES, (ub0_ref, ub1_ref)):
        for lo in range(0, count, 128):
            w = min(128, count - lo)
            at = 256 + (first + lo) // 128
            extra_ref[at : at + 1, 0:w] = ref[:, lo : lo + w]


def split_kernel(keep0_ref, got0_ref, keep1_ref, got1_ref, after_ref, *refs):
    me = here()
    refs[-1][...] = jnp.zeros((8, 128), f32)
    lo = 0
    for i, size in enumerate(SIZES):
        send_ref, mine_ref = refs[i], refs[len(SIZES) + i]
        high = jnp.where(keeps_high(me, ORDERS[i], 0), 1, 0)
        half = size // 2
        for j in range(2):

            def store(ref, lo=lo):
                first = 0
                for (_, _, rows), keep_ref, got_ref in zip(
                    PIECES, (keep0_ref, keep1_ref), (got0_ref, got1_ref)
                ):
                    at = slice(max(lo - first, 0), min(lo + half - first, rows))
                    if at.start < at.stop:
                        total = keep_ref[at, :] + got_ref[at, :].astype(f32)
                        to = slice(at.start + first - lo, at.stop + first - lo)
                        ref[to, :] = total.astype(ref.dtype)
                    first += rows

            pl.when(high == j)(functools.partial(store, mine_ref))
            pl.when(high != j)(functools.partial(store, send_ref))
            lo += half


def unpack_kernel(mine_ref, theirs_ref, up_ref, down_ref, taps_ref, bias_ref, gain_ref, shift_ref, up_bias_ref, down_bias_ref):
    core0 = lax.axis_index("narrow") % 2 == 0
    for l in range(HT):
        w = min(128, HID - 128 * l)
        rows = slice(l * C, l * C + C)
        one = mine_ref[rows, :].astype(f32)
        two = theirs_ref[rows, :].astype(f32)
        up_ref[:, 128 * l : 128 * l + w] = jnp.where(core0, one, two)[:, 0:w]
        down_ref[:, 128 * l : 128 * l + w] = jnp.where(core0, two, one)[:, 0:w]
    extra = mine_ref[ROWS:, :].astype(f32) + theirs_ref[ROWS:, :].astype(f32)
    for g in range(GROUPS):
        taps_ref[:, lanes(g)] = extra[g * 64 : g * 64 + 49, 0 : group_width(g)]
    for k, ref in enumerate((bias_ref, gain_ref, shift_ref, down_bias_ref)):
        at = 49 + k
        vector = jnp.concatenate([extra[g * 64 + at : g * 64 + at + 1] for g in range(GROUPS)], axis=1)
        ref[...] = vector[:, 0:C].reshape(C)
    vector = jnp.concatenate([extra[256 + l : 257 + l] for l in range(HT)], axis=1)
    up_bias_ref[...] = vector[:, 0:HID].reshape(HID)


def back_tile(t, p_ref, weight_ref, y_ref, tile_ref, gated_ref, mask_ref, out_ref, sem):
    at = slice(t * TE * TE, (t + 1) * TE * TE)
    y_ref[...] = gated_ref[at, :].astype(f32)

    def place(g, h, r):
        return (pl.ds(r * TE + 8 * h, 8), pl.ds(pl.multiple_of(g * 128, 128), 128))

    def start(t, g, h):
        return [y_ref[place(g, h, r)] for r in range(TE)]

    def finish(t, g, h, rows):
        for r in range(TE):
            y_ref[place(g, h, r)] = rows[r]

    convolve(p_ref, weight_ref, start, finish, True, (t,))
    tile_ref[...] = (y_ref[:, 0:C] * mask_ref[at, :]).astype(bf16).reshape(TE, TE, C)
    copy = pltpu.make_async_copy(tile_ref, out_ref.at[t], sem)
    copy.start()
    copy.wait()


def back_first_kernel(
    beside_ref,
    cg_ref,
    mask_ref,
    gated_ref,
    n1_ref,
    n2_ref,
    w1_ref,
    w2_ref,
    taps_ref,
    out_ref,
    p_ref,
    rn_ref,
    rw_ref,
    weight_ref,
    y_ref,
    tile_ref,
    neighbours_ref,
    sem,
):
    copy = pltpu.make_async_copy(beside_ref, neighbours_ref, sem)
    copy.start()
    for s in range(2):
        place_centre(padded_lanes(cg_ref[s].reshape(TE * TE, C).astype(f32)), s, p_ref)
    place_rows(n1_ref, n2_ref, rn_ref)
    place_columns(w1_ref, w2_ref, rw_ref)
    take_weights(weight_ref, taps_ref)
    copy.wait()

    def borders(t, g):
        border_rows(neighbours_ref, p_ref, rn_ref, t, g)
        border_columns(neighbours_ref, p_ref, rn_ref, rw_ref, t, g, column_in(p_ref, t, g))

    each_group(borders)
    back_tile(0, p_ref, weight_ref, y_ref, tile_ref, gated_ref, mask_ref, out_ref, sem)


def back_second_kernel(
    p_ref, mask_ref, gated_ref, taps_ref, before_ref, out_ref, weight_ref, y_ref, tile_ref, sem
):
    take_weights(weight_ref, taps_ref)
    back_tile(1, p_ref, weight_ref, y_ref, tile_ref, gated_ref, mask_ref, out_ref, sem)


def params(size=16):
    return pltpu.CompilerParams(vmem_limit_bytes=size * 1024 * 1024)


def estimate():
    return pl.CostEstimate(flops=10**9, bytes_accessed=16 * 10**6, transcendentals=0)


NEIGHBOURS = pltpu.SMEM((2, 8), jnp.int32)
P_SCRATCH = pltpu.VMEM((2, GROUPS, 22 * PITCH, 128), f32)
RN_SCRATCH = pltpu.VMEM((2, 2, GROUPS, 48, 128), f32)
RW_SCRATCH = pltpu.VMEM((2, 2, GROUPS, 80, 128), f32)
W_SCRATCH = pltpu.VMEM((56, CP), f32)
Y_SCRATCH = pltpu.VMEM((CELLS, CP), f32)


def swap_pairs(kind):
    axis, offset = kind
    pairs = []
    for w in range(32):
        for n in range(4):
            if axis == "narrow":
                up = (n - offset) % 2 == 0
                other = (w, (n + (1 if up else -1)) % 4)
            else:
                up = (w - offset) % 2 == 0
                other = ((w + (1 if up else -1)) % 32, n)
            pairs.append((w * 4 + n, other[0] * 4 + other[1]))
    return pairs


def swap(x, kind):
    return lax.ppermute(x, AXES, swap_pairs(kind))


def flip(x, mask):
    return lax.ppermute(x, AXES, [(i, i ^ mask) for i in range(128)])


STAGES = {
    "x1": (2, (1, 6)),
    "x2": (66, (6,)),
    "z1": (4, (2, 3)),
    "z2": (12, (3,)),
    "y1": (16, (4, 5)),
    "y2": (48, (5,)),
}
ORDERS = (
    ("x1", "y1", "z1", "x2", "y2", "z2"),
    ("y1", "z1", "x1", "y2", "z2", "x2"),
    ("z1", "x1", "y1", "z2", "x2", "y2"),
)
DEPTH = 2


def parity(me, bits):
    return sum((me >> bit) & 1 for bit in bits) & 1


def exchange(x, order, stage):
    masks = [STAGES[order[(stage + 3 * core) % 6]][0] for core in range(2)]
    return lax.ppermute(x, AXES, [(i, i ^ masks[i & 1]) for i in range(128)])


def keeps_high(me, order, stage):
    zero, one = (parity(me, STAGES[order[(stage + 3 * core) % 6]][1]) for core in range(2))
    return jnp.where(me % 2 == 0, zero, one) == 1


def halved(part, order, stage, high):
    half = part.shape[0] // 2
    low_rows, high_rows = part[0:half], part[half:]
    send = jnp.where(high, low_rows, high_rows).astype(bf16)
    keep = jnp.where(high, high_rows, low_rows)
    return keep + exchange(send, order, stage).astype(f32)


def doubled(part, order, stage):
    mine = part.astype(bf16)
    return mine.astype(f32) + exchange(mine, order, stage).astype(f32)


def joined(part, order, stage, high):
    got = exchange(part, order, stage)
    return jnp.concatenate([jnp.where(high, got, part), jnp.where(high, part, got)], axis=0)


def together(*values):
    return lax.optimization_barrier(values)


def local(
    field,
    cotangent,
    land,
    neighbours,
    depth_weight,
    depth_bias,
    ln_gain,
    ln_shift,
    up_weight,
    up_bias,
    down_weight,
):
    me = here()
    shape = jax.ShapeDtypeStruct
    stay = lambda v: pltpu.with_memory_space_constraint(v, pltpu.HBM)
    high = [[keeps_high(me, order, stage) for stage in range(DEPTH)] for order in ORDERS]
    high, field = together(high, field)
    neighbours = stay(neighbours)
    narrow_shape = shape((2, 48, CP), bf16)
    wide_shape = shape((SIDE_ROWS, 128), bf16)
    wide_scratch = [
        pltpu.VMEM((2, GROUPS, TE * TE, 128), f32),
        RN_SCRATCH,
        RW_SCRATCH,
        pltpu.VMEM((2, SIDE_ROWS, 128), f32),
    ]
    p_shape = shape((2, GROUPS, 22 * PITCH, 128), f32)

    s1, s2, field, land = pl.pallas_call(
        narrow_kernel,
        out_shape=(
            narrow_shape,
            narrow_shape,
            shape((2, TE, TE, C), bf16),
            shape((2, TE, TE), jnp.int32),
        ),
        in_specs=[HBM] * 2,
        out_specs=(VMEM,) * 4,
        scratch_shapes=[pltpu.SemaphoreType.DMA((2,))],
        compiler_params=params(4),
        name="pack_rows",
    )(stay(field), stay(land))
    n1, n2 = swap(s1, ("narrow", 0)), swap(s2, ("narrow", 1))
    mask, gated, gated_t, down_bias_sum, up_held, down_held, taps, small = pl.pallas_call(
        hold_kernel,
        out_shape=(
            shape((CELLS, C), f32),
            shape((CELLS, CP), bf16),
            shape((CP, CELLS), bf16),
            shape((1, C), f32),
            shape((C, HID), bf16),
            shape((C, HID), bf16),
            shape((49, C), f32),
            shape((4, HID), f32),
        ),
        in_specs=[VMEM] + [HBM] * 8,
        out_specs=(VMEM,) * 8,
        scratch_shapes=[
            pltpu.VMEM((2, TE, TE, C), bf16),
            pltpu.VMEM((C,), f32),
            pltpu.VMEM((C,), f32),
            pltpu.VMEM((C,), f32),
            pltpu.VMEM((HID,), f32),
            pltpu.SemaphoreType.DMA((8,)),
        ],
        compiler_params=params(8),
        cost_estimate=estimate(),
        name="hold",
    )(
        land,
        stay(cotangent),
        stay(depth_weight),
        stay(depth_bias),
        stay(ln_gain),
        stay(ln_shift),
        stay(up_bias),
        stay(up_weight),
        stay(down_weight.T),
    )
    s1, s2 = pl.pallas_call(
        functools.partial(wide_kernel, True),
        out_shape=(wide_shape, wide_shape),
        in_specs=[VMEM] * 4,
        out_specs=(VMEM, VMEM),
        scratch_shapes=wide_scratch,
        compiler_params=params(8),
        name="pack_columns",
    )(field, mask, n1, n2)
    s1, s2, n1, n2 = together(s1, s2, n1, n2)
    w2, w1 = swap(s2, ("wide", 1)), swap(s1, ("wide", 0))
    p, y = pl.pallas_call(
        prep_kernel,
        out_shape=(p_shape, shape((2, GROUPS, TE * TE, 128), f32)),
        in_specs=[HBM] + [VMEM] * 6,
        out_specs=(VMEM,) * 2,
        scratch_shapes=[RN_SCRATCH, W_SCRATCH, NEIGHBOURS, pltpu.SemaphoreType.DMA],
        compiler_params=params(8),
        cost_estimate=estimate(),
        name="prep",
    )(neighbours, field, mask, n1, n2, taps, small)

    def piece_shapes(piece):
        _, count, rows = PIECES[piece]
        return (
            shape((rows, 128), f32),
            shape((rows, 128), bf16),
            shape((CELLS, C), f32),
            shape((1, count), f32),
        )

    keep0, send0, ng0, ub0, z, r, border, normed, normed_t = pl.pallas_call(
        front_kernel,
        out_shape=piece_shapes(0)
        + (
            shape((CELLS, C), f32),
            shape((CELLS, 128), f32),
            shape((2, GROUPS, 6 * 24, 128), f32),
            shape((CELLS, CP), bf16),
            shape((CP, CELLS), bf16),
        ),
        in_specs=[HBM] + [VMEM] * 12,
        out_specs=(VMEM,) * 9,
        scratch_shapes=[
            RN_SCRATCH,
            RW_SCRATCH,
            W_SCRATCH,
            pltpu.VMEM((2, GROUPS, TE * TE, 128), f32),
            NEIGHBOURS,
            pltpu.SemaphoreType.DMA,
        ],
        compiler_params=params(14),
        name="front",
    )(
        neighbours,
        n1,
        n2,
        w1,
        w2,
        p,
        y,
        gated,
        gated_t,
        taps,
        small,
        up_held,
        down_held,
    )
    got0 = flip(send0, 1)
    keep1, send1, ng1, ub1 = pl.pallas_call(
        functools.partial(hidden, 1),
        out_shape=piece_shapes(1),
        in_specs=[VMEM] * 7,
        out_specs=(VMEM,) * 4,
        compiler_params=params(12),
        cost_estimate=estimate(),
        name="hidden",
    )(normed, normed_t, gated, gated_t, small, up_held, down_held)
    got1 = flip(send1, 1)
    cg, g1, g2, cg_wide, sums = pl.pallas_call(
        grad_kernel,
        out_shape=(
            shape((2, TE, TE, C), bf16),
            narrow_shape,
            narrow_shape,
            shape((CELLS, CP), f32),
            shape((3, C), f32),
        ),
        in_specs=[VMEM] * 5,
        out_specs=(VMEM,) * 5,
        compiler_params=params(4),
        cost_estimate=estimate(),
        name="grad",
    )(ng0, ng1, z, r, small)

    halves = [size // 2 for size in SIZES]
    pieces = pl.pallas_call(
        split_kernel,
        out_shape=tuple(shape((half, 128), bf16) for half in halves)
        + tuple(shape((half, 128), f32) for half in halves)
        + (shape((8, 128), f32),),
        in_specs=[VMEM] * 5,
        out_specs=(VMEM,) * (2 * len(SIZES) + 1),
        compiler_params=params(4),
        name="split",
    )(keep0, got0, keep1, got1, sums)

    orders = list(enumerate(ORDERS))
    got = [exchange(pieces[i], order, 0) for i, order in orders]
    n1, n2 = swap(g1, ("narrow", 0)), swap(g2, ("narrow", 1))
    extra = pl.pallas_call(
        taps_kernel,
        out_shape=shape((EXTRA, 128), f32),
        in_specs=[VMEM] * 8,
        out_specs=VMEM,
        scratch_shapes=[
            pltpu.VMEM(p_shape.shape, f32),
            pltpu.VMEM((GROUPS, 49, 8, 128), f32),
        ],
        compiler_params=params(8),
        cost_estimate=estimate(),
        name="taps",
    )(pieces[-1], cg_wide, p, border, sums, ub0, ub1, down_bias_sum)
    parts = [pieces[len(SIZES) + i] + got[i].astype(f32) for i, order in orders]
    parts[-1] = jnp.concatenate([parts[-1], extra], axis=0)
    parts[-1], n1, n2 = together(parts[-1], n1, n2)
    s1, s2 = pl.pallas_call(
        functools.partial(wide_kernel, False),
        out_shape=(wide_shape, wide_shape),
        in_specs=[VMEM] * 3,
        out_specs=(VMEM, VMEM),
        scratch_shapes=wide_scratch,
        compiler_params=params(8),
        name="pack_columns_back",
    )(cg, n1, n2)
    parts, s1, s2 = together(parts, s1, s2)
    w2, w1 = swap(s2, ("wide", 1)), swap(s1, ("wide", 0))
    for stage in range(1, DEPTH):
        parts = [halved(parts[i], order, stage, high[i][stage]) for i, order in orders]
    for stage in range(DEPTH, 6):
        parts = [doubled(parts[i], order, stage) for i, order in orders]
        if stage == 4:
            parts[-1], w1, w2 = together(parts[-1], w1, w2)
    parts = [part.astype(bf16) for part in parts]
    for stage in reversed(range(1, DEPTH)):
        parts = [joined(parts[i], order, stage, high[i][stage]) for i, order in orders]
    parts[-1], w1, w2 = together(parts[-1], w1, w2)

    tile_scratch = [
        W_SCRATCH,
        pltpu.VMEM((TE * TE, CP), f32),
        pltpu.VMEM((TE, TE, C), bf16),
    ]
    field_grad, grad_p = pl.pallas_call(
        back_first_kernel,
        out_shape=(shape((2, TE, TE, C), bf16), p_shape),
        in_specs=[HBM] + [VMEM] * 8,
        out_specs=(HBM, VMEM),
        scratch_shapes=[RN_SCRATCH, RW_SCRATCH]
        + tile_scratch
        + [NEIGHBOURS, pltpu.SemaphoreType.DMA],
        compiler_params=params(8),
        cost_estimate=estimate(),
        name="back_first",
    )(neighbours, cg, mask, gated, n1, n2, w1, w2, taps)
    matrix = [joined(parts[i], order, 0, high[i][0]) for i, order in orders[:-1]]
    last = parts[-1]
    order = ORDERS[-1]
    got = exchange(last, order, 0)
    one, two = last[0 : halves[-1]], got[0 : halves[-1]]
    upper = high[-1][0]
    extra = (last[halves[-1] :].astype(f32) + got[halves[-1] :].astype(f32)).astype(bf16)
    mine = jnp.concatenate(
        matrix + [jnp.where(upper, two, one), jnp.where(upper, one, two), extra], axis=0
    )
    mine, field_grad = together(mine, field_grad)
    theirs = flip(mine, 1)
    field_grad = pl.pallas_call(
        back_second_kernel,
        out_shape=shape((2, TE, TE, C), bf16),
        in_specs=[VMEM] * 4 + [HBM],
        out_specs=HBM,
        scratch_shapes=tile_scratch + [pltpu.SemaphoreType.DMA],
        input_output_aliases={4: 0},
        compiler_params=params(8),
        cost_estimate=estimate(),
        name="back_second",
    )(grad_p, mask, gated, taps, field_grad)
    theirs, field_grad = together(theirs, field_grad)
    up_grad, down_grad, *rest = pl.pallas_call(
        unpack_kernel,
        out_shape=(
            shape((C, HID), f32),
            shape((C, HID), f32),
            shape((49, C), f32),
            shape((C,), f32),
            shape((C,), f32),
            shape((C,), f32),
            shape((HID,), f32),
            shape((C,), f32),
        ),
        in_specs=[VMEM] * 2,
        out_specs=(VMEM,) * 8,
        compiler_params=params(12),
        name="unpack",
    )(mine, theirs)
    depth_grad, depth_bias_grad, gain_grad, shift_grad, up_bias_grad, down_bias_grad = rest
    return (
        field_grad,
        depth_grad,
        depth_bias_grad,
        gain_grad,
        shift_grad,
        up_grad,
        up_bias_grad,
        down_grad.T,
        down_bias_grad,
    )


def solution(mesh):
    return jax.shard_map(
        local,
        mesh=mesh,
        in_specs=(
            P(("wide", "narrow"), None, None, None),
            P(("wide", "narrow"), None, None, None),
            P(("wide", "narrow"), None, None),
            P(("wide", "narrow"), None),
            P(),
            P(),
            P(),
            P(),
            P(),
            P(),
            P(),
        ),
        out_specs=(P(("wide", "narrow"), None, None, None), P(), P(), P(), P(), P(), P(), P(), P()),
        check_vma=False,
    )
```

```python
import functools

import jax
import jax.numpy as jnp
from jax import lax
from jax.experimental import pallas as pl
from jax.experimental.pallas import tpu as pltpu
from jax.sharding import PartitionSpec as P

epsilon = 1e-06
gelu_root = 0.7978845608028654
gelu_cubic = 0.044715

C = 400
CP = 512
HID = 1600
TE = 16
CELLS = 512
GROUPS = 4
HT = 13
PITCH = 32
ROWS = HT * C + 16
PIECES = ((0, 1024, 8 * C), (1024, 576, 5 * C + 16))
EXTRA = 272
SIZES = (1856, 1856, 1504)
AXES = ("wide", "narrow")
SLOT_ROWS = 3 * 72 + 16
SIDE_ROWS = 2 * SLOT_ROWS
f32 = jnp.float32
bf16 = jnp.bfloat16
VMEM = pl.BlockSpec(memory_space=pltpu.VMEM)
SMEM = pl.BlockSpec(memory_space=pltpu.SMEM)
HBM = pl.BlockSpec(memory_space=pltpu.HBM)


def group_width(g):
    return min(128, C - 128 * g)


def lanes(g):
    return slice(128 * g, 128 * g + group_width(g))


def land_mask(land, tiles=2):
    spread = jnp.broadcast_to(land.astype(f32)[:, :, None], (tiles * TE, TE, C))
    return spread.reshape(tiles * TE * TE, C)


def zero_lanes(ref):
    ref[...] = jnp.zeros(ref.shape, ref.dtype)


def pack_narrow(tile_rows, even, first_ref, second_ref):
    for ref in (first_ref, second_ref):
        zero_lanes(ref)
    for s in range(2):
        north = tile_rows(s, 0)
        south = tile_rows(s, TE - 3)
        first_ref[s, :, 0:C] = jnp.where(even, south, north).astype(bf16)
        second_ref[s, :, 0:C] = jnp.where(even, north, south).astype(bf16)


def narrow_kernel(field_ref, land_ref, first_ref, second_ref, held_ref, cells_ref, sems):
    copies = [
        pltpu.make_async_copy(field_ref, held_ref, sems.at[0]),
        pltpu.make_async_copy(land_ref, cells_ref, sems.at[1]),
    ]
    for copy in copies:
        copy.start()
    for copy in copies:
        copy.wait()

    def tile_rows(s, row):
        cells = held_ref[s, row : row + 3].reshape(3 * TE, C).astype(f32)
        land = cells_ref[s, row : row + 3].astype(f32)
        return cells * jnp.broadcast_to(land[:, :, None], (3, TE, C)).reshape(3 * TE, C)

    pack_narrow(tile_rows, lax.axis_index("narrow") % 2 == 0, first_ref, second_ref)


def wide_kernel(masked, *refs):
    if masked:
        tiles_ref, mask_ref, n1_ref, n2_ref, first_ref, second_ref, m_ref, r_ref, o_ref, q_ref = refs
    else:
        tiles_ref, n1_ref, n2_ref, first_ref, second_ref, m_ref, r_ref, o_ref, q_ref = refs
    n_even = lax.axis_index("narrow") % 2 == 0
    w_even = lax.axis_index("wide") % 2 == 0
    zero_lanes(o_ref)
    for s in range(2):
        cells = tiles_ref[s].reshape(TE * TE, C).astype(f32)
        if masked:
            cells = cells * mask_ref[s * TE * TE : (s + 1) * TE * TE, :]
        one = n1_ref[s].astype(f32)
        two = n2_ref[s].astype(f32)
        from_north = jnp.where(n_even, two, one)
        from_south = jnp.where(n_even, one, two)
        for g in range(GROUPS):
            m_ref[s, g, :, 0 : group_width(g)] = cells[:, lanes(g)]
            r_ref[0, s, g] = from_north[:, 128 * g : 128 * g + 128]
            r_ref[1, s, g] = from_south[:, 128 * g : 128 * g + 128]
    for s in range(2):
        for g in range(GROUPS):
            w = group_width(g)
            for side in range(2):
                for c in range(3):
                    col = c + side * (TE - 3)
                    at = c * 22
                    o_ref[side, s, g, at : at + 3, :] = r_ref[0, s, g, pl.ds(col, 3, stride=TE), :]
                    o_ref[side, s, g, at + 3 : at + 19, 0:w] = m_ref[s, g, pl.ds(col, TE, stride=TE), 0:w]
                    o_ref[side, s, g, at + 19 : at + 22, :] = r_ref[1, s, g, pl.ds(col, 3, stride=TE), :]
            west = o_ref[0, s, g, 0:72, :]
            east = o_ref[1, s, g, 0:72, :]
            at = s * SLOT_ROWS + g * 72
            for k, value in enumerate((jnp.where(w_even, east, west), jnp.where(w_even, west, east))):
                if g < GROUPS - 1:
                    q_ref[k, at : at + 72, :] = value
                else:
                    blocks = [value[8 * j : 8 * j + 8, 0:16] for j in range(9)]
                    q_ref[k, at : at + 8, :] = jnp.concatenate(blocks[0:8], axis=1)
                    q_ref[k, at + 8 : at + 16, :] = jnp.concatenate(
                        [blocks[8], jnp.zeros((8, 112), f32)], axis=1
                    )
    first_ref[...] = q_ref[0].astype(bf16)
    second_ref[...] = q_ref[1].astype(bf16)


def place_centre(cells, s, p_ref):
    for g in range(GROUPS):
        for r in range(TE):
            at = (r + 3) * PITCH + 8
            p_ref[s, g, at : at + TE, :] = cells[r * TE : (r + 1) * TE, 128 * g : 128 * g + 128]


def padded_lanes(cells):
    return jnp.concatenate([cells, jnp.zeros((cells.shape[0], CP - C), cells.dtype)], axis=1)


def place_rows(n1_ref, n2_ref, rn_ref):
    n_even = lax.axis_index("narrow") % 2 == 0
    for s in range(2):
        one = n1_ref[s].astype(f32)
        two = n2_ref[s].astype(f32)
        north = jnp.where(n_even, two, one)
        south = jnp.where(n_even, one, two)
        for g in range(GROUPS):
            at = slice(128 * g, 128 * g + 128)
            rn_ref[0, s, g] = north[:, at]
            rn_ref[1, s, g] = south[:, at]


def place_columns(w1_ref, w2_ref, rw_ref):
    w_even = lax.axis_index("wide") % 2 == 0
    one = w1_ref[...].astype(f32)
    two = w2_ref[...].astype(f32)
    for side, value in enumerate((jnp.where(w_even, two, one), jnp.where(w_even, one, two))):
        for s in range(2):
            for g in range(GROUPS):
                at = s * SLOT_ROWS + g * 72
                if g < GROUPS - 1:
                    rw_ref[side, s, g, 0:72, :] = value[at : at + 72]
                else:
                    for j in range(9):
                        rows = value[at : at + 8] if j < 8 else value[at + 8 : at + 16]
                        lane = 16 * j % 128
                        block = jnp.concatenate(
                            [rows[:, lane : lane + 16], jnp.zeros((8, 112), f32)], axis=1
                        )
                        rw_ref[side, s, g, 8 * j : 8 * j + 8, :] = block


def entry_of(neighbours_ref, t, d):
    e = neighbours_ref[t, d]
    near = jnp.maximum(e, 0)
    return e >= 0, near // 2, near % 2


def chosen(options, present):
    value = options[-1][1]
    for test, other in reversed(options[:-1]):
        value = jnp.where(test, other, value)
    return jnp.where(present, value, 0.0)


def here():
    return lax.axis_index("wide") * lax.axis_size("narrow") + lax.axis_index("narrow")


def border_rows(neighbours_ref, p_ref, rn_ref, t, g):
    for d in range(2):
        present, device, slot = entry_of(neighbours_ref, t, d)
        from_row = 3 + TE - 3 if d == 0 else 3
        to_row = 0 if d == 0 else 3 + TE
        for i in range(3):
            own = p_ref[slot, g, pl.ds((from_row + i) * PITCH + 8, TE), :]
            other = rn_ref[d, slot, g, pl.ds(i * TE, TE), :]
            p_ref[t, g, pl.ds((to_row + i) * PITCH + 8, TE), :] = chosen(
                [(device == here(), own), (None, other)], present
            )


def border_columns(neighbours_ref, p_ref, rn_ref, rw_ref, t, g, put):
    narrow = lax.axis_size("narrow")
    for d in range(2):
        present, device, slot = entry_of(neighbours_ref, t, 2 + d)
        from_col = 8 + TE - 3 if d == 0 else 8
        for c in range(3):
            own = p_ref[slot, g, pl.ds(3 * PITCH + from_col + c, TE, stride=PITCH), :]
            other = rw_ref[d, slot, g, pl.ds(c * 22 + 3, TE), :]
            put(d, c, 3, TE, chosen([(device == here(), own), (None, other)], present))
    for d in range(4):
        south, east = d // 2, d % 2
        present, device, slot = entry_of(neighbours_ref, t, 4 + d)
        same_w = device // narrow == lax.axis_index("wide")
        same_n = device % narrow == lax.axis_index("narrow")
        from_row = 3 if south else 3 + TE - 3
        to_row = 3 + TE if south else 0
        from_col = 8 if east else 8 + TE - 3
        for c in range(3):
            own = p_ref[slot, g, pl.ds(from_row * PITCH + from_col + c, 3, stride=PITCH), :]
            beyond = rn_ref[south, slot, g, pl.ds(from_col - 8 + c, 3, stride=TE), :]
            beside = rw_ref[east, slot, g, pl.ds(c * 22 + from_row, 3), :]
            across = rw_ref[east, slot, g, pl.ds(c * 22 + (19 if south else 0), 3), :]
            put(
                east,
                c,
                to_row,
                3,
                chosen(
                    [(device == here(), own), (same_w, beyond), (same_n, beside), (None, across)], present
                ),
            )


def column_in(p_ref, t, g):
    def put(side, c, row, count, value):
        at = row * PITCH + (8 + TE if side else 5) + c
        p_ref[t, g, pl.ds(at, count, stride=PITCH), :] = value

    return put


def each_group(body, tiles=(0, 1)):
    def step(i, _):
        body(tiles[0] + i // GROUPS, i % GROUPS)
        return _

    lax.fori_loop(0, len(tiles) * GROUPS, step, 0)


def weight_rows(weight_ref, g, taps):
    at = pl.ds(pl.multiple_of(g * 128, 128), 128)
    return [jnp.broadcast_to(weight_ref[pl.ds(k, 1), at], (8, 128)) for k in taps]


def convolve(p_ref, weight_ref, start, finish, flip, tiles=(0, 1)):
    def body(t, g):
        for h in range(2):
            total = start(t, g, h)
            for b in range(7):
                taps = [48 - (7 * a + b) if flip else 7 * a + b for a in range(7)]
                weights = weight_rows(weight_ref, g, taps)
                for row in range(22):
                    x = p_ref[t, g, pl.ds(row * PITCH + 5 + b + 8 * h, 8), :]
                    for a in range(7):
                        r = row - a
                        if 0 <= r < TE:
                            total[r] = total[r] + weights[a] * x
            finish(t, g, h, total)

    each_group(body, tiles)


def gelu_pair(hidden):
    square = hidden * hidden
    bent = jnp.tanh(gelu_root * hidden * (1.0 + gelu_cubic * square))
    half = 0.5 * (1.0 + bent)
    slope = half + 0.5 * hidden * (1.0 - bent * bent) * (gelu_root * (1.0 + 3.0 * gelu_cubic * square))
    return hidden * half, slope


def take_weights(weight_ref, depth_weight_ref):
    weight_ref[...] = jnp.zeros(weight_ref.shape, f32)
    weight_ref[0:49, 0:C] = depth_weight_ref[...]


def hold_kernel(
    land_ref,
    cot_ref,
    depth_weight_ref,
    depth_bias_ref,
    gain_ref,
    shift_ref,
    up_bias_ref,
    up_ref,
    down_ref,
    mask_ref,
    gated_ref,
    gated_t_ref,
    down_bias_ref,
    up_out_ref,
    down_out_ref,
    taps_ref,
    small_ref,
    cot_in_ref,
    bias_in_ref,
    gain_in_ref,
    shift_in_ref,
    up_bias_in_ref,
    sems,
):
    pairs = (
        (cot_ref, cot_in_ref),
        (depth_weight_ref, taps_ref),
        (depth_bias_ref, bias_in_ref),
        (gain_ref, gain_in_ref),
        (shift_ref, shift_in_ref),
        (up_bias_ref, up_bias_in_ref),
        (up_ref, up_out_ref),
        (down_ref, down_out_ref),
    )
    copies = [pltpu.make_async_copy(a, b, sems.at[k]) for k, (a, b) in enumerate(pairs)]
    for copy in copies:
        copy.start()
    mask_ref[...] = land_mask(land_ref[...].reshape(2 * TE, TE))
    copies[0].wait()
    gated = cot_in_ref[...].reshape(CELLS, C).astype(f32) * mask_ref[...]
    gated_ref[...] = padded_lanes(gated).astype(bf16)
    gated_t_ref[...] = gated_ref[...].T
    down_bias_ref[...] = jnp.sum(gated, axis=0, keepdims=True)
    for copy in copies[1:]:
        copy.wait()
    small_ref[0:1, 0:C] = bias_in_ref[...].reshape(1, C)
    small_ref[1:2, 0:C] = gain_in_ref[...].reshape(1, C)
    small_ref[2:3, 0:C] = shift_in_ref[...].reshape(1, C)
    small_ref[3:4, :] = up_bias_in_ref[...].reshape(1, HID)


def prep_kernel(
    beside_ref,
    field_ref,
    mask_ref,
    n1_ref,
    n2_ref,
    taps_ref,
    small_ref,
    p_ref,
    y_ref,
    rn_ref,
    weight_ref,
    neighbours_ref,
    sem,
):
    copy = pltpu.make_async_copy(beside_ref, neighbours_ref, sem)
    copy.start()
    p_ref[...] = jnp.zeros(p_ref.shape, f32)
    for s in range(2):
        cells = field_ref[s].reshape(TE * TE, C).astype(f32)
        place_centre(padded_lanes(cells * mask_ref[s * TE * TE : (s + 1) * TE * TE, :]), s, p_ref)
    place_rows(n1_ref, n2_ref, rn_ref)
    take_weights(weight_ref, taps_ref)
    weight_ref[49:50, 0:C] = small_ref[0:1, 0:C]
    copy.wait()
    each_group(lambda t, g: border_rows(neighbours_ref, p_ref, rn_ref, t, g))

    def start(t, g, h):
        return weight_rows(weight_ref, g, [49]) * TE

    def finish(t, g, h, rows):
        for r in range(TE):
            y_ref[t, g, pl.ds(r * TE + 8 * h, 8), :] = rows[r]

    convolve(p_ref, weight_ref, start, finish, False)


def front_kernel(
    beside_ref,
    n1_ref,
    n2_ref,
    w1_ref,
    w2_ref,
    p_ref,
    y_in_ref,
    gated_ref,
    gated_t_ref,
    depth_weight_ref,
    small_ref,
    up_ref,
    down_ref,
    keep_ref,
    send_ref,
    ng_ref,
    up_bias_sum_ref,
    z_ref,
    r_ref,
    border_ref,
    normed_ref,
    normed_t_ref,
    rn_ref,
    rw_ref,
    weight_ref,
    y_ref,
    neighbours_ref,
    sem,
):
    copy = pltpu.make_async_copy(beside_ref, neighbours_ref, sem)
    copy.start()
    place_rows(n1_ref, n2_ref, rn_ref)
    place_columns(w1_ref, w2_ref, rw_ref)
    take_weights(weight_ref, depth_weight_ref)
    y_ref[...] = y_in_ref[...]
    copy.wait()

    def sides(t, g):
        def put(side, c, row, count, value):
            border_ref[t, g, pl.ds((side * 3 + c) * 24 + row, count), :] = value

        border_columns(neighbours_ref, p_ref, rn_ref, rw_ref, t, g, put)
        at = pl.ds(pl.multiple_of(g * 128, 128), 128)
        for side in range(2):
            for out in range(3):
                col = out + side * (TE - 3)
                total = y_ref[t, g, pl.ds(col, TE, stride=TE), :]
                for c in range(3):
                    b = (19 + c if side else c) - col
                    if 0 <= b < 7:
                        for a in range(7):
                            cells = border_ref[t, g, pl.ds((side * 3 + c) * 24 + a, TE), :]
                            total = total + weight_ref[pl.ds(7 * a + b, 1), at] * cells
                y_ref[t, g, pl.ds(col, TE, stride=TE), :] = total

    each_group(sides)

    normed_ref[...] = jnp.zeros(normed_ref.shape, bf16)
    step_rows = 128

    def norm(i, _):
        at = pl.ds(pl.multiple_of(i * step_rows, step_rows), step_rows)
        inside = pl.ds(pl.multiple_of((i % 2) * step_rows, step_rows), step_rows)
        conv = jnp.concatenate([y_ref[i // 2, g, inside, :] for g in range(GROUPS)], axis=1)[:, 0:C]
        mean = jnp.sum(conv, axis=1, keepdims=True) * (1.0 / C)
        dev = conv - mean
        var = jnp.sum(dev * dev, axis=1, keepdims=True) * (1.0 / C)
        rstd = lax.rsqrt(var + epsilon)
        zhat = dev * rstd
        z_ref[at, :] = zhat
        r_ref[at, :] = jnp.broadcast_to(rstd, (step_rows, 128))
        normed_ref[at, 0:C] = (zhat * small_ref[1:2, 0:C] + small_ref[2:3, 0:C]).astype(bf16)
        return _

    lax.fori_loop(0, CELLS // step_rows, norm, 0)
    normed_t_ref[...] = normed_ref[...].T

    hidden(
        0,
        normed_ref,
        normed_t_ref,
        gated_ref,
        gated_t_ref,
        small_ref,
        up_ref,
        down_ref,
        keep_ref,
        send_ref,
        ng_ref,
        up_bias_sum_ref,
    )


def hidden(
    piece,
    normed_ref,
    normed_t_ref,
    gated_ref,
    gated_t_ref,
    small_ref,
    up_ref,
    down_ref,
    keep_ref,
    send_ref,
    ng_ref,
    up_bias_sum_ref,
):
    core0 = lax.axis_index("narrow") % 2 == 0
    first, count, rows = PIECES[piece]
    used = (count + 127) // 128 * C
    if used < rows:
        keep_ref[used:, :] = jnp.zeros((rows - used, 128), f32)
        send_ref[used:, :] = jnp.zeros((rows - used, 128), bf16)

    def products(lo, width):
        at = slice(first + lo, first + lo + width)
        h = jnp.dot(normed_ref[:, 0:C], up_ref[:, at], preferred_element_type=f32) + small_ref[3:4, at]
        ag = jnp.dot(gated_ref[:, 0:C], down_ref[:, at], preferred_element_type=f32)
        return h, ag

    def gradients(lo, width, h, ag):
        at = slice(first + lo, first + lo + width)
        act, slope = gelu_pair(h)
        hg = ag * slope
        hgb = hg.astype(bf16)
        dg = jnp.dot(gated_t_ref[0:C, :], act.astype(bf16), preferred_element_type=f32)
        ug = jnp.dot(normed_t_ref[0:C, :], hgb, preferred_element_type=f32)
        ng = lax.dot_general(hgb, up_ref[:, at], (((1,), (1,)), ((), ())), preferred_element_type=f32)
        if lo == 0:
            ng_ref[...] = ng
        else:
            ng_ref[...] += ng
        up_bias_sum_ref[:, lo : lo + width] = jnp.sum(hgb.astype(f32), axis=0, keepdims=True)
        keep = jnp.where(core0, ug, dg)
        send = jnp.where(core0, dg, ug).astype(bf16)
        for k in range((width + 127) // 128):
            w = min(128, width - 128 * k)
            at = slice((lo // 128 + k) * C, (lo // 128 + k + 1) * C)
            if w < 128:
                keep_ref[at, :] = jnp.zeros((C, 128), f32)
                send_ref[at, :] = jnp.zeros((C, 128), bf16)
            keep_ref[at, 0:w] = keep[:, 128 * k : 128 * k + w]
            send_ref[at, 0:w] = send[:, 128 * k : 128 * k + w]

    cut = 512 if piece == 0 else 256
    chunks = ((0, cut), (cut, count - cut))
    ready = products(*chunks[0])
    for i, chunk in enumerate(chunks):
        current = ready
        if i + 1 < len(chunks):
            ready = products(*chunks[i + 1])
        gradients(*chunk, *current)


def grad_kernel(
    ng0_ref,
    ng1_ref,
    z_ref,
    r_ref,
    small_ref,
    cg_ref,
    g1_ref,
    g2_ref,
    y_ref,
    sums_ref,
):
    y_ref[...] = jnp.zeros(y_ref.shape, f32)
    step_rows = 128

    def back(i, sums):
        at = pl.ds(pl.multiple_of(i * step_rows, step_rows), step_rows)
        ng = ng0_ref[at, :] + ng1_ref[at, :]
        zhat = z_ref[at, :]
        rstd = r_ref[at, 0:1]
        q = ng * small_ref[1:2, 0:C]
        a = jnp.sum(q, axis=1, keepdims=True) * (1.0 / C)
        b = jnp.sum(q * zhat, axis=1, keepdims=True) * (1.0 / C)
        cg = (rstd * (q - a - zhat * b)).astype(bf16)
        cg_ref[i // 2, pl.ds((i % 2) * 8, 8)] = cg.reshape(8, TE, C)
        wide = cg.astype(f32)
        y_ref[at, 0:C] = wide
        return (
            sums[0] + jnp.sum(ng * zhat, axis=0, keepdims=True),
            sums[1] + jnp.sum(ng, axis=0, keepdims=True),
            sums[2] + jnp.sum(wide, axis=0, keepdims=True),
        )

    zero = jnp.zeros((1, C), f32)
    gain_sum, shift_sum, bias_sum = lax.fori_loop(0, CELLS // step_rows, back, (zero, zero, zero))
    sums_ref[0:1, :] = bias_sum
    sums_ref[1:2, :] = gain_sum
    sums_ref[2:3, :] = shift_sum

    def tile_rows(s, row):
        at = s * TE * TE + row * TE
        return y_ref[at : at + 3 * TE, 0:C]

    pack_narrow(tile_rows, lax.axis_index("narrow") % 2 == 0, g1_ref, g2_ref)

def taps_kernel(
    after_ref, y_ref, p_in_ref, border_ref, sums_ref, ub0_ref, ub1_ref, down_bias_ref, extra_ref, p_ref, dw_ref
):
    p_ref[...] = p_in_ref[...]
    dw_ref[...] = jnp.zeros(dw_ref.shape, f32)

    def taps(t, g):
        put = column_in(p_ref, t, g)
        for side in range(2):
            for c in range(3):
                put(side, c, 0, 22, border_ref[t, g, pl.ds((side * 3 + c) * 24, 22), :])
        for h in range(2):
            cg = [
                y_ref[
                    pl.ds(t * TE * TE + r * TE + 8 * h, 8),
                    pl.ds(pl.multiple_of(g * 128, 128), 128),
                ]
                for r in range(TE)
            ]
            for b in range(7):
                total = [None] * 7
                for row in range(22):
                    x = p_ref[t, g, pl.ds(row * PITCH + 5 + b + 8 * h, 8), :]
                    for a in range(7):
                        r = row - a
                        if 0 <= r < TE:
                            term = x * cg[r]
                            total[a] = term if total[a] is None else total[a] + term
                for a in range(7):
                    dw_ref[g, 7 * a + b] += total[a]

    each_group(taps)

    extra_ref[...] = jnp.zeros(extra_ref.shape, f32)
    for g in range(GROUPS):
        w = group_width(g)
        extra_ref[g * 64 : g * 64 + 49, :] = jnp.sum(dw_ref[g], axis=1)
        extra_ref[g * 64 + 49 : g * 64 + 50, 0:w] = sums_ref[0:1, lanes(g)]
        extra_ref[g * 64 + 50 : g * 64 + 51, 0:w] = sums_ref[1:2, lanes(g)]
        extra_ref[g * 64 + 51 : g * 64 + 52, 0:w] = sums_ref[2:3, lanes(g)]
        extra_ref[g * 64 + 52 : g * 64 + 53, 0:w] = down_bias_ref[:, lanes(g)]
    for (first, count, _), ref in zip(PIECES, (ub0_ref, ub1_ref)):
        for lo in range(0, count, 128):
            w = min(128, count - lo)
            at = 256 + (first + lo) // 128
            extra_ref[at : at + 1, 0:w] = ref[:, lo : lo + w]


def split_kernel(keep0_ref, got0_ref, keep1_ref, got1_ref, after_ref, *refs):
    me = here()
    refs[-1][...] = jnp.zeros((8, 128), f32)
    lo = 0
    for i, size in enumerate(SIZES):
        send_ref, mine_ref = refs[i], refs[len(SIZES) + i]
        high = jnp.where(keeps_high(me, ORDERS[i], 0), 1, 0)
        half = size // 2
        for j in range(2):

            def store(ref, lo=lo):
                first = 0
                for (_, _, rows), keep_ref, got_ref in zip(
                    PIECES, (keep0_ref, keep1_ref), (got0_ref, got1_ref)
                ):
                    at = slice(max(lo - first, 0), min(lo + half - first, rows))
                    if at.start < at.stop:
                        total = keep_ref[at, :] + got_ref[at, :].astype(f32)
                        to = slice(at.start + first - lo, at.stop + first - lo)
                        ref[to, :] = total.astype(ref.dtype)
                    first += rows

            pl.when(high == j)(functools.partial(store, mine_ref))
            pl.when(high != j)(functools.partial(store, send_ref))
            lo += half


def unpack_kernel(mine_ref, theirs_ref, up_ref, down_ref, taps_ref, bias_ref, gain_ref, shift_ref, up_bias_ref, down_bias_ref):
    core0 = lax.axis_index("narrow") % 2 == 0
    for l in range(HT):
        w = min(128, HID - 128 * l)
        rows = slice(l * C, l * C + C)
        one = mine_ref[rows, :].astype(f32)
        two = theirs_ref[rows, :].astype(f32)
        up_ref[:, 128 * l : 128 * l + w] = jnp.where(core0, one, two)[:, 0:w]
        down_ref[:, 128 * l : 128 * l + w] = jnp.where(core0, two, one)[:, 0:w]
    extra = mine_ref[ROWS:, :].astype(f32) + theirs_ref[ROWS:, :].astype(f32)
    for g in range(GROUPS):
        taps_ref[:, lanes(g)] = extra[g * 64 : g * 64 + 49, 0 : group_width(g)]
    for k, ref in enumerate((bias_ref, gain_ref, shift_ref, down_bias_ref)):
        at = 49 + k
        vector = jnp.concatenate([extra[g * 64 + at : g * 64 + at + 1] for g in range(GROUPS)], axis=1)
        ref[...] = vector[:, 0:C].reshape(C)
    vector = jnp.concatenate([extra[256 + l : 257 + l] for l in range(HT)], axis=1)
    up_bias_ref[...] = vector[:, 0:HID].reshape(HID)


def back_tile(t, p_ref, weight_ref, y_ref, tile_ref, gated_ref, mask_ref, out_ref, sem):
    at = slice(t * TE * TE, (t + 1) * TE * TE)
    y_ref[...] = gated_ref[at, :].astype(f32)

    def place(g, h, r):
        return (pl.ds(r * TE + 8 * h, 8), pl.ds(pl.multiple_of(g * 128, 128), 128))

    def start(t, g, h):
        return [y_ref[place(g, h, r)] for r in range(TE)]

    def finish(t, g, h, rows):
        for r in range(TE):
            y_ref[place(g, h, r)] = rows[r]

    convolve(p_ref, weight_ref, start, finish, True, (t,))
    tile_ref[...] = (y_ref[:, 0:C] * mask_ref[at, :]).astype(bf16).reshape(TE, TE, C)
    copy = pltpu.make_async_copy(tile_ref, out_ref.at[t], sem)
    copy.start()
    copy.wait()


def back_first_kernel(
    beside_ref,
    cg_ref,
    mask_ref,
    gated_ref,
    n1_ref,
    n2_ref,
    w1_ref,
    w2_ref,
    taps_ref,
    out_ref,
    p_ref,
    rn_ref,
    rw_ref,
    weight_ref,
    y_ref,
    tile_ref,
    neighbours_ref,
    sem,
):
    copy = pltpu.make_async_copy(beside_ref, neighbours_ref, sem)
    copy.start()
    for s in range(2):
        place_centre(padded_lanes(cg_ref[s].reshape(TE * TE, C).astype(f32)), s, p_ref)
    place_rows(n1_ref, n2_ref, rn_ref)
    place_columns(w1_ref, w2_ref, rw_ref)
    take_weights(weight_ref, taps_ref)
    copy.wait()

    def borders(t, g):
        border_rows(neighbours_ref, p_ref, rn_ref, t, g)
        border_columns(neighbours_ref, p_ref, rn_ref, rw_ref, t, g, column_in(p_ref, t, g))

    each_group(borders)
    back_tile(0, p_ref, weight_ref, y_ref, tile_ref, gated_ref, mask_ref, out_ref, sem)


def back_second_kernel(
    p_ref, mask_ref, gated_ref, taps_ref, before_ref, out_ref, weight_ref, y_ref, tile_ref, sem
):
    take_weights(weight_ref, taps_ref)
    back_tile(1, p_ref, weight_ref, y_ref, tile_ref, gated_ref, mask_ref, out_ref, sem)


def params(size=16):
    return pltpu.CompilerParams(vmem_limit_bytes=size * 1024 * 1024)


def estimate():
    return pl.CostEstimate(flops=10**9, bytes_accessed=16 * 10**6, transcendentals=0)


NEIGHBOURS = pltpu.SMEM((2, 8), jnp.int32)
P_SCRATCH = pltpu.VMEM((2, GROUPS, 22 * PITCH, 128), f32)
RN_SCRATCH = pltpu.VMEM((2, 2, GROUPS, 48, 128), f32)
RW_SCRATCH = pltpu.VMEM((2, 2, GROUPS, 80, 128), f32)
W_SCRATCH = pltpu.VMEM((56, CP), f32)
Y_SCRATCH = pltpu.VMEM((CELLS, CP), f32)


def swap_pairs(kind):
    axis, offset = kind
    pairs = []
    for w in range(32):
        for n in range(4):
            if axis == "narrow":
                up = (n - offset) % 2 == 0
                other = (w, (n + (1 if up else -1)) % 4)
            else:
                up = (w - offset) % 2 == 0
                other = ((w + (1 if up else -1)) % 32, n)
            pairs.append((w * 4 + n, other[0] * 4 + other[1]))
    return pairs


def swap(x, kind):
    return lax.ppermute(x, AXES, swap_pairs(kind))


def flip(x, mask):
    return lax.ppermute(x, AXES, [(i, i ^ mask) for i in range(128)])


STAGES = {
    "x1": (2, (1, 6)),
    "x2": (66, (6,)),
    "z1": (4, (2, 3)),
    "z2": (12, (3,)),
    "y1": (16, (4, 5)),
    "y2": (48, (5,)),
}
ORDERS = (
    ("x1", "y1", "z1", "x2", "y2", "z2"),
    ("y1", "z1", "x1", "y2", "z2", "x2"),
    ("z1", "x1", "y1", "z2", "x2", "y2"),
)
DEPTH = 2


def parity(me, bits):
    return sum((me >> bit) & 1 for bit in bits) & 1


def exchange(x, order, stage):
    masks = [STAGES[order[(stage + 3 * core) % 6]][0] for core in range(2)]
    return lax.ppermute(x, AXES, [(i, i ^ masks[i & 1]) for i in range(128)])


def keeps_high(me, order, stage):
    zero, one = (parity(me, STAGES[order[(stage + 3 * core) % 6]][1]) for core in range(2))
    return jnp.where(me % 2 == 0, zero, one) == 1


def halved(part, order, stage, high):
    half = part.shape[0] // 2
    low_rows, high_rows = part[0:half], part[half:]
    send = jnp.where(high, low_rows, high_rows).astype(bf16)
    keep = jnp.where(high, high_rows, low_rows)
    return keep + exchange(send, order, stage).astype(f32)


def doubled(part, order, stage):
    mine = part.astype(bf16)
    return mine.astype(f32) + exchange(mine, order, stage).astype(f32)


def joined(part, order, stage, high):
    got = exchange(part, order, stage)
    return jnp.concatenate([jnp.where(high, got, part), jnp.where(high, part, got)], axis=0)


def together(*values):
    return lax.optimization_barrier(values)


def local(
    field,
    cotangent,
    land,
    neighbours,
    depth_weight,
    depth_bias,
    ln_gain,
    ln_shift,
    up_weight,
    up_bias,
    down_weight,
):
    me = here()
    shape = jax.ShapeDtypeStruct
    stay = lambda v: pltpu.with_memory_space_constraint(v, pltpu.HBM)
    high = [[keeps_high(me, order, stage) for stage in range(DEPTH)] for order in ORDERS]
    high, field = together(high, field)
    neighbours = stay(neighbours)
    narrow_shape = shape((2, 48, CP), bf16)
    wide_shape = shape((SIDE_ROWS, 128), bf16)
    wide_scratch = [
        pltpu.VMEM((2, GROUPS, TE * TE, 128), f32),
        RN_SCRATCH,
        RW_SCRATCH,
        pltpu.VMEM((2, SIDE_ROWS, 128), f32),
    ]
    p_shape = shape((2, GROUPS, 22 * PITCH, 128), f32)

    s1, s2, field, land = pl.pallas_call(
        narrow_kernel,
        out_shape=(
            narrow_shape,
            narrow_shape,
            shape((2, TE, TE, C), bf16),
            shape((2, TE, TE), jnp.int32),
        ),
        in_specs=[HBM] * 2,
        out_specs=(VMEM,) * 4,
        scratch_shapes=[pltpu.SemaphoreType.DMA((2,))],
        compiler_params=params(4),
        name="pack_rows",
    )(stay(field), stay(land))
    n1, n2 = swap(s1, ("narrow", 0)), swap(s2, ("narrow", 1))
    mask, gated, gated_t, down_bias_sum, up_held, down_held, taps, small = pl.pallas_call(
        hold_kernel,
        out_shape=(
            shape((CELLS, C), f32),
            shape((CELLS, CP), bf16),
            shape((CP, CELLS), bf16),
            shape((1, C), f32),
            shape((C, HID), bf16),
            shape((C, HID), bf16),
            shape((49, C), f32),
            shape((4, HID), f32),
        ),
        in_specs=[VMEM] + [HBM] * 8,
        out_specs=(VMEM,) * 8,
        scratch_shapes=[
            pltpu.VMEM((2, TE, TE, C), bf16),
            pltpu.VMEM((C,), f32),
            pltpu.VMEM((C,), f32),
            pltpu.VMEM((C,), f32),
            pltpu.VMEM((HID,), f32),
            pltpu.SemaphoreType.DMA((8,)),
        ],
        compiler_params=params(8),
        cost_estimate=estimate(),
        name="hold",
    )(
        land,
        stay(cotangent),
        stay(depth_weight),
        stay(depth_bias),
        stay(ln_gain),
        stay(ln_shift),
        stay(up_bias),
        stay(up_weight),
        stay(down_weight.T),
    )
    s1, s2 = pl.pallas_call(
        functools.partial(wide_kernel, True),
        out_shape=(wide_shape, wide_shape),
        in_specs=[VMEM] * 4,
        out_specs=(VMEM, VMEM),
        scratch_shapes=wide_scratch,
        compiler_params=params(8),
        name="pack_columns",
    )(field, mask, n1, n2)
    s1, s2, n1, n2 = together(s1, s2, n1, n2)
    w2, w1 = swap(s2, ("wide", 1)), swap(s1, ("wide", 0))
    p, y = pl.pallas_call(
        prep_kernel,
        out_shape=(p_shape, shape((2, GROUPS, TE * TE, 128), f32)),
        in_specs=[HBM] + [VMEM] * 6,
        out_specs=(VMEM,) * 2,
        scratch_shapes=[RN_SCRATCH, W_SCRATCH, NEIGHBOURS, pltpu.SemaphoreType.DMA],
        compiler_params=params(8),
        cost_estimate=estimate(),
        name="prep",
    )(neighbours, field, mask, n1, n2, taps, small)

    def piece_shapes(piece):
        _, count, rows = PIECES[piece]
        return (
            shape((rows, 128), f32),
            shape((rows, 128), bf16),
            shape((CELLS, C), f32),
            shape((1, count), f32),
        )

    keep0, send0, ng0, ub0, z, r, border, normed, normed_t = pl.pallas_call(
        front_kernel,
        out_shape=piece_shapes(0)
        + (
            shape((CELLS, C), f32),
            shape((CELLS, 128), f32),
            shape((2, GROUPS, 6 * 24, 128), f32),
            shape((CELLS, CP), bf16),
            shape((CP, CELLS), bf16),
        ),
        in_specs=[HBM] + [VMEM] * 12,
        out_specs=(VMEM,) * 9,
        scratch_shapes=[
            RN_SCRATCH,
            RW_SCRATCH,
            W_SCRATCH,
            pltpu.VMEM((2, GROUPS, TE * TE, 128), f32),
            NEIGHBOURS,
            pltpu.SemaphoreType.DMA,
        ],
        compiler_params=params(14),
        name="front",
    )(
        neighbours,
        n1,
        n2,
        w1,
        w2,
        p,
        y,
        gated,
        gated_t,
        taps,
        small,
        up_held,
        down_held,
    )
    got0 = flip(send0, 1)
    keep1, send1, ng1, ub1 = pl.pallas_call(
        functools.partial(hidden, 1),
        out_shape=piece_shapes(1),
        in_specs=[VMEM] * 7,
        out_specs=(VMEM,) * 4,
        compiler_params=params(12),
        cost_estimate=estimate(),
        name="hidden",
    )(normed, normed_t, gated, gated_t, small, up_held, down_held)
    got1 = flip(send1, 1)
    cg, g1, g2, cg_wide, sums = pl.pallas_call(
        grad_kernel,
        out_shape=(
            shape((2, TE, TE, C), bf16),
            narrow_shape,
            narrow_shape,
            shape((CELLS, CP), f32),
            shape((3, C), f32),
        ),
        in_specs=[VMEM] * 5,
        out_specs=(VMEM,) * 5,
        compiler_params=params(4),
        cost_estimate=estimate(),
        name="grad",
    )(ng0, ng1, z, r, small)

    halves = [size // 2 for size in SIZES]
    pieces = pl.pallas_call(
        split_kernel,
        out_shape=tuple(shape((half, 128), bf16) for half in halves)
        + tuple(shape((half, 128), f32) for half in halves)
        + (shape((8, 128), f32),),
        in_specs=[VMEM] * 5,
        out_specs=(VMEM,) * (2 * len(SIZES) + 1),
        compiler_params=params(4),
        name="split",
    )(keep0, got0, keep1, got1, sums)

    orders = list(enumerate(ORDERS))
    got = [exchange(pieces[i], order, 0) for i, order in orders]
    n1, n2 = swap(g1, ("narrow", 0)), swap(g2, ("narrow", 1))
    extra = pl.pallas_call(
        taps_kernel,
        out_shape=shape((EXTRA, 128), f32),
        in_specs=[VMEM] * 8,
        out_specs=VMEM,
        scratch_shapes=[
            pltpu.VMEM(p_shape.shape, f32),
            pltpu.VMEM((GROUPS, 49, 8, 128), f32),
        ],
        compiler_params=params(8),
        cost_estimate=estimate(),
        name="taps",
    )(pieces[-1], cg_wide, p, border, sums, ub0, ub1, down_bias_sum)
    parts = [pieces[len(SIZES) + i] + got[i].astype(f32) for i, order in orders]
    parts[-1] = jnp.concatenate([parts[-1], extra], axis=0)
    parts, n1, n2 = together(parts, n1, n2)
    s1, s2 = pl.pallas_call(
        functools.partial(wide_kernel, False),
        out_shape=(wide_shape, wide_shape),
        in_specs=[VMEM] * 3,
        out_specs=(VMEM, VMEM),
        scratch_shapes=wide_scratch,
        compiler_params=params(8),
        name="pack_columns_back",
    )(cg, n1, n2)
    for stage in range(1, DEPTH):
        parts = [halved(parts[i], order, stage, high[i][stage]) for i, order in orders]
    w1, w2 = swap(s1, ("wide", 0)), swap(s2, ("wide", 1))
    for stage in range(DEPTH, 6):
        parts = [doubled(parts[i], order, stage) for i, order in orders]
        if stage == 4:
            parts[-1], w1, w2 = together(parts[-1], w1, w2)
    parts = [part.astype(bf16) for part in parts]
    for stage in reversed(range(1, DEPTH)):
        parts = [joined(parts[i], order, stage, high[i][stage]) for i, order in orders]
    parts[-1], w1, w2 = together(parts[-1], w1, w2)

    tile_scratch = [
        W_SCRATCH,
        pltpu.VMEM((TE * TE, CP), f32),
        pltpu.VMEM((TE, TE, C), bf16),
    ]
    field_grad, grad_p = pl.pallas_call(
        back_first_kernel,
        out_shape=(shape((2, TE, TE, C), bf16), p_shape),
        in_specs=[HBM] + [VMEM] * 8,
        out_specs=(HBM, VMEM),
        scratch_shapes=[RN_SCRATCH, RW_SCRATCH]
        + tile_scratch
        + [NEIGHBOURS, pltpu.SemaphoreType.DMA],
        compiler_params=params(8),
        cost_estimate=estimate(),
        name="back_first",
    )(neighbours, cg, mask, gated, n1, n2, w1, w2, taps)
    matrix = [joined(parts[i], order, 0, high[i][0]) for i, order in orders[:-1]]
    last = parts[-1]
    order = ORDERS[-1]
    got = exchange(last, order, 0)
    one, two = last[0 : halves[-1]], got[0 : halves[-1]]
    upper = high[-1][0]
    extra = (last[halves[-1] :].astype(f32) + got[halves[-1] :].astype(f32)).astype(bf16)
    mine = jnp.concatenate(
        matrix + [jnp.where(upper, two, one), jnp.where(upper, one, two), extra], axis=0
    )
    mine, field_grad = together(mine, field_grad)
    theirs = flip(mine, 1)
    field_grad = pl.pallas_call(
        back_second_kernel,
        out_shape=shape((2, TE, TE, C), bf16),
        in_specs=[VMEM] * 4 + [HBM],
        out_specs=HBM,
        scratch_shapes=tile_scratch + [pltpu.SemaphoreType.DMA],
        input_output_aliases={4: 0},
        compiler_params=params(8),
        cost_estimate=estimate(),
        name="back_second",
    )(grad_p, mask, gated, taps, field_grad)
    theirs, field_grad = together(theirs, field_grad)
    up_grad, down_grad, *rest = pl.pallas_call(
        unpack_kernel,
        out_shape=(
            shape((C, HID), f32),
            shape((C, HID), f32),
            shape((49, C), f32),
            shape((C,), f32),
            shape((C,), f32),
            shape((C,), f32),
            shape((HID,), f32),
            shape((C,), f32),
        ),
        in_specs=[VMEM] * 2,
        out_specs=(VMEM,) * 8,
        compiler_params=params(12),
        name="unpack",
    )(mine, theirs)
    depth_grad, depth_bias_grad, gain_grad, shift_grad, up_bias_grad, down_bias_grad = rest
    return (
        field_grad,
        depth_grad,
        depth_bias_grad,
        gain_grad,
        shift_grad,
        up_grad,
        up_bias_grad,
        down_grad.T,
        down_bias_grad,
    )


def solution(mesh):
    return jax.shard_map(
        local,
        mesh=mesh,
        in_specs=(
            P(("wide", "narrow"), None, None, None),
            P(("wide", "narrow"), None, None, None),
            P(("wide", "narrow"), None, None),
            P(("wide", "narrow"), None),
            P(),
            P(),
            P(),
            P(),
            P(),
            P(),
            P(),
        ),
        out_specs=(P(("wide", "narrow"), None, None, None), P(), P(), P(), P(), P(), P(), P(), P()),
        check_vma=False,
    )
```

```python
import functools

import jax
import jax.numpy as jnp
from jax import lax
from jax.experimental import pallas as pl
from jax.experimental.pallas import tpu as pltpu
from jax.sharding import PartitionSpec as P

epsilon = 1e-06
gelu_root = 0.7978845608028654
gelu_cubic = 0.044715

C = 400
CP = 512
HID = 1600
TE = 16
CELLS = 512
GROUPS = 4
HT = 13
PITCH = 32
ROWS = HT * C + 16
PIECES = ((0, 1024, 8 * C), (1024, 576, 5 * C + 16))
EXTRA = 272
SIZES = (1856, 1856, 1504)
AXES = ("wide", "narrow")
SLOT_ROWS = 3 * 72 + 16
SIDE_ROWS = 2 * SLOT_ROWS
f32 = jnp.float32
bf16 = jnp.bfloat16
VMEM = pl.BlockSpec(memory_space=pltpu.VMEM)
SMEM = pl.BlockSpec(memory_space=pltpu.SMEM)
HBM = pl.BlockSpec(memory_space=pltpu.HBM)


def group_width(g):
    return min(128, C - 128 * g)


def lanes(g):
    return slice(128 * g, 128 * g + group_width(g))


def land_mask(land, tiles=2):
    spread = jnp.broadcast_to(land.astype(f32)[:, :, None], (tiles * TE, TE, C))
    return spread.reshape(tiles * TE * TE, C)


def zero_lanes(ref):
    ref[...] = jnp.zeros(ref.shape, ref.dtype)


def pack_narrow(tile_rows, even, first_ref, second_ref):
    for ref in (first_ref, second_ref):
        zero_lanes(ref)
    for s in range(2):
        north = tile_rows(s, 0)
        south = tile_rows(s, TE - 3)
        first_ref[s, :, 0:C] = jnp.where(even, south, north).astype(bf16)
        second_ref[s, :, 0:C] = jnp.where(even, north, south).astype(bf16)


def narrow_kernel(field_ref, land_ref, first_ref, second_ref, held_ref, cells_ref, sems):
    copies = [
        pltpu.make_async_copy(field_ref, held_ref, sems.at[0]),
        pltpu.make_async_copy(land_ref, cells_ref, sems.at[1]),
    ]
    for copy in copies:
        copy.start()
    for copy in copies:
        copy.wait()

    def tile_rows(s, row):
        cells = held_ref[s, row : row + 3].reshape(3 * TE, C).astype(f32)
        land = cells_ref[s, row : row + 3].astype(f32)
        return cells * jnp.broadcast_to(land[:, :, None], (3, TE, C)).reshape(3 * TE, C)

    pack_narrow(tile_rows, lax.axis_index("narrow") % 2 == 0, first_ref, second_ref)


def wide_kernel(masked, *refs):
    if masked:
        tiles_ref, mask_ref, n1_ref, n2_ref, first_ref, second_ref, m_ref, r_ref, o_ref, q_ref = refs
    else:
        tiles_ref, n1_ref, n2_ref, first_ref, second_ref, m_ref, r_ref, o_ref, q_ref = refs
    n_even = lax.axis_index("narrow") % 2 == 0
    w_even = lax.axis_index("wide") % 2 == 0
    zero_lanes(o_ref)
    for s in range(2):
        cells = tiles_ref[s].reshape(TE * TE, C).astype(f32)
        if masked:
            cells = cells * mask_ref[s * TE * TE : (s + 1) * TE * TE, :]
        one = n1_ref[s].astype(f32)
        two = n2_ref[s].astype(f32)
        from_north = jnp.where(n_even, two, one)
        from_south = jnp.where(n_even, one, two)
        for g in range(GROUPS):
            m_ref[s, g, 0 : TE * TE, 0 : group_width(g)] = cells[:, lanes(g)]
            r_ref[0, s, g, 0:48, :] = from_north[:, 128 * g : 128 * g + 128]
            r_ref[1, s, g, 0:48, :] = from_south[:, 128 * g : 128 * g + 128]
    for s in range(2):
        for g in range(GROUPS):
            w = group_width(g)
            for side in range(2):
                for c in range(3):
                    col = c + side * (TE - 3)
                    at = c * 22
                    o_ref[side, s, g, at : at + 3, :] = r_ref[0, s, g, pl.ds(col, 3, stride=TE), :]
                    o_ref[side, s, g, at + 3 : at + 19, 0:w] = m_ref[s, g, pl.ds(col, TE, stride=TE), 0:w]
                    o_ref[side, s, g, at + 19 : at + 22, :] = r_ref[1, s, g, pl.ds(col, 3, stride=TE), :]
            west = o_ref[0, s, g, 0:72, :]
            east = o_ref[1, s, g, 0:72, :]
            at = s * SLOT_ROWS + g * 72
            for k, value in enumerate((jnp.where(w_even, east, west), jnp.where(w_even, west, east))):
                if g < GROUPS - 1:
                    q_ref[k, at : at + 72, :] = value
                else:
                    blocks = [value[8 * j : 8 * j + 8, 0:16] for j in range(9)]
                    q_ref[k, at : at + 8, :] = jnp.concatenate(blocks[0:8], axis=1)
                    q_ref[k, at + 8 : at + 16, :] = jnp.concatenate(
                        [blocks[8], jnp.zeros((8, 112), f32)], axis=1
                    )
    first_ref[...] = q_ref[0].astype(bf16)
    second_ref[...] = q_ref[1].astype(bf16)


def place_centre(cells, s, p_ref):
    for g in range(GROUPS):
        for r in range(TE):
            at = (r + 3) * PITCH + 8
            p_ref[s, g, at : at + TE, :] = cells[r * TE : (r + 1) * TE, 128 * g : 128 * g + 128]


def padded_lanes(cells):
    return jnp.concatenate([cells, jnp.zeros((cells.shape[0], CP - C), cells.dtype)], axis=1)


def place_rows(n1_ref, n2_ref, rn_ref):
    n_even = lax.axis_index("narrow") % 2 == 0
    for s in range(2):
        one = n1_ref[s].astype(f32)
        two = n2_ref[s].astype(f32)
        north = jnp.where(n_even, two, one)
        south = jnp.where(n_even, one, two)
        for g in range(GROUPS):
            at = slice(128 * g, 128 * g + 128)
            rn_ref[0, s, g, 0:48, :] = north[:, at]
            rn_ref[1, s, g, 0:48, :] = south[:, at]


def place_columns(w1_ref, w2_ref, rw_ref):
    w_even = lax.axis_index("wide") % 2 == 0
    one = w1_ref[...].astype(f32)
    two = w2_ref[...].astype(f32)
    for side, value in enumerate((jnp.where(w_even, two, one), jnp.where(w_even, one, two))):
        for s in range(2):
            for g in range(GROUPS):
                at = s * SLOT_ROWS + g * 72
                if g < GROUPS - 1:
                    rw_ref[side, s, g, 0:72, :] = value[at : at + 72]
                else:
                    for j in range(9):
                        rows = value[at : at + 8] if j < 8 else value[at + 8 : at + 16]
                        lane = 16 * j % 128
                        block = jnp.concatenate(
                            [rows[:, lane : lane + 16], jnp.zeros((8, 112), f32)], axis=1
                        )
                        rw_ref[side, s, g, 8 * j : 8 * j + 8, :] = block


def entry_of(neighbours_ref, t, d):
    e = neighbours_ref[t, d]
    near = jnp.maximum(e, 0)
    return e >= 0, near // 2, near % 2


def chosen(options, present):
    value = options[-1][1]
    for test, other in reversed(options[:-1]):
        value = jnp.where(test, other, value)
    return jnp.where(present, value, 0.0)


def here():
    return lax.axis_index("wide") * lax.axis_size("narrow") + lax.axis_index("narrow")


def border_rows(neighbours_ref, p_ref, rn_ref, t, g):
    for d in range(2):
        present, device, slot = entry_of(neighbours_ref, t, d)
        from_row = 3 + TE - 3 if d == 0 else 3
        to_row = 0 if d == 0 else 3 + TE
        for i in range(3):
            own = p_ref[slot, g, pl.ds((from_row + i) * PITCH + 8, TE), :]
            other = rn_ref[d, slot, g, pl.ds(i * TE, TE), :]
            p_ref[t, g, pl.ds((to_row + i) * PITCH + 8, TE), :] = chosen(
                [(device == here(), own), (None, other)], present
            )


def border_columns(neighbours_ref, p_ref, rn_ref, rw_ref, t, g, put):
    narrow = lax.axis_size("narrow")
    for d in range(2):
        present, device, slot = entry_of(neighbours_ref, t, 2 + d)
        from_col = 8 + TE - 3 if d == 0 else 8
        for c in range(3):
            own = p_ref[slot, g, pl.ds(3 * PITCH + from_col + c, TE, stride=PITCH), :]
            other = rw_ref[d, slot, g, pl.ds(c * 22 + 3, TE), :]
            put(d, c, 3, TE, chosen([(device == here(), own), (None, other)], present))
    for d in range(4):
        south, east = d // 2, d % 2
        present, device, slot = entry_of(neighbours_ref, t, 4 + d)
        same_w = device // narrow == lax.axis_index("wide")
        same_n = device % narrow == lax.axis_index("narrow")
        from_row = 3 if south else 3 + TE - 3
        to_row = 3 + TE if south else 0
        from_col = 8 if east else 8 + TE - 3
        for c in range(3):
            own = p_ref[slot, g, pl.ds(from_row * PITCH + from_col + c, 3, stride=PITCH), :]
            beyond = rn_ref[south, slot, g, pl.ds(from_col - 8 + c, 3, stride=TE), :]
            beside = rw_ref[east, slot, g, pl.ds(c * 22 + from_row, 3), :]
            across = rw_ref[east, slot, g, pl.ds(c * 22 + (19 if south else 0), 3), :]
            put(
                east,
                c,
                to_row,
                3,
                chosen(
                    [(device == here(), own), (same_w, beyond), (same_n, beside), (None, across)], present
                ),
            )


def column_in(p_ref, t, g):
    def put(side, c, row, count, value):
        at = row * PITCH + (8 + TE if side else 5) + c
        p_ref[t, g, pl.ds(at, count, stride=PITCH), :] = value

    return put


def each_group(body, tiles=(0, 1)):
    def step(i, _):
        body(tiles[0] + i // GROUPS, i % GROUPS)
        return _

    lax.fori_loop(0, len(tiles) * GROUPS, step, 0)


def weight_rows(weight_ref, g, taps):
    at = pl.ds(pl.multiple_of(g * 128, 128), 128)
    return [jnp.broadcast_to(weight_ref[pl.ds(k, 1), at], (8, 128)) for k in taps]


def convolve(p_ref, weight_ref, start, finish, flip, tiles=(0, 1)):
    def body(t, g):
        for h in range(2):
            total = start(t, g, h)
            for b in range(7):
                taps = [48 - (7 * a + b) if flip else 7 * a + b for a in range(7)]
                weights = weight_rows(weight_ref, g, taps)
                for row in range(22):
                    x = p_ref[t, g, pl.ds(row * PITCH + 5 + b + 8 * h, 8), :]
                    for a in range(7):
                        r = row - a
                        if 0 <= r < TE:
                            total[r] = total[r] + weights[a] * x
            finish(t, g, h, total)

    each_group(body, tiles)


def gelu_pair(hidden):
    square = hidden * hidden
    bent = jnp.tanh(gelu_root * hidden * (1.0 + gelu_cubic * square))
    half = 0.5 * (1.0 + bent)
    slope = half + 0.5 * hidden * (1.0 - bent * bent) * (gelu_root * (1.0 + 3.0 * gelu_cubic * square))
    return hidden * half, slope


def take_weights(weight_ref, depth_weight_ref):
    weight_ref[...] = jnp.zeros(weight_ref.shape, f32)
    weight_ref[0:49, 0:C] = depth_weight_ref[...]


def hold_kernel(
    land_ref,
    cot_ref,
    depth_weight_ref,
    depth_bias_ref,
    gain_ref,
    shift_ref,
    up_bias_ref,
    up_ref,
    down_ref,
    mask_ref,
    gated_ref,
    gated_t_ref,
    down_bias_ref,
    up_out_ref,
    down_out_ref,
    taps_ref,
    small_ref,
    cot_in_ref,
    bias_in_ref,
    gain_in_ref,
    shift_in_ref,
    up_bias_in_ref,
    sems,
):
    pairs = (
        (cot_ref, cot_in_ref),
        (depth_weight_ref, taps_ref),
        (depth_bias_ref, bias_in_ref),
        (gain_ref, gain_in_ref),
        (shift_ref, shift_in_ref),
        (up_bias_ref, up_bias_in_ref),
        (up_ref, up_out_ref),
        (down_ref, down_out_ref),
    )
    copies = [pltpu.make_async_copy(a, b, sems.at[k]) for k, (a, b) in enumerate(pairs)]
    for copy in copies:
        copy.start()
    mask_ref[...] = land_mask(land_ref[...].reshape(2 * TE, TE))
    copies[0].wait()
    gated = cot_in_ref[...].reshape(CELLS, C).astype(f32) * mask_ref[...]
    gated_ref[...] = padded_lanes(gated).astype(bf16)
    gated_t_ref[...] = gated_ref[...].T
    down_bias_ref[...] = jnp.sum(gated, axis=0, keepdims=True)
    for copy in copies[1:]:
        copy.wait()
    small_ref[0:1, 0:C] = bias_in_ref[...].reshape(1, C)
    small_ref[1:2, 0:C] = gain_in_ref[...].reshape(1, C)
    small_ref[2:3, 0:C] = shift_in_ref[...].reshape(1, C)
    small_ref[3:4, :] = up_bias_in_ref[...].reshape(1, HID)


def prep_kernel(
    beside_ref,
    field_ref,
    mask_ref,
    n1_ref,
    n2_ref,
    taps_ref,
    small_ref,
    p_ref,
    y_ref,
    rn_ref,
    weight_ref,
    neighbours_ref,
    sem,
):
    copy = pltpu.make_async_copy(beside_ref, neighbours_ref, sem)
    copy.start()
    p_ref[...] = jnp.zeros(p_ref.shape, f32)
    for s in range(2):
        cells = field_ref[s].reshape(TE * TE, C).astype(f32)
        place_centre(padded_lanes(cells * mask_ref[s * TE * TE : (s + 1) * TE * TE, :]), s, p_ref)
    place_rows(n1_ref, n2_ref, rn_ref)
    take_weights(weight_ref, taps_ref)
    weight_ref[49:50, 0:C] = small_ref[0:1, 0:C]
    copy.wait()
    each_group(lambda t, g: border_rows(neighbours_ref, p_ref, rn_ref, t, g))

    def start(t, g, h):
        return weight_rows(weight_ref, g, [49]) * TE

    def finish(t, g, h, rows):
        for r in range(TE):
            y_ref[t, g, pl.ds(r * TE + 8 * h, 8), :] = rows[r]

    convolve(p_ref, weight_ref, start, finish, False)


def front_kernel(
    beside_ref,
    n1_ref,
    n2_ref,
    w1_ref,
    w2_ref,
    p_ref,
    y_in_ref,
    gated_ref,
    gated_t_ref,
    depth_weight_ref,
    small_ref,
    up_ref,
    down_ref,
    keep_ref,
    send_ref,
    ng_ref,
    up_bias_sum_ref,
    z_ref,
    r_ref,
    border_ref,
    normed_ref,
    normed_t_ref,
    rn_ref,
    rw_ref,
    weight_ref,
    y_ref,
    neighbours_ref,
    sem,
):
    copy = pltpu.make_async_copy(beside_ref, neighbours_ref, sem)
    copy.start()
    place_rows(n1_ref, n2_ref, rn_ref)
    place_columns(w1_ref, w2_ref, rw_ref)
    take_weights(weight_ref, depth_weight_ref)
    y_ref[:, :, 0 : TE * TE, :] = y_in_ref[...]
    copy.wait()

    def sides(t, g):
        def put(side, c, row, count, value):
            border_ref[t, g, pl.ds((side * 3 + c) * 24 + row, count), :] = value

        border_columns(neighbours_ref, p_ref, rn_ref, rw_ref, t, g, put)
        at = pl.ds(pl.multiple_of(g * 128, 128), 128)
        for side in range(2):
            for out in range(3):
                col = out + side * (TE - 3)
                total = y_ref[t, g, pl.ds(col, TE, stride=TE), :]
                for c in range(3):
                    b = (19 + c if side else c) - col
                    if 0 <= b < 7:
                        for a in range(7):
                            cells = border_ref[t, g, pl.ds((side * 3 + c) * 24 + a, TE), :]
                            total = total + weight_ref[pl.ds(7 * a + b, 1), at] * cells
                y_ref[t, g, pl.ds(col, TE, stride=TE), :] = total

    each_group(sides)

    normed_ref[...] = jnp.zeros(normed_ref.shape, bf16)
    step_rows = 128

    def norm(i, _):
        at = pl.ds(pl.multiple_of(i * step_rows, step_rows), step_rows)
        inside = pl.ds(pl.multiple_of((i % 2) * step_rows, step_rows), step_rows)
        conv = jnp.concatenate([y_ref[i // 2, g, inside, :] for g in range(GROUPS)], axis=1)[:, 0:C]
        mean = jnp.sum(conv, axis=1, keepdims=True) * (1.0 / C)
        dev = conv - mean
        var = jnp.sum(dev * dev, axis=1, keepdims=True) * (1.0 / C)
        rstd = lax.rsqrt(var + epsilon)
        zhat = dev * rstd
        z_ref[at, :] = zhat
        r_ref[at, :] = jnp.broadcast_to(rstd, (step_rows, 128))
        normed_ref[at, 0:C] = (zhat * small_ref[1:2, 0:C] + small_ref[2:3, 0:C]).astype(bf16)
        return _

    lax.fori_loop(0, CELLS // step_rows, norm, 0)
    normed_t_ref[...] = normed_ref[...].T

    hidden(
        0,
        normed_ref,
        normed_t_ref,
        gated_ref,
        gated_t_ref,
        small_ref,
        up_ref,
        down_ref,
        keep_ref,
        send_ref,
        ng_ref,
        up_bias_sum_ref,
    )


def hidden(
    piece,
    normed_ref,
    normed_t_ref,
    gated_ref,
    gated_t_ref,
    small_ref,
    up_ref,
    down_ref,
    keep_ref,
    send_ref,
    ng_ref,
    up_bias_sum_ref,
):
    core0 = lax.axis_index("narrow") % 2 == 0
    first, count, rows = PIECES[piece]
    used = (count + 127) // 128 * C
    if used < rows:
        keep_ref[used:, :] = jnp.zeros((rows - used, 128), f32)
        send_ref[used:, :] = jnp.zeros((rows - used, 128), bf16)

    def products(lo, width):
        at = slice(first + lo, first + lo + width)
        h = jnp.dot(normed_ref[:, 0:C], up_ref[:, at], preferred_element_type=f32) + small_ref[3:4, at]
        ag = jnp.dot(gated_ref[:, 0:C], down_ref[:, at], preferred_element_type=f32)
        return h, ag

    def gradients(lo, width, h, ag):
        at = slice(first + lo, first + lo + width)
        act, slope = gelu_pair(h)
        hg = ag * slope
        hgb = hg.astype(bf16)
        dg = jnp.dot(gated_t_ref[0:C, :], act.astype(bf16), preferred_element_type=f32)
        ug = jnp.dot(normed_t_ref[0:C, :], hgb, preferred_element_type=f32)
        ng = lax.dot_general(hgb, up_ref[:, at], (((1,), (1,)), ((), ())), preferred_element_type=f32)
        if lo == 0:
            ng_ref[...] = ng
        else:
            ng_ref[...] += ng
        up_bias_sum_ref[:, lo : lo + width] = jnp.sum(hgb.astype(f32), axis=0, keepdims=True)
        keep = jnp.where(core0, ug, dg)
        send = jnp.where(core0, dg, ug).astype(bf16)
        for k in range((width + 127) // 128):
            w = min(128, width - 128 * k)
            at = slice((lo // 128 + k) * C, (lo // 128 + k + 1) * C)
            if w < 128:
                keep_ref[at, :] = jnp.zeros((C, 128), f32)
                send_ref[at, :] = jnp.zeros((C, 128), bf16)
            keep_ref[at, 0:w] = keep[:, 128 * k : 128 * k + w]
            send_ref[at, 0:w] = send[:, 128 * k : 128 * k + w]

    cut = 512 if piece == 0 else 256
    chunks = ((0, cut), (cut, count - cut))
    ready = products(*chunks[0])
    for i, chunk in enumerate(chunks):
        current = ready
        if i + 1 < len(chunks):
            ready = products(*chunks[i + 1])
        gradients(*chunk, *current)


def grad_kernel(
    ng0_ref,
    ng1_ref,
    z_ref,
    r_ref,
    small_ref,
    cg_ref,
    g1_ref,
    g2_ref,
    y_ref,
    sums_ref,
):
    y_ref[...] = jnp.zeros(y_ref.shape, f32)
    step_rows = 128

    def back(i, sums):
        at = pl.ds(pl.multiple_of(i * step_rows, step_rows), step_rows)
        ng = ng0_ref[at, :] + ng1_ref[at, :]
        zhat = z_ref[at, :]
        rstd = r_ref[at, 0:1]
        q = ng * small_ref[1:2, 0:C]
        a = jnp.sum(q, axis=1, keepdims=True) * (1.0 / C)
        b = jnp.sum(q * zhat, axis=1, keepdims=True) * (1.0 / C)
        cg = (rstd * (q - a - zhat * b)).astype(bf16)
        cg_ref[i // 2, pl.ds((i % 2) * 8, 8)] = cg.reshape(8, TE, C)
        wide = cg.astype(f32)
        y_ref[at, 0:C] = wide
        return (
            sums[0] + jnp.sum(ng * zhat, axis=0, keepdims=True),
            sums[1] + jnp.sum(ng, axis=0, keepdims=True),
            sums[2] + jnp.sum(wide, axis=0, keepdims=True),
        )

    zero = jnp.zeros((1, C), f32)
    gain_sum, shift_sum, bias_sum = lax.fori_loop(0, CELLS // step_rows, back, (zero, zero, zero))
    sums_ref[0:1, :] = bias_sum
    sums_ref[1:2, :] = gain_sum
    sums_ref[2:3, :] = shift_sum

    def tile_rows(s, row):
        at = s * TE * TE + row * TE
        return y_ref[at : at + 3 * TE, 0:C]

    pack_narrow(tile_rows, lax.axis_index("narrow") % 2 == 0, g1_ref, g2_ref)

def taps_kernel(
    after_ref, y_ref, p_in_ref, border_ref, sums_ref, ub0_ref, ub1_ref, down_bias_ref, extra_ref, p_ref, dw_ref
):
    p_ref[...] = p_in_ref[...]
    dw_ref[...] = jnp.zeros(dw_ref.shape, f32)

    def taps(t, g):
        put = column_in(p_ref, t, g)
        for side in range(2):
            for c in range(3):
                put(side, c, 0, 22, border_ref[t, g, pl.ds((side * 3 + c) * 24, 22), :])
        for h in range(2):
            cg = [
                y_ref[
                    pl.ds(t * TE * TE + r * TE + 8 * h, 8),
                    pl.ds(pl.multiple_of(g * 128, 128), 128),
                ]
                for r in range(TE)
            ]
            for b in range(7):
                total = [None] * 7
                for row in range(22):
                    x = p_ref[t, g, pl.ds(row * PITCH + 5 + b + 8 * h, 8), :]
                    for a in range(7):
                        r = row - a
                        if 0 <= r < TE:
                            term = x * cg[r]
                            total[a] = term if total[a] is None else total[a] + term
                for a in range(7):
                    dw_ref[g, 7 * a + b] += total[a]

    each_group(taps)

    extra_ref[...] = jnp.zeros(extra_ref.shape, f32)
    for g in range(GROUPS):
        w = group_width(g)
        extra_ref[g * 64 : g * 64 + 49, :] = jnp.sum(dw_ref[g], axis=1)
        extra_ref[g * 64 + 49 : g * 64 + 50, 0:w] = sums_ref[0:1, lanes(g)]
        extra_ref[g * 64 + 50 : g * 64 + 51, 0:w] = sums_ref[1:2, lanes(g)]
        extra_ref[g * 64 + 51 : g * 64 + 52, 0:w] = sums_ref[2:3, lanes(g)]
        extra_ref[g * 64 + 52 : g * 64 + 53, 0:w] = down_bias_ref[:, lanes(g)]
    for (first, count, _), ref in zip(PIECES, (ub0_ref, ub1_ref)):
        for lo in range(0, count, 128):
            w = min(128, count - lo)
            at = 256 + (first + lo) // 128
            extra_ref[at : at + 1, 0:w] = ref[:, lo : lo + w]


def split_kernel(keep0_ref, got0_ref, keep1_ref, got1_ref, after_ref, *refs):
    me = here()
    refs[-1][...] = jnp.zeros((8, 128), f32)
    lo = 0
    for i, size in enumerate(SIZES):
        send_ref, mine_ref = refs[i], refs[len(SIZES) + i]
        high = jnp.where(keeps_high(me, ORDERS[i], 0), 1, 0)
        half = size // 2
        for j in range(2):

            def store(ref, lo=lo):
                first = 0
                for (_, _, rows), keep_ref, got_ref in zip(
                    PIECES, (keep0_ref, keep1_ref), (got0_ref, got1_ref)
                ):
                    at = slice(max(lo - first, 0), min(lo + half - first, rows))
                    if at.start < at.stop:
                        total = keep_ref[at, :] + got_ref[at, :].astype(f32)
                        to = slice(at.start + first - lo, at.stop + first - lo)
                        ref[to, :] = total.astype(ref.dtype)
                    first += rows

            pl.when(high == j)(functools.partial(store, mine_ref))
            pl.when(high != j)(functools.partial(store, send_ref))
            lo += half


def unpack_kernel(mine_ref, theirs_ref, up_ref, down_ref, taps_ref, bias_ref, gain_ref, shift_ref, up_bias_ref, down_bias_ref):
    core0 = lax.axis_index("narrow") % 2 == 0
    for l in range(HT):
        w = min(128, HID - 128 * l)
        rows = slice(l * C, l * C + C)
        one = mine_ref[rows, :].astype(f32)
        two = theirs_ref[rows, :].astype(f32)
        up_ref[:, 128 * l : 128 * l + w] = jnp.where(core0, one, two)[:, 0:w]
        down_ref[:, 128 * l : 128 * l + w] = jnp.where(core0, two, one)[:, 0:w]
    extra = mine_ref[ROWS:, :].astype(f32) + theirs_ref[ROWS:, :].astype(f32)
    for g in range(GROUPS):
        taps_ref[:, lanes(g)] = extra[g * 64 : g * 64 + 49, 0 : group_width(g)]
    for k, ref in enumerate((bias_ref, gain_ref, shift_ref, down_bias_ref)):
        at = 49 + k
        vector = jnp.concatenate([extra[g * 64 + at : g * 64 + at + 1] for g in range(GROUPS)], axis=1)
        ref[...] = vector[:, 0:C].reshape(C)
    vector = jnp.concatenate([extra[256 + l : 257 + l] for l in range(HT)], axis=1)
    up_bias_ref[...] = vector[:, 0:HID].reshape(HID)


def back_tile(t, p_ref, weight_ref, y_ref, tile_ref, gated_ref, mask_ref, out_ref, sem):
    at = slice(t * TE * TE, (t + 1) * TE * TE)
    y_ref[...] = gated_ref[at, :].astype(f32)

    def place(g, h, r):
        return (pl.ds(r * TE + 8 * h, 8), pl.ds(pl.multiple_of(g * 128, 128), 128))

    def start(t, g, h):
        return [y_ref[place(g, h, r)] for r in range(TE)]

    def finish(t, g, h, rows):
        for r in range(TE):
            y_ref[place(g, h, r)] = rows[r]

    convolve(p_ref, weight_ref, start, finish, True, (t,))
    tile_ref[...] = (y_ref[:, 0:C] * mask_ref[at, :]).astype(bf16).reshape(TE, TE, C)
    copy = pltpu.make_async_copy(tile_ref, out_ref.at[t], sem)
    copy.start()
    copy.wait()


def back_first_kernel(
    beside_ref,
    cg_ref,
    mask_ref,
    gated_ref,
    n1_ref,
    n2_ref,
    w1_ref,
    w2_ref,
    taps_ref,
    out_ref,
    p_ref,
    rn_ref,
    rw_ref,
    weight_ref,
    y_ref,
    tile_ref,
    neighbours_ref,
    sem,
):
    copy = pltpu.make_async_copy(beside_ref, neighbours_ref, sem)
    copy.start()
    for s in range(2):
        place_centre(padded_lanes(cg_ref[s].reshape(TE * TE, C).astype(f32)), s, p_ref)
    place_rows(n1_ref, n2_ref, rn_ref)
    place_columns(w1_ref, w2_ref, rw_ref)
    take_weights(weight_ref, taps_ref)
    copy.wait()

    def borders(t, g):
        border_rows(neighbours_ref, p_ref, rn_ref, t, g)
        border_columns(neighbours_ref, p_ref, rn_ref, rw_ref, t, g, column_in(p_ref, t, g))

    each_group(borders)
    back_tile(0, p_ref, weight_ref, y_ref, tile_ref, gated_ref, mask_ref, out_ref, sem)


def back_second_kernel(
    p_ref, mask_ref, gated_ref, taps_ref, before_ref, out_ref, weight_ref, y_ref, tile_ref, sem
):
    take_weights(weight_ref, taps_ref)
    back_tile(1, p_ref, weight_ref, y_ref, tile_ref, gated_ref, mask_ref, out_ref, sem)


def params(size=16):
    return pltpu.CompilerParams(vmem_limit_bytes=size * 1024 * 1024)


def estimate():
    return pl.CostEstimate(flops=10**9, bytes_accessed=16 * 10**6, transcendentals=0)


NEIGHBOURS = pltpu.SMEM((2, 8), jnp.int32)
P_SCRATCH = pltpu.VMEM((2, GROUPS, 23 * PITCH, 128), f32)
RN_SCRATCH = pltpu.VMEM((2, 2, GROUPS, 64, 128), f32)
RW_SCRATCH = pltpu.VMEM((2, 2, GROUPS, 80, 128), f32)
W_SCRATCH = pltpu.VMEM((56, CP), f32)
Y_SCRATCH = pltpu.VMEM((CELLS, CP), f32)


def swap_pairs(kind):
    axis, offset = kind
    pairs = []
    for w in range(32):
        for n in range(4):
            if axis == "narrow":
                up = (n - offset) % 2 == 0
                other = (w, (n + (1 if up else -1)) % 4)
            else:
                up = (w - offset) % 2 == 0
                other = ((w + (1 if up else -1)) % 32, n)
            pairs.append((w * 4 + n, other[0] * 4 + other[1]))
    return pairs


def swap(x, kind):
    return lax.ppermute(x, AXES, swap_pairs(kind))


def flip(x, mask):
    return lax.ppermute(x, AXES, [(i, i ^ mask) for i in range(128)])


STAGES = {
    "x1": (2, (1, 6)),
    "x2": (66, (6,)),
    "z1": (4, (2, 3)),
    "z2": (12, (3,)),
    "y1": (16, (4, 5)),
    "y2": (48, (5,)),
}
ORDERS = (
    ("x1", "y1", "z1", "x2", "y2", "z2"),
    ("y1", "z1", "x1", "y2", "z2", "x2"),
    ("z1", "x1", "y1", "z2", "x2", "y2"),
)
DEPTH = 2


def parity(me, bits):
    return sum((me >> bit) & 1 for bit in bits) & 1


def exchange(x, order, stage):
    masks = [STAGES[order[(stage + 3 * core) % 6]][0] for core in range(2)]
    return lax.ppermute(x, AXES, [(i, i ^ masks[i & 1]) for i in range(128)])


def keeps_high(me, order, stage):
    zero, one = (parity(me, STAGES[order[(stage + 3 * core) % 6]][1]) for core in range(2))
    return jnp.where(me % 2 == 0, zero, one) == 1


def halved(part, order, stage, high):
    half = part.shape[0] // 2
    low_rows, high_rows = part[0:half], part[half:]
    send = jnp.where(high, low_rows, high_rows).astype(bf16)
    keep = jnp.where(high, high_rows, low_rows)
    return keep + exchange(send, order, stage).astype(f32)


def doubled(part, order, stage):
    mine = part.astype(bf16)
    return mine.astype(f32) + exchange(mine, order, stage).astype(f32)


def joined(part, order, stage, high):
    got = exchange(part, order, stage)
    return jnp.concatenate([jnp.where(high, got, part), jnp.where(high, part, got)], axis=0)


def together(*values):
    return lax.optimization_barrier(values)


def local(
    field,
    cotangent,
    land,
    neighbours,
    depth_weight,
    depth_bias,
    ln_gain,
    ln_shift,
    up_weight,
    up_bias,
    down_weight,
):
    me = here()
    shape = jax.ShapeDtypeStruct
    stay = lambda v: pltpu.with_memory_space_constraint(v, pltpu.HBM)
    high = [[keeps_high(me, order, stage) for stage in range(DEPTH)] for order in ORDERS]
    high, field = together(high, field)
    neighbours = stay(neighbours)
    narrow_shape = shape((2, 48, CP), bf16)
    wide_shape = shape((SIDE_ROWS, 128), bf16)
    wide_scratch = [
        pltpu.VMEM((2, GROUPS, TE * TE + TE, 128), f32),
        RN_SCRATCH,
        RW_SCRATCH,
        pltpu.VMEM((2, SIDE_ROWS, 128), f32),
    ]
    p_shape = shape((2, GROUPS, 23 * PITCH, 128), f32)

    s1, s2, field, land = pl.pallas_call(
        narrow_kernel,
        out_shape=(
            narrow_shape,
            narrow_shape,
            shape((2, TE, TE, C), bf16),
            shape((2, TE, TE), jnp.int32),
        ),
        in_specs=[HBM] * 2,
        out_specs=(VMEM,) * 4,
        scratch_shapes=[pltpu.SemaphoreType.DMA((2,))],
        compiler_params=params(4),
        name="pack_rows",
    )(stay(field), stay(land))
    n1, n2 = swap(s1, ("narrow", 0)), swap(s2, ("narrow", 1))
    mask, gated, gated_t, down_bias_sum, up_held, down_held, taps, small = pl.pallas_call(
        hold_kernel,
        out_shape=(
            shape((CELLS, C), f32),
            shape((CELLS, CP), bf16),
            shape((CP, CELLS), bf16),
            shape((1, C), f32),
            shape((C, HID), bf16),
            shape((C, HID), bf16),
            shape((49, C), f32),
            shape((4, HID), f32),
        ),
        in_specs=[VMEM] + [HBM] * 8,
        out_specs=(VMEM,) * 8,
        scratch_shapes=[
            pltpu.VMEM((2, TE, TE, C), bf16),
            pltpu.VMEM((C,), f32),
            pltpu.VMEM((C,), f32),
            pltpu.VMEM((C,), f32),
            pltpu.VMEM((HID,), f32),
            pltpu.SemaphoreType.DMA((8,)),
        ],
        compiler_params=params(8),
        cost_estimate=estimate(),
        name="hold",
    )(
        land,
        stay(cotangent),
        stay(depth_weight),
        stay(depth_bias),
        stay(ln_gain),
        stay(ln_shift),
        stay(up_bias),
        stay(up_weight),
        stay(down_weight.T),
    )
    s1, s2 = pl.pallas_call(
        functools.partial(wide_kernel, True),
        out_shape=(wide_shape, wide_shape),
        in_specs=[VMEM] * 4,
        out_specs=(VMEM, VMEM),
        scratch_shapes=wide_scratch,
        compiler_params=params(8),
        name="pack_columns",
    )(field, mask, n1, n2)
    s1, s2, n1, n2 = together(s1, s2, n1, n2)
    w2, w1 = swap(s2, ("wide", 1)), swap(s1, ("wide", 0))
    p, y = pl.pallas_call(
        prep_kernel,
        out_shape=(p_shape, shape((2, GROUPS, TE * TE, 128), f32)),
        in_specs=[HBM] + [VMEM] * 6,
        out_specs=(VMEM,) * 2,
        scratch_shapes=[RN_SCRATCH, W_SCRATCH, NEIGHBOURS, pltpu.SemaphoreType.DMA],
        compiler_params=params(8),
        cost_estimate=estimate(),
        name="prep",
    )(neighbours, field, mask, n1, n2, taps, small)

    def piece_shapes(piece):
        _, count, rows = PIECES[piece]
        return (
            shape((rows, 128), f32),
            shape((rows, 128), bf16),
            shape((CELLS, C), f32),
            shape((1, count), f32),
        )

    keep0, send0, ng0, ub0, z, r, border, normed, normed_t = pl.pallas_call(
        front_kernel,
        out_shape=piece_shapes(0)
        + (
            shape((CELLS, C), f32),
            shape((CELLS, 128), f32),
            shape((2, GROUPS, 6 * 24, 128), f32),
            shape((CELLS, CP), bf16),
            shape((CP, CELLS), bf16),
        ),
        in_specs=[HBM] + [VMEM] * 12,
        out_specs=(VMEM,) * 9,
        scratch_shapes=[
            RN_SCRATCH,
            RW_SCRATCH,
            W_SCRATCH,
            pltpu.VMEM((2, GROUPS, TE * TE + TE, 128), f32),
            NEIGHBOURS,
            pltpu.SemaphoreType.DMA,
        ],
        compiler_params=params(14),
        name="front",
    )(
        neighbours,
        n1,
        n2,
        w1,
        w2,
        p,
        y,
        gated,
        gated_t,
        taps,
        small,
        up_held,
        down_held,
    )
    got0 = flip(send0, 1)
    keep1, send1, ng1, ub1 = pl.pallas_call(
        functools.partial(hidden, 1),
        out_shape=piece_shapes(1),
        in_specs=[VMEM] * 7,
        out_specs=(VMEM,) * 4,
        compiler_params=params(12),
        cost_estimate=estimate(),
        name="hidden",
    )(normed, normed_t, gated, gated_t, small, up_held, down_held)
    got1 = flip(send1, 1)
    cg, g1, g2, cg_wide, sums = pl.pallas_call(
        grad_kernel,
        out_shape=(
            shape((2, TE, TE, C), bf16),
            narrow_shape,
            narrow_shape,
            shape((CELLS, CP), f32),
            shape((3, C), f32),
        ),
        in_specs=[VMEM] * 5,
        out_specs=(VMEM,) * 5,
        compiler_params=params(4),
        cost_estimate=estimate(),
        name="grad",
    )(ng0, ng1, z, r, small)

    halves = [size // 2 for size in SIZES]
    pieces = pl.pallas_call(
        split_kernel,
        out_shape=tuple(shape((half, 128), bf16) for half in halves)
        + tuple(shape((half, 128), f32) for half in halves)
        + (shape((8, 128), f32),),
        in_specs=[VMEM] * 5,
        out_specs=(VMEM,) * (2 * len(SIZES) + 1),
        compiler_params=params(4),
        name="split",
    )(keep0, got0, keep1, got1, sums)

    orders = list(enumerate(ORDERS))
    got = [exchange(pieces[i], order, 0) for i, order in orders]
    n1, n2 = swap(g1, ("narrow", 0)), swap(g2, ("narrow", 1))
    extra = pl.pallas_call(
        taps_kernel,
        out_shape=shape((EXTRA, 128), f32),
        in_specs=[VMEM] * 8,
        out_specs=VMEM,
        scratch_shapes=[
            pltpu.VMEM(p_shape.shape, f32),
            pltpu.VMEM((GROUPS, 49, 8, 128), f32),
        ],
        compiler_params=params(8),
        cost_estimate=estimate(),
        name="taps",
    )(pieces[-1], cg_wide, p, border, sums, ub0, ub1, down_bias_sum)
    parts = [pieces[len(SIZES) + i] + got[i].astype(f32) for i, order in orders]
    parts[-1] = jnp.concatenate([parts[-1], extra], axis=0)
    parts, n1, n2 = together(parts, n1, n2)
    s1, s2 = pl.pallas_call(
        functools.partial(wide_kernel, False),
        out_shape=(wide_shape, wide_shape),
        in_specs=[VMEM] * 3,
        out_specs=(VMEM, VMEM),
        scratch_shapes=wide_scratch,
        compiler_params=params(8),
        name="pack_columns_back",
    )(cg, n1, n2)
    for stage in range(1, DEPTH):
        parts = [halved(parts[i], order, stage, high[i][stage]) for i, order in orders]
    w1, w2 = swap(s1, ("wide", 0)), swap(s2, ("wide", 1))
    for stage in range(DEPTH, 6):
        parts = [doubled(parts[i], order, stage) for i, order in orders]
        if stage == 4:
            parts[-1], w1, w2 = together(parts[-1], w1, w2)
    parts = [part.astype(bf16) for part in parts]
    for stage in reversed(range(1, DEPTH)):
        parts = [joined(parts[i], order, stage, high[i][stage]) for i, order in orders]
    parts[-1], w1, w2 = together(parts[-1], w1, w2)

    tile_scratch = [
        W_SCRATCH,
        pltpu.VMEM((TE * TE, CP), f32),
        pltpu.VMEM((TE, TE, C), bf16),
    ]
    field_grad, grad_p = pl.pallas_call(
        back_first_kernel,
        out_shape=(shape((2, TE, TE, C), bf16), p_shape),
        in_specs=[HBM] + [VMEM] * 8,
        out_specs=(HBM, VMEM),
        scratch_shapes=[RN_SCRATCH, RW_SCRATCH]
        + tile_scratch
        + [NEIGHBOURS, pltpu.SemaphoreType.DMA],
        compiler_params=params(8),
        cost_estimate=estimate(),
        name="back_first",
    )(neighbours, cg, mask, gated, n1, n2, w1, w2, taps)
    matrix = [joined(parts[i], order, 0, high[i][0]) for i, order in orders[:-1]]
    last = parts[-1]
    order = ORDERS[-1]
    got = exchange(last, order, 0)
    one, two = last[0 : halves[-1]], got[0 : halves[-1]]
    upper = high[-1][0]
    extra = (last[halves[-1] :].astype(f32) + got[halves[-1] :].astype(f32)).astype(bf16)
    mine = jnp.concatenate(
        matrix + [jnp.where(upper, two, one), jnp.where(upper, one, two), extra], axis=0
    )
    mine, field_grad = together(mine, field_grad)
    theirs = flip(mine, 1)
    field_grad = pl.pallas_call(
        back_second_kernel,
        out_shape=shape((2, TE, TE, C), bf16),
        in_specs=[VMEM] * 4 + [HBM],
        out_specs=HBM,
        scratch_shapes=tile_scratch + [pltpu.SemaphoreType.DMA],
        input_output_aliases={4: 0},
        compiler_params=params(8),
        cost_estimate=estimate(),
        name="back_second",
    )(grad_p, mask, gated, taps, field_grad)
    theirs, field_grad = together(theirs, field_grad)
    up_grad, down_grad, *rest = pl.pallas_call(
        unpack_kernel,
        out_shape=(
            shape((C, HID), f32),
            shape((C, HID), f32),
            shape((49, C), f32),
            shape((C,), f32),
            shape((C,), f32),
            shape((C,), f32),
            shape((HID,), f32),
            shape((C,), f32),
        ),
        in_specs=[VMEM] * 2,
        out_specs=(VMEM,) * 8,
        compiler_params=params(12),
        name="unpack",
    )(mine, theirs)
    depth_grad, depth_bias_grad, gain_grad, shift_grad, up_bias_grad, down_bias_grad = rest
    return (
        field_grad,
        depth_grad,
        depth_bias_grad,
        gain_grad,
        shift_grad,
        up_grad,
        up_bias_grad,
        down_grad.T,
        down_bias_grad,
    )


def solution(mesh):
    return jax.shard_map(
        local,
        mesh=mesh,
        in_specs=(
            P(("wide", "narrow"), None, None, None),
            P(("wide", "narrow"), None, None, None),
            P(("wide", "narrow"), None, None),
            P(("wide", "narrow"), None),
            P(),
            P(),
            P(),
            P(),
            P(),
            P(),
            P(),
        ),
        out_specs=(P(("wide", "narrow"), None, None, None), P(), P(), P(), P(), P(), P(), P(), P()),
        check_vma=False,
    )
```
